32 devices in a mesh: dp: 4 (over z), seq: 8 (over y, x, core).
Axes of the slice: x: 2, y: 2, z: 4, core: 2. Of those that a mesh axis runs over, the one named last changes fastest.
Arguments:
- inputs: float32 [8, 2048, 512], P('dp', 'seq'), may hold values from -6 to 6
- out_grad: float32 [8, 2048, 512], P('dp', 'seq'), may hold values from -6 to 6
- ln_gain: float32 [2, 512], P(None, 'dp'), may hold values from 0.1 to 1.9
- ln_bias: float32 [2, 512], P(None, 'dp'), may hold values from -3 to 3
- nu_log: float32 [2, 256], P(None, 'dp'), may hold values from -12 to -3
- theta_log: float32 [2, 256], P(None, 'dp'), may hold values from -5 to 0
- gamma_log: float32 [2, 256], P(None, 'dp'), may hold values from -7 to -1
- in_map: float32 [2, 512, 512], P(None, 'dp'), may hold values from -0.25 to 0.25
- out_map: float32 [2, 512, 512], P(None, 'dp'), may hold values from -0.25 to 0.25
- skip_gain: float32 [2, 512], P(None, 'dp'), may hold values from -4 to 4
- glu_weight: float32 [2, 512, 1024], P(None, 'dp'), may hold values from -0.25 to 0.25
- glu_bias: float32 [2, 1024], P(None, 'dp'), may hold values from -3 to 3
Outputs:
- output: float32 [8, 2048, 512], P('dp', 'seq')
- input_grad: float32 [8, 2048, 512], P('dp', 'seq')
- grad_ln_gain: float32 [2, 512], P(None, 'dp')
- grad_ln_bias: float32 [2, 512], P(None, 'dp')
- grad_nu_log: float32 [2, 256], P(None, 'dp')
- grad_theta_log: float32 [2, 256], P(None, 'dp')
- grad_gamma_log: float32 [2, 256], P(None, 'dp')
- grad_in_map: float32 [2, 512, 512], P(None, 'dp')
- grad_out_map: float32 [2, 512, 512], P(None, 'dp')
- grad_skip_gain: float32 [2, 512], P(None, 'dp')
- grad_glu_weight: float32 [2, 512, 1024], P(None, 'dp')
- grad_glu_bias: float32 [2, 1024], P(None, 'dp')
The draws below stay inside these ranges and needn't reach their ends.
All inputs are finite; a program needn't handle non-finite values.
Results may differ from the reference program's by a relative error of at most 0.0004.
Values sent between devices are 32-bit elements; how exact they have to be, the bound alone decides.
No kernel may reach another device: no remote copies, remote signals or barrier semaphores. Data moves between devices by JAX's collectives and lax.ppermute only.
A program may use at most 192 MiB of HBM per device.

```python
import jax
import jax.numpy as jnp
from jax import lax

H = 512
N = 256
LAYERS = 2
LENGTH = 2048
SEQS = 8


def decay_rates(key, lowest, highest):
    share = jax.random.uniform(key, (LAYERS, N), jnp.float32)
    return lowest * (highest / lowest) ** share


def draw_nu_log(key, part):
    rates = decay_rates(key, 0.5 / LENGTH, 1.0 / 30.0)
    return jnp.log(rates)


def draw_gamma_log(key, part):
    rates = decay_rates(key, 0.5 / LENGTH, 1.0 / 30.0)
    key = jax.random.fold_in(key, 7)
    jitter = jax.random.uniform(key, (LAYERS, N), jnp.float32, -0.3, 0.3)
    return 0.5 * jnp.log(1.0 - jnp.exp(-2.0 * rates)) + jitter


def shard_levels(key, shape, shards, least, largest):
    loudness = 1.0
    for dim, shards_of in shards:
        steps = jax.random.uniform(jax.random.fold_in(jax.random.fold_in(key, 6), dim), (shards_of,), jnp.float32, least / len(shards), largest / len(shards))
        loudness = loudness * jnp.repeat(jnp.exp(steps), shape[dim] // shards_of).reshape((-1,) + (1,) * (len(shape) - 1 - dim))
    return loudness


def scatter_about(own_key, dims, scale, most, split=(), dtype=jnp.bfloat16):
    drawn = jax.random.normal(own_key, dims, jnp.float32) * scale
    if len(split) > 0:
        drawn = shard_levels(own_key, dims, split, -0.22, 0.18) * drawn
    return jnp.clip(drawn, min=-most, max=most).astype(dtype)


def setup_inputs(seed: int = 0) -> dict:
    key_of = jax.random.split(jax.random.key(seed), 13)
    inputs = scatter_about(key_of[0], (SEQS, LENGTH, H), 1.0, 6.0, ((0, 4), (1, 8)), jnp.float32)
    out_grad = scatter_about(key_of[1], (SEQS, LENGTH, H), 1.0, 6.0, ((0, 4), (1, 8)), jnp.float32)
    ln_gain = jnp.clip(1.0 + 0.18 * jax.random.normal(key_of[2], (LAYERS, H), jnp.float32), 0.1, 1.9)
    ln_bias = scatter_about(key_of[3], (LAYERS, H), 0.5, 3.0, ((1, 4),), jnp.float32)
    nu_log = draw_nu_log(jax.random.fold_in(key_of[12], 71), 0)
    theta_log = jnp.clip(-5.0 + 5.0 * jax.random.uniform(key_of[5], (LAYERS, N), jnp.float32) ** shard_levels(key_of[5], (LAYERS, N), ((1, 4),), -0.2, 0.2), -5.0, 0.0)
    gamma_log = draw_gamma_log(jax.random.fold_in(key_of[12], 71), 0)
    in_map = scatter_about(key_of[7], (LAYERS, H, 2 * N), H ** -0.5, 0.25, ((1, 4),), jnp.float32)
    out_map = scatter_about(key_of[8], (LAYERS, 2 * N, H), (2 * N) ** -0.5, 0.25, ((1, 4),), jnp.float32)
    skip_gain = scatter_about(key_of[9], (LAYERS, H), 1.0, 4.0, ((1, 4),), jnp.float32)
    glu_weight = scatter_about(key_of[10], (LAYERS, H, 2 * H), H ** -0.5, 0.25, ((1, 4),), jnp.float32)
    glu_bias = scatter_about(key_of[11], (LAYERS, 2 * H), 0.5, 3.0, ((1, 4),), jnp.float32)
    return dict(inputs=inputs, out_grad=out_grad, ln_gain=ln_gain, ln_bias=ln_bias, nu_log=nu_log, theta_log=theta_log, gamma_log=gamma_log, in_map=in_map, out_map=out_map, skip_gain=skip_gain, glu_weight=glu_weight, glu_bias=glu_bias)


@jax.custom_vjp
def low(v):
    return lax.optimization_barrier(v.astype(jnp.bfloat16)).astype(jnp.float32)

@jax.custom_vjp
def low_back(v):
    return v

def low_keep(v):
    return (low(v), None)

def low_pass(kept, grad):
    return (grad,)

def back_keep(v):
    return (v, None)

def back_low(kept, grad):
    return (low(grad),)
low.defvjp(low_keep, low_pass)
low_back.defvjp(back_keep, back_low)
norm_eps = 1e-05

def matmul(left_side, right_side):
    return jnp.dot(left_side, right_side, precision=lax.Precision.HIGHEST, preferred_element_type=jnp.float32)

def layer_norm(activation, norm_gain, norm_bias):
    centred = activation - lax.optimization_barrier(jnp.mean(activation, -1, keepdims=True))
    spread = lax.optimization_barrier(jnp.mean(centred * centred, -1, keepdims=True))
    return centred * lax.rsqrt(spread + norm_eps) * norm_gain + norm_bias

def block_scan(lam_pair, state_pair, block_pair):
    lam_re, lam_im = lam_pair

    def advance(carry_pair, drive_pair):
        state_re, state_im = carry_pair
        drive_re, drive_im = drive_pair
        next_re = lam_re * state_re - lam_im * state_im + drive_re
        next_im = lam_re * state_im + lam_im * state_re + drive_im
        return ((next_re, next_im), (next_re, next_im))
    return lax.scan(advance, state_pair, block_pair)

def recurrence(drive_re, drive_im, lam_re, lam_im):
    length_now, width_now = drive_re.shape
    span_len = min(128, length_now)
    blocks = (drive_re.reshape(length_now // span_len, span_len, width_now), drive_im.reshape(length_now // span_len, span_len, width_now))
    runner = jax.checkpoint(block_scan)

    def outer_step(state_pair, block_pair):
        return runner((lam_re, lam_im), state_pair, block_pair)
    zero_state = jnp.zeros((width_now,), jnp.float32)
    _, (states_re, states_im) = lax.scan(outer_step, (zero_state, zero_state), blocks)
    return (states_re.reshape(length_now, width_now), states_im.reshape(length_now, width_now))

def forward(activation, ln_gain, ln_bias, nu_log, theta_log, gamma_log, in_map, out_map, skip_gain, glu_weight, glu_bias):
    for layer_num in range(LAYERS):
        normed = layer_norm(activation, ln_gain[layer_num], ln_bias[layer_num])
        gamma = jnp.exp(gamma_log[layer_num])
        driven = matmul(normed, in_map[layer_num])
        rate = jnp.exp(nu_log[layer_num])
        angle = jnp.exp(theta_log[layer_num])
        modulus = jnp.exp(-rate)
        lam_re = modulus * jnp.cos(angle)
        lam_im = modulus * jnp.sin(angle)
        states_re, states_im = recurrence(driven[:, :N] * gamma, driven[:, N:] * gamma, lam_re, lam_im)
        states = jnp.concatenate([states_re, states_im], 1)
        mixed = matmul(states, out_map[layer_num]) + skip_gain[layer_num] * normed
        active = jax.nn.gelu(mixed)
        both = matmul(active, glu_weight[layer_num]) + glu_bias[layer_num]
        activation = activation + both[:, :H] * jax.nn.sigmoid(both[:, H:])
    return activation

def reference(inputs, out_grad, ln_gain, ln_bias, nu_log, theta_log, gamma_log, in_map, out_map, skip_gain, glu_weight, glu_bias):
    params = (ln_gain, ln_bias, nu_log, theta_log, gamma_log, in_map, out_map, skip_gain, glu_weight, glu_bias)

    def per_sequence(totals, seq_pair):
        seq_in, seq_cot = seq_pair
        result, pullback = jax.vjp(forward, seq_in, *params)
        grads = pullback(seq_cot)
        totals = tuple((run + new for run, new in zip(totals, grads[1:])))
        return (totals, (result, grads[0]))
    zeros = tuple((jnp.zeros_like(item) for item in params))
    totals, (output, input_grad) = lax.scan(per_sequence, zeros, (inputs, out_grad))
    return (output, input_grad, totals[0], totals[1], totals[2], totals[3], totals[4], totals[5], totals[6], totals[7], totals[8], totals[9])
```

```python
import functools
import math

import jax
import jax.numpy as jnp
from jax import lax
from jax.experimental import pallas as pl
from jax.experimental.pallas import tpu as pltpu
from jax.sharding import PartitionSpec as P

NORM_EPS = 1e-05
GROUPS = 8
WIDE = 256
SMALL = 8
TABLE = 16
F32 = jnp.float32
BF16 = jnp.bfloat16
GELU_C = math.sqrt(2.0 / math.pi)

GAIN, BIAS, SKIP, BIAS_V, BIAS_G, GAMMA, LAM, LAM1, LAM2, LAM4, LAM8, RATES = range(12)


class Dims:
    def __init__(self, inputs, in_map, dp, seq):
        self.B, self.Tb, self.H = inputs.shape
        self.layers, self.Hd = in_map.shape[:2]
        self.N = self.H // 2
        self.T = self.B * self.Tb
        self.R = self.B * GROUPS
        self.L = self.Tb // GROUPS
        self.D, self.S = dp, seq
        self.q = max(16, self.Hd // seq)
        self.used = self.Hd // self.q


def cmul(ar, ai, br, bi):
    return ar * br - ai * bi, ar * bi + ai * br


def split(x):
    hi = x.astype(BF16)
    return hi, (x - hi.astype(F32)).astype(BF16)


def dot3(ah, al, bh, bl, dims):
    def one(a, b):
        return lax.dot_general(a, b, (dims, ((), ())), preferred_element_type=F32)

    return one(ah, bh) + (one(ah, bl) + one(al, bh))


def product(ah, al, wh, wl, dst, transposed=False, add=False):
    for n in range(dst.shape[1] // WIDE):
        cols = slice(n * WIDE, (n + 1) * WIDE)
        if transposed:
            res = dot3(ah[...], al[...], wh[cols, :], wl[cols, :], ((1,), (1,)))
        else:
            res = dot3(ah[...], al[...], wh[:, cols], wl[:, cols], ((1,), (0,)))
        dst[:, cols] = dst[:, cols] + res if add else res


def each_step(dim, fn, unroll=2, reverse=False, init=0):
    def one(i, carry):
        j = dim.L - 1 - i if reverse else i
        rows = pl.ds(pl.multiple_of(j * dim.R, dim.R), dim.R)
        return fn(j, rows, carry)

    return lax.fori_loop(0, dim.L, one, init, unroll=unroll)


def row(table, index, n=1):
    return table[index : index + n, :]


def lam_of(dim, table, index, reverse):
    pair = table[index : index + 1, :]
    real, imag = pair[:, : dim.N], pair[:, dim.N :]
    return real, -imag if reverse else imag


def chunk_scan(dim, table, yr, yi, reverse):
    place = lax.broadcasted_iota(jnp.int32, yr.shape, 0)
    for dist, index in ((1, LAM1), (2, LAM2), (4, LAM4)):
        pr, pi = lam_of(dim, table, index, reverse)
        if reverse:
            shift, seen = GROUPS - dist, place < GROUPS - dist
        else:
            shift, seen = dist, place >= dist
        sr = jnp.where(seen, pltpu.roll(yr, shift, 0), 0.0)
        si = jnp.where(seen, pltpu.roll(yi, shift, 0), 0.0)
        mr, mi = cmul(pr, pi, sr, si)
        yr, yi = yr + mr, yi + mi
    return yr, yi


def local_finals(dim, table, drive_ref, cf_ref, f_ref, reverse):
    lr, li = lam_of(dim, table, LAM, reverse)
    lr = jnp.broadcast_to(lr, (dim.R, dim.N))
    li = jnp.broadcast_to(li, (dim.R, dim.N))

    def step(j, rows, carry):
        d = drive_ref[rows, :]
        mr, mi = cmul(lr, li, *carry)
        return mr + d[:, : dim.N], mi + d[:, dim.N :]

    zero = jnp.zeros((dim.R, dim.N), F32)
    fr, fi = each_step(dim, step, 4, reverse, (zero, zero))
    cf_ref[:, : dim.N] = fr
    cf_ref[:, dim.N :] = fi
    last = 0 if reverse else GROUPS - 1
    for b in range(dim.B):
        rows = slice(b * GROUPS, (b + 1) * GROUPS)
        yr, yi = chunk_scan(dim, table, fr[rows], fi[rows], reverse)
        f_ref[b : b + 1, : dim.N] = yr[last : last + 1]
        f_ref[b : b + 1, dim.N :] = yi[last : last + 1]


def entries_of(dim, table, cf_ref, g_ref, en_ref, reverse):
    me = lax.axis_index("seq")
    lr, li = lam_of(dim, table, LAM8, reverse)
    xr = jnp.zeros((dim.B, dim.N), F32)
    xi = xr
    order = reversed(range(dim.S)) if reverse else range(dim.S)
    for other in order:
        ahead = other > me if reverse else other < me
        g = g_ref[other]
        mr, mi = cmul(lr, li, xr, xi)
        xr = jnp.where(ahead, mr + g[:, : dim.N], xr)
        xi = jnp.where(ahead, mi + g[:, dim.N :], xi)
    for b in range(dim.B):
        rows = slice(b * GROUPS, (b + 1) * GROUPS)
        f = cf_ref[rows, :]
        place = lax.broadcasted_iota(jnp.int32, f.shape, 0)
        x = jnp.concatenate([xr[b : b + 1], xi[b : b + 1]], 1)
        if reverse:
            y = jnp.where(place == GROUPS - 1, x, pltpu.roll(f, GROUPS - 1, 0))
        else:
            y = jnp.where(place == 0, x, pltpu.roll(f, 1, 0))
        yr, yi = chunk_scan(dim, table, y[:, : dim.N], y[:, dim.N :], reverse)
        en_ref[rows, : dim.N] = yr
        en_ref[rows, dim.N :] = yi


def norm_step(dim, x, table):
    mean = jnp.mean(x, -1, keepdims=True)
    centred = x - mean
    var = jnp.mean(centred * centred, -1, keepdims=True)
    rstd = lax.rsqrt(var + NORM_EPS)
    xhat = centred * rstd
    return xhat, rstd, xhat * row(table, GAIN) + row(table, BIAS)


def front(dim, load_act, table, w_in, xhat, rstd, drive, cf, fin, ah, al, wh, wl):
    def norm(j, rows, _):
        xh, rs, normed = norm_step(dim, load_act(j, rows), table)
        xhat[rows, :] = xh
        rstd[rows, :] = jnp.broadcast_to(rs, (dim.R, 128))
        ah[rows, :], al[rows, :] = split(normed)
        return 0

    each_step(dim, norm, 4)
    w_in.fill(wh, wl)
    product(ah, al, wh, wl, drive)

    def scale(j, rows, _):
        drive[rows, :] = drive[rows, :] * row(table, GAMMA)
        return 0

    each_step(dim, scale, 4)
    local_finals(dim, table, drive, cf, fin, False)


def gelu_parts(m):
    inner = GELU_C * (m + 0.044715 * (m * m * m))
    th = jnp.tanh(inner)
    return th


def back(dim, table, drive, cf, g, xhat, w_out, w_gv, w_gg, en, states, mixed, active, v, s, ah, al, wh, wl):
    entries_of(dim, table, cf, g, en, False)
    lr, li = lam_of(dim, table, LAM, False)
    lr = jnp.broadcast_to(lr, (dim.R, dim.N))
    li = jnp.broadcast_to(li, (dim.R, dim.N))

    def scan(j, rows, carry):
        d = drive[rows, :]
        mr, mi = cmul(lr, li, *carry)
        both = jnp.concatenate([mr + d[:, : dim.N], mi + d[:, dim.N :]], 1)
        states[rows, :] = both
        ah[rows, :], al[rows, :] = split(both)
        return both[:, : dim.N], both[:, dim.N :]

    each_step(dim, scan, 4, False, (en[:, : dim.N], en[:, dim.N :]))
    w_out.fill(wh, wl)
    product(ah, al, wh, wl, mixed)

    def gelu(j, rows, _):
        normed = xhat[rows, :] * row(table, GAIN) + row(table, BIAS)
        m = mixed[rows, :] + row(table, SKIP) * normed
        mixed[rows, :] = m
        a = (0.5 * m) * (1.0 + gelu_parts(m))
        active[rows, :] = a
        ah[rows, :], al[rows, :] = split(a)
        return 0

    each_step(dim, gelu, 2)
    w_gv.fill(wh, wl)
    product(ah, al, wh, wl, v)
    w_gg.fill(wh, wl)
    product(ah, al, wh, wl, s)


def gate(dim, table, v, s, rows):
    vv = v[rows, :] + row(table, BIAS_V)
    ss = jax.nn.sigmoid(s[rows, :] + row(table, BIAS_G))
    v[rows, :] = vv
    s[rows, :] = ss
    return vv * ss


def top(dim, table, load_dact, v, s, mixed, xhat, w_gv, w_gg, w_out, dv, dg, dmixed, ds, rcf, rfin, sums, ah, al, bh, bl, wh, wl):
    def dgate(j, rows, carry):
        dact = load_dact(j, rows)
        ss, vv = s[rows, :], v[rows, :]
        a = dact * ss
        b = a * vv * (1.0 - ss)
        dv[rows, :] = a
        dg[rows, :] = b
        ah[rows, :], al[rows, :] = split(a)
        bh[rows, :], bl[rows, :] = split(b)
        return carry[0] + a, carry[1] + b

    zero = jnp.zeros((dim.R, dim.H), F32)
    sv, sg = each_step(dim, dgate, 2, False, (zero, zero))
    sums[BIAS_V : BIAS_V + 1, :] = jnp.sum(sv, 0, keepdims=True)
    sums[BIAS_G : BIAS_G + 1, :] = jnp.sum(sg, 0, keepdims=True)
    w_gv.fill(wh, wl)
    product(ah, al, wh, wl, dmixed, True)
    w_gg.fill(wh, wl)
    product(bh, bl, wh, wl, dmixed, True, True)

    def dgelu(j, rows, carry):
        m = mixed[rows, :]
        th = gelu_parts(m)
        slope = 0.5 * (1.0 + th) + (0.5 * m) * (1.0 - th * th) * (GELU_C * (1.0 + (3 * 0.044715) * (m * m)))
        d = dmixed[rows, :] * slope
        dmixed[rows, :] = d
        ah[rows, :], al[rows, :] = split(d)
        normed = xhat[rows, :] * row(table, GAIN) + row(table, BIAS)
        return carry + d * normed

    sums[SKIP : SKIP + 1, :] = jnp.sum(each_step(dim, dgelu, 2, False, zero), 0, keepdims=True)
    w_out.fill(wh, wl)
    product(ah, al, wh, wl, ds, True)
    local_finals(dim, table, ds, rcf, rfin, True)


def bottom(dim, table, ds, rcf, gr, states, en, drive, xhat, rstd, dmixed, w_in, load_dact, store, dproj, buf, adj_en, sums, ah, al, wh, wl):
    entries_of(dim, table, rcf, gr, adj_en, True)
    lr, li = lam_of(dim, table, LAM, True)
    lr = jnp.broadcast_to(lr, (dim.R, dim.N))
    li = jnp.broadcast_to(li, (dim.R, dim.N))
    zero = jnp.zeros((dim.R, dim.N), F32)

    def scan(j, rows, carry):
        ar, ai, dr, di, dgam = carry
        d = ds[rows, :]
        mr, mi = cmul(lr, li, ar, ai)
        ar, ai = mr + d[:, : dim.N], mi + d[:, dim.N :]
        earlier = pl.ds(pl.multiple_of(jnp.maximum(j - 1, 0) * dim.R, dim.R), dim.R)
        before = jnp.where(j == 0, en[...], states[earlier, :])
        br, bi = before[:, : dim.N], before[:, dim.N :]
        dr = dr + (ar * br + ai * bi)
        di = di + (ai * br - ar * bi)
        u = drive[rows, :]
        dgam = dgam + (ar * u[:, : dim.N] + ai * u[:, dim.N :])
        dp = jnp.concatenate([ar, ai], 1) * row(table, GAMMA)
        dproj[rows, :] = dp
        ah[rows, :], al[rows, :] = split(dp)
        return ar, ai, dr, di, dgam

    start = (adj_en[:, : dim.N], adj_en[:, dim.N :], zero, zero, zero)
    _, _, dr, di, dgam = each_step(dim, scan, 2, True, start)
    dr, di, dgam = (jnp.sum(x, 0, keepdims=True) for x in (dr, di, dgam))
    fr, fi = lam_of(dim, table, LAM, False)
    rates = row(table, RATES)
    rate, angle = rates[:, : dim.N], rates[:, dim.N :]
    sums[5:6, : dim.N] = -rate * (dr * fr + di * fi)
    sums[5:6, dim.N :] = angle * (di * fr - dr * fi)
    sums[6:7, : dim.N] = dgam
    sums[6:7, dim.N :] = jnp.zeros_like(dgam)
    sums[7:8, :] = jnp.zeros((1, dim.H), F32)

    w_in.fill(wh, wl)
    product(ah, al, wh, wl, buf, True)
    wide = jnp.zeros((dim.R, dim.H), F32)

    def dnorm(j, rows, carry):
        dn = buf[rows, :] + dmixed[rows, :] * row(table, SKIP)
        xh = xhat[rows, :]
        dx = dn * row(table, GAIN)
        m1 = jnp.mean(dx, -1, keepdims=True)
        m2 = jnp.mean(dx * xh, -1, keepdims=True)
        store(j, rows, load_dact(j, rows) + rstd[rows, 0:1] * (dx - m1 - xh * m2))
        return carry[0] + dn * xh, carry[1] + dn

    sgain, sbias = each_step(dim, dnorm, 2, False, (wide, wide))
    sums[GAIN : GAIN + 1, :] = jnp.sum(sgain, 0, keepdims=True)
    sums[BIAS : BIAS + 1, :] = jnp.sum(sbias, 0, keepdims=True)


def split_rows(dim, load, xh, xl):
    def one(j, rows, _):
        xh[rows, :], xl[rows, :] = split(load(rows))
        return 0

    each_step(dim, one, 4)


class Share:
    def __init__(self, dim, nm, extra=0):
        self.nm = nm
        self.q = -(-nm * dim.Hd // (8 * dim.S)) * 8
        self.extra = extra
        self.rows = self.q + extra
        self.step = math.gcd(self.q, dim.Hd)
        self.shape = (dim.S // 2, dim.D, self.rows, dim.H)


def weight_grad(dim, share, m, ah, al, bh, bl, tile, keep, send):
    me = lax.axis_index("seq")
    my = lax.axis_index("dp")
    for h0 in range(0, dim.H, WIDE):
        tile[...] = dot3(ah[:, h0 : h0 + WIDE], al[:, h0 : h0 + WIDE], bh[...], bl[...], ((0,), (0,)))

        def put(odd):
            for r0 in range(0, WIDE, share.step):
                h = h0 + r0
                d, p = h // dim.Hd, m * dim.Hd + h % dim.Hd
                s, off = p // share.q, p % share.q
                dst = keep if (s & 1) == odd else send
                dst[(s ^ me) >> 1, d ^ my, off : off + share.step, :] = tile[r0 : r0 + share.step, :]

        for odd in range(2):
            pl.when(me & 1 == odd)(functools.partial(put, odd))


def call(fn, outs, scratch, *args, flops=0, anywhere=0):
    nbytes = sum(4 * math.prod(x.shape) for x in (*args, *outs))
    spaces = [pl.ANY] * anywhere + [pltpu.VMEM] * (len(args) - anywhere)
    return pl.pallas_call(
        fn,
        out_shape=[jax.ShapeDtypeStruct(s.shape, F32) for s in outs],
        in_specs=[pl.BlockSpec(memory_space=space) for space in spaces],
        out_specs=[pl.BlockSpec(memory_space=pltpu.VMEM)] * len(outs),
        scratch_shapes=scratch,
        compiler_params=pltpu.CompilerParams(vmem_limit_bytes=56 * 1024 * 1024),
        cost_estimate=pl.CostEstimate(flops=flops, bytes_accessed=nbytes, transcendentals=0),
    )(*args)


def f32(*shape):
    return jax.ShapeDtypeStruct(shape, F32)


def halves(dim, n):
    return [pltpu.VMEM((dim.T, dim.H), BF16)] * (2 * n) + [pltpu.VMEM((dim.H, dim.H), BF16)] * 2


def prep_kernel(dim, small, table):
    for layer in range(dim.layers):
        s = small[layer]
        nu, theta, gam = s[5:6, : dim.N], s[5:6, dim.N :], s[6:7, : dim.N]
        rate, angle = jnp.exp(nu), jnp.exp(theta)
        mod = jnp.exp(-rate)
        re, im = mod * jnp.cos(angle), mod * jnp.sin(angle)
        gamma = jnp.exp(gam)

        def put(index, a, b):
            table[layer, index : index + 1, : dim.N] = a
            table[layer, index : index + 1, dim.N :] = b

        table[layer] = jnp.zeros((TABLE, dim.H), F32)
        table[layer, :5, :] = s[:5]
        put(GAMMA, gamma, gamma)
        put(LAM, re, im)
        put(RATES, rate, angle)
        power = 1
        while power < dim.L:
            re, im = cmul(re, im, re, im)
            power *= 2
        for index in (LAM1, LAM2, LAM4, LAM8):
            put(index, re, im)
            re, im = cmul(re, im, re, im)


class Weight:
    def __init__(self, dim, layer, m, sources, own, buf, sem):
        self.dim, self.layer, self.m = dim, layer, m
        self.sources, self.own, self.buf, self.sem = sources, own, buf, sem
        self.here = False

    def moves(self):
        in_map, out_map, glu = self.sources[:3]
        lo = max(self.m - 2, 0) * self.dim.H
        shard = (in_map, out_map, glu, glu)[self.m].at[self.layer, :, pl.ds(lo, self.dim.H)]
        yield pltpu.make_async_copy(shard, self.own, self.sem.at[self.dim.S])
        for k, piece in enumerate(self.sources[3:]):
            yield pltpu.make_async_copy(piece.at[self.m], self.buf.at[k], self.sem.at[k])

    def start(self):
        for move in self.moves():
            move.start()

    def fill(self, wh, wl):
        dim, q = self.dim, self.dim.q
        if not self.here:
            for move in self.moves():
                move.wait()
        self.here = True
        me, my = lax.axis_index("seq"), lax.axis_index("dp")

        def put(start, n, value):
            rows = pl.ds(pl.multiple_of(start, 16), n)
            wh[rows, :], wl[rows, :] = split(value)

        def mine(i, _):
            put(my * dim.Hd + i * 32, 32, self.own[pl.ds(pl.multiple_of(i * 32, 32), 32), :])
            return 0

        lax.fori_loop(0, dim.Hd // 32, mine, 0)

        def one(k, _):
            s = k ^ me

            def block():
                for kz in range(1, dim.D):
                    put((kz ^ my) * dim.Hd + s * q, q, self.buf[k, kz - 1])

            if dim.used < dim.S:
                pl.when(s < dim.used)(block)
            else:
                block()
            return 0

        lax.fori_loop(0, dim.S, one, 0)


def weights_in(dim, names, fn):
    layers = sorted({layer for layer, _ in names})
    first = 3 + len(layers) * dim.S

    def kernel(*refs):
        sources = {layer: refs[:3] + refs[3 + i * dim.S : 3 + (i + 1) * dim.S] for i, layer in enumerate(layers)}
        spare = refs[len(refs) - 3 * len(names) :]
        weights = [
            Weight(dim, layer, m, sources[layer], *spare[3 * i : 3 * i + 3]) for i, (layer, m) in enumerate(names)
        ]
        for w in weights:
            w.start()
        fn(dim, weights, *refs[first : len(refs) - 3 * len(names)])

    scratch = [
        pltpu.VMEM((dim.Hd, dim.H), F32),
        pltpu.VMEM((dim.S, dim.D - 1, dim.q, dim.H), F32),
        pltpu.SemaphoreType.DMA((dim.S + 1,)),
    ] * len(names)
    return kernel, first, scratch


def strided(dim, ref):
    return lambda j, rows: ref[:, j, :]


def plain(ref):
    return lambda j, rows: ref[rows, :]


def k_a0(dim, weights, x, table, xhat, rstd, drive, cf, fin, ah, al, wh, wl):
    front(dim, strided(dim, x), table.at[0], weights[0], xhat, rstd, drive, cf, fin, ah, al, wh, wl)


def k_b0(dim, weights, x, table, drive, cf, g, xhat,
         en, states, mixed, active, v, s, act1, xhat1, rstd1, drive1, cf1, fin1, ah, al, wh, wl):
    t = table.at[0]
    w_out, w_gv, w_gg, w_in1 = weights
    back(dim, t, drive, cf, g, xhat, w_out, w_gv, w_gg, en, states, mixed, active, v, s, ah, al, wh, wl)
    load = strided(dim, x)

    def residual(j, rows):
        act = load(j, rows) + gate(dim, t, v, s, rows)
        act1[rows, :] = act
        return act

    front(dim, residual, table.at[1], w_in1, xhat1, rstd1, drive1, cf1, fin1, ah, al, wh, wl)


def k_b1(dim, weights, act1, out_grad, table, drive, cf, g, xhat,
         out, en, states, active, dv, dg, dmixed, ds, rcf, rfin, sums, ah, al, bh, bl, wh, wl, mixed, v, s):
    t = table.at[1]
    w_out, w_gv, w_gg = weights
    back(dim, t, drive, cf, g, xhat, w_out, w_gv, w_gg, en, states, mixed, active, v, s, ah, al, wh, wl)

    def residual(j, rows, _):
        out[:, j, :] = act1[rows, :] + gate(dim, t, v, s, rows)
        return 0

    each_step(dim, residual, 2)
    sums[...] = jnp.zeros((SMALL, dim.H), F32)
    top(dim, t, strided(dim, out_grad), v, s, mixed, xhat, w_gv, w_gg, w_out, dv, dg, dmixed, ds, rcf, rfin, sums,
        ah, al, bh, bl, wh, wl)


def k_w1(dim, share, active, dv, dg, states, dmixed, keep, send, ah, al, bh, bl, tile):
    split_rows(dim, lambda rows: active[rows, :], ah, al)
    for m, ref in ((0, dv), (1, dg)):
        split_rows(dim, lambda rows: ref[rows, :], bh, bl)
        weight_grad(dim, share, m, ah, al, bh, bl, tile, keep, send)
    split_rows(dim, lambda rows: states[rows, :], ah, al)
    split_rows(dim, lambda rows: dmixed[rows, :], bh, bl)
    weight_grad(dim, share, 2, ah, al, bh, bl, tile, keep, send)


def k_c1(dim, weights, out_grad, table, ds, rcf, gr, states, en, drive, xhat, rstd, dmixed,
         xhat0, mixed0, v0, s0,
         dproj, dmid, dv0, dg0, dmixed0, ds0, rcf0, rfin0, sums1, sums0, ah, al, bh, bl, wh, wl, adj_en):
    w_in, w_gv, w_gg, w_out = weights

    def store(j, rows, value):
        dmid[rows, :] = value

    bottom(dim, table.at[1], ds, rcf, gr, states, en, drive, xhat, rstd, dmixed, w_in, strided(dim, out_grad), store,
           dproj, ds0, adj_en, sums1, ah, al, wh, wl)
    sums0[...] = jnp.zeros((SMALL, dim.H), F32)
    top(dim, table.at[0], plain(dmid), v0, s0, mixed0, xhat0, w_gv, w_gg, w_out, dv0, dg0, dmixed0, ds0, rcf0, rfin0,
        sums0, ah, al, bh, bl, wh, wl)


def k_w2(dim, share, active, dv, dg, states, dmixed, xhat1, dproj1, table, keep, send, ah, al, bh, bl, tile):
    k_w1(dim, share, active, dv, dg, states, dmixed, keep, send, ah, al, bh, bl, tile)
    t = table.at[1]
    split_rows(dim, lambda rows: xhat1[rows, :] * row(t, GAIN) + row(t, BIAS), ah, al)
    split_rows(dim, lambda rows: dproj1[rows, :], bh, bl)
    weight_grad(dim, share, 3, ah, al, bh, bl, tile, keep, send)


def k_c0(share, dim, weights, table, ds, rcf, gr, states, en, drive, xhat, rstd, dmixed, dmid, sums1a, sums1b, sums0a,
         input_grad, keep, send, ah, al, bh, bl, wh, wl, adj_en, dproj, buf, sums0, tile):
    t = table.at[0]

    def store(j, rows, value):
        input_grad[:, j, :] = value

    bottom(dim, t, ds, rcf, gr, states, en, drive, xhat, rstd, dmixed, weights[0], plain(dmid), store, dproj, buf, adj_en,
           sums0, ah, al, wh, wl)
    split_rows(dim, lambda rows: xhat[rows, :] * row(t, GAIN) + row(t, BIAS), bh, bl)
    weight_grad(dim, share, 0, bh, bl, ah, al, tile, keep, send)
    place = lax.broadcasted_iota(jnp.int32, (SMALL, dim.H), 0)
    upper = (place >= SKIP) & (place <= BIAS_G)
    tile[0:SMALL, :] = jnp.where(upper, sums0a[...], sums0[...])
    tile[SMALL : 2 * SMALL, :] = jnp.where(upper, sums1a[...], sums1b[...])
    me = lax.axis_index("seq")
    n = -(-2 * SMALL // dim.S)

    def put(odd):
        for s in range(dim.S):
            dst = keep if (s & 1) == odd else send
            lo = min(s * n, 2 * SMALL - n)
            for d in range(dim.D):
                dst[(s ^ me) >> 1, d, share.q : share.q + n, :] = tile[lo : lo + n, :]

    for odd in range(2):
        pl.when(me & 1 == odd)(functools.partial(put, odd))


def swap(x, axis, mask):
    count = lax.axis_size(axis)
    return lax.ppermute(x, axis, [(i, i ^ mask) for i in range(count)])


def plane_gather(dim, x):
    pieces = [None] * dim.S
    pieces[0] = x
    for k in range(2, dim.S, 2):
        pieces[k] = swap(x, "seq", k)
    for k in range(0, dim.S, 2):
        pieces[k + 1] = swap(pieces[k], "seq", 1)
    return pieces


def reduce_share(dim, keep, send):
    got = swap(send, "seq", 1)
    half = [keep[k] + got[k] for k in range(dim.S // 2)]
    total = half[0]
    for k in range(1, dim.S // 2):
        total = total + swap(half[k], "seq", 2 * k)
    out = total[0]
    for k in range(1, dim.D):
        out = out + swap(total[k], "dp", k)
    return out


def unpack_kernel(dim, shares, *refs):
    count = len(shares) * dim.S
    pieces, (g_in, g_out, g_glu, vectors) = refs[:count], refs[count:]
    me = lax.axis_index("seq")
    n = -(-2 * SMALL // dim.S)

    def place(layer, kind, rows, value):
        if kind == "in":
            g_in[layer, rows, :] = value
        elif kind == "out":
            g_out[layer, rows, :] = value
        elif kind == "gv":
            g_glu[layer, rows, 0 : dim.H] = value
        else:
            g_glu[layer, rows, dim.H : 2 * dim.H] = value

    for i, (share, kinds) in enumerate(shares):
        for k in range(dim.S):
            src = pieces[i * dim.S + k]
            s = k ^ me

            def one(known):
                for off in range(0, share.q, share.step):
                    p = known * share.q + off
                    m = p // dim.Hd
                    if m < share.nm:
                        layer, kind = kinds[m]
                        r = p % dim.Hd
                        place(layer, kind, slice(r, r + share.step), src[off : off + share.step, :])
                if share.extra:
                    lo = min(known * n, 2 * SMALL - n)
                    vectors[lo : lo + n, :] = src[share.q : share.q + n, :]

            for known in range(dim.S):
                pl.when(s == known)(functools.partial(one, known))


def unpack(dim, shares, pieces):
    args = [p for group in pieces for p in group]
    outs = [f32(dim.layers, dim.Hd, dim.H), f32(dim.layers, dim.Hd, dim.H), f32(dim.layers, dim.Hd, 2 * dim.H),
            f32(2 * SMALL, dim.H)]
    return call(functools.partial(unpack_kernel, dim, shares), outs, [], *args)


def spread(vec, width, my):
    count = width // vec.shape[1]
    lane = lax.broadcasted_iota(jnp.int32, (vec.shape[0], width), 1)
    return jnp.where(lane // vec.shape[1] == my, jnp.tile(vec, (1, count)), 0.0)


def body(inputs, out_grad, ln_gain, ln_bias, nu_log, theta_log, gamma_log, in_map, out_map, skip_gain, glu_weight, glu_bias):
    dim = Dims(inputs, in_map, lax.axis_size("dp"), lax.axis_size("seq"))
    T, H, N, R, B, D, S = dim.T, dim.H, dim.N, dim.R, dim.B, dim.D, dim.S
    me, my = lax.axis_index("seq"), lax.axis_index("dp")
    x = inputs.reshape(R, dim.L, H)
    og = out_grad.reshape(R, dim.L, H)

    both = spread(glu_bias, 2 * H, my)
    small = jnp.stack(
        [
            spread(ln_gain, H, my),
            spread(ln_bias, H, my),
            spread(skip_gain, H, my),
            both[:, :H],
            both[:, H:],
            jnp.concatenate([spread(nu_log, N, my), spread(theta_log, N, my)], 1),
            spread(gamma_log, H, my),
            jnp.zeros_like(ln_gain, shape=(dim.layers, H)),
        ],
        1,
    )
    pieces = []
    table = None
    start = jnp.minimum(me, dim.used - 1) * dim.q
    for layer in range(dim.layers):

        def cut(w, lo):
            return lax.dynamic_slice(w, (layer, start, lo), (1, dim.q, H))[0]

        mine = jnp.concatenate([cut(in_map, 0), cut(out_map, 0), cut(glu_weight, 0), cut(glu_weight, H)], 0)
        if layer == 0:
            mine = jnp.concatenate([small.reshape(-1, H), mine], 0)
        others = [swap(mine, "dp", k) for k in range(1, D)]
        if layer == 0:
            first = dim.layers * SMALL
            total = mine[:first]
            for other in others:
                total = total + other[:first]
            table = call(
                functools.partial(prep_kernel, dim), [f32(dim.layers, TABLE, H)], [], total.reshape(small.shape)
            )[0]
            others = [other[first:] for other in others]
        joined = jnp.stack([other.reshape(4, dim.q, H) for other in others], 1)
        pieces.append(plane_gather(dim, joined))

    unit = 2 * T * H * H
    big, ent, fins = f32(T, H), f32(R, H), f32(B, H)
    stat = f32(T, 128)
    vec = f32(SMALL, H)

    def k(fn, names, outs, scratch, *args, n):
        kernel, count, own = weights_in(dim, names, fn)
        layers = sorted({layer for layer, _ in names})
        sources = [in_map, out_map, glu_weight] + [p for layer in layers for p in pieces[layer]]
        return call(kernel, outs, scratch + own, *sources, *args, flops=3 * n * unit, anywhere=count)

    def carried(fin):
        return lax.all_gather(fin, "seq")

    xhat0, rstd0, drive0, cf0, fin0 = k(
        k_a0, [(0, 0)], [big, stat, big, ent, fins], halves(dim, 1), x, table, n=1
    )
    g0 = carried(fin0)
    en0, states0, mixed0, active0, v0, s0, act1, xhat1, rstd1, drive1, cf1, fin1 = k(
        k_b0,
        [(0, 1), (0, 2), (0, 3), (1, 0)],
        [ent, big, big, big, big, big, big, big, stat, big, ent, fins],
        halves(dim, 1),
        x, table, drive0, cf0, g0, xhat0,
        n=4,
    )
    g1 = carried(fin1)
    spare = [pltpu.VMEM((T, H), F32)]
    out, en1, states1, active1, dv1, dg1, dmixed1, ds1, rcf1, rfin1, sums1a = k(
        k_b1,
        [(1, 1), (1, 2), (1, 3)],
        [f32(R, dim.L, H), ent, big, big, big, big, big, big, ent, fins, vec],
        halves(dim, 2) + spare * 3,
        act1, og, table, drive1, cf1, g1, xhat1,
        n=6,
    )
    gr1 = carried(rfin1)
    share1, share2, share3 = Share(dim, 3), Share(dim, 4), Share(dim, 1, 8)
    tile = [pltpu.VMEM((WIDE, H), F32)]
    pair = [pltpu.VMEM((T, H), BF16)] * 4
    keep1, send1 = call(
        functools.partial(k_w1, dim, share1), [f32(*share1.shape)] * 2, pair + tile,
        active1, dv1, dg1, states1, dmixed1, flops=9 * unit,
    )
    dproj1, dmid, dv0, dg0, dmixed0, ds0, rcf0, rfin0, sums1b, sums0a = k(
        k_c1,
        [(1, 0), (0, 2), (0, 3), (0, 1)],
        [big, big, big, big, big, big, ent, fins, vec, vec],
        halves(dim, 2) + [pltpu.VMEM((R, H), F32)],
        og, table, ds1, rcf1, gr1, states1, en1, drive1, xhat1, rstd1, dmixed1,
        xhat0, mixed0, v0, s0,
        n=4,
    )
    gr0 = carried(rfin0)
    keep2, send2 = call(
        functools.partial(k_w2, dim, share2), [f32(*share2.shape)] * 2, pair + tile,
        active0, dv0, dg0, states0, dmixed0, xhat1, dproj1, table, flops=12 * unit,
    )
    input_grad, keep3, send3 = k(
        functools.partial(k_c0, share3),
        [(0, 0)],
        [f32(R, dim.L, H)] + [f32(*share3.shape)] * 2,
        halves(dim, 2) + [pltpu.VMEM((R, H), F32)] + spare * 2 + [pltpu.VMEM((SMALL, H), F32)] + tile,
        table, ds0, rcf0, gr0, states0, en0, drive0, xhat0, rstd0, dmixed0, dmid, sums1a, sums1b, sums0a,
        n=2,
    )
    shared = [plane_gather(dim, reduce_share(dim, a, b)) for a, b in ((keep1, send1), (keep2, send2), (keep3, send3))]
    kinds1 = [(1, "gv"), (1, "gg"), (1, "out")]
    kinds2 = [(0, "gv"), (0, "gg"), (0, "out"), (1, "in")]
    kinds3 = [(0, "in")]
    g_in, g_out, g_glu, vectors = unpack(
        dim, [(share1, kinds1), (share2, kinds2), (share3, kinds3)], shared
    )
    vectors = vectors.reshape(2, SMALL, H)

    def own(index, lo, width, total):
        rows = vectors[:, index, lo : lo + width]
        part = width // D if total is None else total
        return lax.dynamic_slice_in_dim(rows, my * part, part, 1)

    glu_rows = jnp.concatenate([vectors[:, BIAS_V], vectors[:, BIAS_G]], 1)
    part = 2 * H // D
    return (
        out.reshape(inputs.shape),
        input_grad.reshape(inputs.shape),
        own(GAIN, 0, H, None),
        own(BIAS, 0, H, None),
        own(5, 0, N, None),
        own(5, N, N, None),
        own(6, 0, N, None),
        g_in,
        g_out,
        own(SKIP, 0, H, None),
        g_glu,
        lax.dynamic_slice_in_dim(glu_rows, my * part, part, 1),
    )


def solution(mesh):
    act, vec, mat = P("dp", "seq", None), P(None, "dp"), P(None, "dp", None)
    in_specs = (act, act, vec, vec, vec, vec, vec, mat, mat, vec, mat, vec)
    out_specs = (act, act, vec, vec, vec, vec, vec, mat, mat, vec, mat, vec)
    return jax.shard_map(body, mesh=mesh, in_specs=in_specs, out_specs=out_specs, check_vma=False)
```

```python
import functools
import math

import jax
import jax.numpy as jnp
from jax import lax
from jax.experimental import pallas as pl
from jax.experimental.pallas import tpu as pltpu
from jax.sharding import PartitionSpec as P

NORM_EPS = 1e-05
GROUPS = 8
WIDE = 256
SMALL = 8
TABLE = 16
F32 = jnp.float32
BF16 = jnp.bfloat16
GELU_C = math.sqrt(2.0 / math.pi)

GAIN, BIAS, SKIP, BIAS_V, BIAS_G, GAMMA, LAM, LAM1, LAM2, LAM4, LAM8, RATES = range(12)


CHUNKS = (((0, 0),), ((0, 1), (0, 2), (0, 3), (1, 0)), ((1, 1), (1, 2), (1, 3)))


class Dims:
    def __init__(self, inputs, in_map, dp, seq):
        self.B, self.Tb, self.H = inputs.shape
        self.layers, self.Hd = in_map.shape[:2]
        self.N = self.H // 2
        self.T = self.B * self.Tb
        self.R = self.B * GROUPS
        self.L = self.Tb // GROUPS
        self.D, self.S = dp, seq
        self.q = max(16, self.Hd // seq)
        self.used = self.Hd // self.q


def cmul(ar, ai, br, bi):
    return ar * br - ai * bi, ar * bi + ai * br


def split(x):
    hi = x.astype(BF16)
    return hi, (x - hi.astype(F32)).astype(BF16)


def dot3(ah, al, bh, bl, dims):
    def one(a, b):
        return lax.dot_general(a, b, (dims, ((), ())), preferred_element_type=F32)

    return one(ah, bh) + (one(ah, bl) + one(al, bh))


def product(ah, al, wh, wl, dst, transposed=False, add=False):
    for n in range(dst.shape[1] // WIDE):
        cols = slice(n * WIDE, (n + 1) * WIDE)
        if transposed:
            res = dot3(ah[...], al[...], wh[cols, :], wl[cols, :], ((1,), (1,)))
        else:
            res = dot3(ah[...], al[...], wh[:, cols], wl[:, cols], ((1,), (0,)))
        dst[:, cols] = dst[:, cols] + res if add else res


def each_step(dim, fn, unroll=2, reverse=False, init=0):
    def one(i, carry):
        j = dim.L - 1 - i if reverse else i
        rows = pl.ds(pl.multiple_of(j * dim.R, dim.R), dim.R)
        return fn(j, rows, carry)

    return lax.fori_loop(0, dim.L, one, init, unroll=unroll)


def row(table, index, n=1):
    return table[index : index + n, :]


def lam_of(dim, table, index, reverse):
    pair = table[index : index + 1, :]
    real, imag = pair[:, : dim.N], pair[:, dim.N :]
    return real, -imag if reverse else imag


def chunk_scan(dim, table, yr, yi, reverse):
    place = lax.broadcasted_iota(jnp.int32, yr.shape, 0)
    for dist, index in ((1, LAM1), (2, LAM2), (4, LAM4)):
        pr, pi = lam_of(dim, table, index, reverse)
        if reverse:
            shift, seen = GROUPS - dist, place < GROUPS - dist
        else:
            shift, seen = dist, place >= dist
        sr = jnp.where(seen, pltpu.roll(yr, shift, 0), 0.0)
        si = jnp.where(seen, pltpu.roll(yi, shift, 0), 0.0)
        mr, mi = cmul(pr, pi, sr, si)
        yr, yi = yr + mr, yi + mi
    return yr, yi


def local_finals(dim, table, drive_ref, cf_ref, f_ref, reverse):
    lr, li = lam_of(dim, table, LAM, reverse)
    lr = jnp.broadcast_to(lr, (dim.R, dim.N))
    li = jnp.broadcast_to(li, (dim.R, dim.N))

    def step(j, rows, carry):
        d = drive_ref[rows, :]
        mr, mi = cmul(lr, li, *carry)
        return mr + d[:, : dim.N], mi + d[:, dim.N :]

    zero = jnp.zeros((dim.R, dim.N), F32)
    fr, fi = each_step(dim, step, 4, reverse, (zero, zero))
    cf_ref[:, : dim.N] = fr
    cf_ref[:, dim.N :] = fi
    last = 0 if reverse else GROUPS - 1
    for b in range(dim.B):
        rows = slice(b * GROUPS, (b + 1) * GROUPS)
        yr, yi = chunk_scan(dim, table, fr[rows], fi[rows], reverse)
        f_ref[b : b + 1, : dim.N] = yr[last : last + 1]
        f_ref[b : b + 1, dim.N :] = yi[last : last + 1]


def entries_of(dim, table, cf_ref, g_ref, en_ref, reverse):
    me = lax.axis_index("seq")
    lr, li = lam_of(dim, table, LAM8, reverse)
    xr = jnp.zeros((dim.B, dim.N), F32)
    xi = xr
    order = reversed(range(dim.S)) if reverse else range(dim.S)
    for other in order:
        ahead = other > me if reverse else other < me
        g = g_ref[other]
        mr, mi = cmul(lr, li, xr, xi)
        xr = jnp.where(ahead, mr + g[:, : dim.N], xr)
        xi = jnp.where(ahead, mi + g[:, dim.N :], xi)
    for b in range(dim.B):
        rows = slice(b * GROUPS, (b + 1) * GROUPS)
        f = cf_ref[rows, :]
        place = lax.broadcasted_iota(jnp.int32, f.shape, 0)
        x = jnp.concatenate([xr[b : b + 1], xi[b : b + 1]], 1)
        if reverse:
            y = jnp.where(place == GROUPS - 1, x, pltpu.roll(f, GROUPS - 1, 0))
        else:
            y = jnp.where(place == 0, x, pltpu.roll(f, 1, 0))
        yr, yi = chunk_scan(dim, table, y[:, : dim.N], y[:, dim.N :], reverse)
        en_ref[rows, : dim.N] = yr
        en_ref[rows, dim.N :] = yi


def norm_step(dim, x, table):
    mean = jnp.mean(x, -1, keepdims=True)
    centred = x - mean
    var = jnp.mean(centred * centred, -1, keepdims=True)
    rstd = lax.rsqrt(var + NORM_EPS)
    xhat = centred * rstd
    return xhat, rstd, xhat * row(table, GAIN) + row(table, BIAS)


def front(dim, load_act, table, w_in, xhat, rstd, drive, cf, fin, ah, al, wh, wl):
    def norm(j, rows, _):
        xh, rs, normed = norm_step(dim, load_act(j, rows), table)
        xhat[rows, :] = xh
        rstd[rows, :] = jnp.broadcast_to(rs, (dim.R, 128))
        ah[rows, :], al[rows, :] = split(normed)
        return 0

    each_step(dim, norm, 4)
    w_in.fill(wh, wl)
    product(ah, al, wh, wl, drive)

    def scale(j, rows, _):
        drive[rows, :] = drive[rows, :] * row(table, GAMMA)
        return 0

    each_step(dim, scale, 4)
    local_finals(dim, table, drive, cf, fin, False)


def gelu_parts(m):
    inner = GELU_C * (m + 0.044715 * (m * m * m))
    th = jnp.tanh(inner)
    return th


def back(dim, table, drive, cf, g, xhat, w_out, w_gv, w_gg, en, states, mixed, active, v, s, ah, al, wh, wl):
    entries_of(dim, table, cf, g, en, False)
    lr, li = lam_of(dim, table, LAM, False)
    lr = jnp.broadcast_to(lr, (dim.R, dim.N))
    li = jnp.broadcast_to(li, (dim.R, dim.N))

    def scan(j, rows, carry):
        d = drive[rows, :]
        mr, mi = cmul(lr, li, *carry)
        both = jnp.concatenate([mr + d[:, : dim.N], mi + d[:, dim.N :]], 1)
        states[rows, :] = both
        ah[rows, :], al[rows, :] = split(both)
        return both[:, : dim.N], both[:, dim.N :]

    each_step(dim, scan, 4, False, (en[:, : dim.N], en[:, dim.N :]))
    w_out.fill(wh, wl)
    product(ah, al, wh, wl, mixed)

    def gelu(j, rows, _):
        normed = xhat[rows, :] * row(table, GAIN) + row(table, BIAS)
        m = mixed[rows, :] + row(table, SKIP) * normed
        mixed[rows, :] = m
        a = (0.5 * m) * (1.0 + gelu_parts(m))
        active[rows, :] = a
        ah[rows, :], al[rows, :] = split(a)
        return 0

    each_step(dim, gelu, 2)
    w_gv.fill(wh, wl)
    product(ah, al, wh, wl, v)
    w_gg.fill(wh, wl)
    product(ah, al, wh, wl, s)


def gate(dim, table, v, s, rows):
    vv = v[rows, :] + row(table, BIAS_V)
    ss = jax.nn.sigmoid(s[rows, :] + row(table, BIAS_G))
    v[rows, :] = vv
    s[rows, :] = ss
    return vv * ss


def top(dim, table, load_dact, v, s, mixed, xhat, w_gv, w_gg, w_out, dv, dg, dmixed, ds, rcf, rfin, sums, ah, al, bh, bl, wh, wl):
    def dgate(j, rows, carry):
        dact = load_dact(j, rows)
        ss, vv = s[rows, :], v[rows, :]
        a = dact * ss
        b = a * vv * (1.0 - ss)
        dv[rows, :] = a
        dg[rows, :] = b
        ah[rows, :], al[rows, :] = split(a)
        bh[rows, :], bl[rows, :] = split(b)
        return carry[0] + a, carry[1] + b

    zero = jnp.zeros((dim.R, dim.H), F32)
    sv, sg = each_step(dim, dgate, 2, False, (zero, zero))
    sums[BIAS_V : BIAS_V + 1, :] = jnp.sum(sv, 0, keepdims=True)
    sums[BIAS_G : BIAS_G + 1, :] = jnp.sum(sg, 0, keepdims=True)
    w_gv.fill(wh, wl)
    product(ah, al, wh, wl, dmixed, True)
    w_gg.fill(wh, wl)
    product(bh, bl, wh, wl, dmixed, True, True)

    def dgelu(j, rows, carry):
        m = mixed[rows, :]
        th = gelu_parts(m)
        slope = 0.5 * (1.0 + th) + (0.5 * m) * (1.0 - th * th) * (GELU_C * (1.0 + (3 * 0.044715) * (m * m)))
        d = dmixed[rows, :] * slope
        dmixed[rows, :] = d
        ah[rows, :], al[rows, :] = split(d)
        normed = xhat[rows, :] * row(table, GAIN) + row(table, BIAS)
        return carry + d * normed

    sums[SKIP : SKIP + 1, :] = jnp.sum(each_step(dim, dgelu, 2, False, zero), 0, keepdims=True)
    w_out.fill(wh, wl)
    product(ah, al, wh, wl, ds, True)
    local_finals(dim, table, ds, rcf, rfin, True)


def bottom(dim, table, ds, rcf, gr, states, en, drive, xhat, rstd, dmixed, w_in, load_dact, store, dproj, buf, adj_en, sums, ah, al, wh, wl):
    entries_of(dim, table, rcf, gr, adj_en, True)
    lr, li = lam_of(dim, table, LAM, True)
    lr = jnp.broadcast_to(lr, (dim.R, dim.N))
    li = jnp.broadcast_to(li, (dim.R, dim.N))
    zero = jnp.zeros((dim.R, dim.N), F32)

    def scan(j, rows, carry):
        ar, ai, dr, di, dgam = carry
        d = ds[rows, :]
        mr, mi = cmul(lr, li, ar, ai)
        ar, ai = mr + d[:, : dim.N], mi + d[:, dim.N :]
        earlier = pl.ds(pl.multiple_of(jnp.maximum(j - 1, 0) * dim.R, dim.R), dim.R)
        before = jnp.where(j == 0, en[...], states[earlier, :])
        br, bi = before[:, : dim.N], before[:, dim.N :]
        dr = dr + (ar * br + ai * bi)
        di = di + (ai * br - ar * bi)
        u = drive[rows, :]
        dgam = dgam + (ar * u[:, : dim.N] + ai * u[:, dim.N :])
        dp = jnp.concatenate([ar, ai], 1) * row(table, GAMMA)
        dproj[rows, :] = dp
        ah[rows, :], al[rows, :] = split(dp)
        return ar, ai, dr, di, dgam

    start = (adj_en[:, : dim.N], adj_en[:, dim.N :], zero, zero, zero)
    _, _, dr, di, dgam = each_step(dim, scan, 2, True, start)
    dr, di, dgam = (jnp.sum(x, 0, keepdims=True) for x in (dr, di, dgam))
    fr, fi = lam_of(dim, table, LAM, False)
    rates = row(table, RATES)
    rate, angle = rates[:, : dim.N], rates[:, dim.N :]
    sums[5:6, : dim.N] = -rate * (dr * fr + di * fi)
    sums[5:6, dim.N :] = angle * (di * fr - dr * fi)
    sums[6:7, : dim.N] = dgam
    sums[6:7, dim.N :] = jnp.zeros_like(dgam)
    sums[7:8, :] = jnp.zeros((1, dim.H), F32)

    w_in.fill(wh, wl)
    product(ah, al, wh, wl, buf, True)
    wide = jnp.zeros((dim.R, dim.H), F32)

    def dnorm(j, rows, carry):
        dn = buf[rows, :] + dmixed[rows, :] * row(table, SKIP)
        xh = xhat[rows, :]
        dx = dn * row(table, GAIN)
        m1 = jnp.mean(dx, -1, keepdims=True)
        m2 = jnp.mean(dx * xh, -1, keepdims=True)
        store(j, rows, load_dact(j, rows) + rstd[rows, 0:1] * (dx - m1 - xh * m2))
        return carry[0] + dn * xh, carry[1] + dn

    sgain, sbias = each_step(dim, dnorm, 2, False, (wide, wide))
    sums[GAIN : GAIN + 1, :] = jnp.sum(sgain, 0, keepdims=True)
    sums[BIAS : BIAS + 1, :] = jnp.sum(sbias, 0, keepdims=True)


def split_rows(dim, load, xh, xl):
    def one(j, rows, _):
        xh[rows, :], xl[rows, :] = split(load(rows))
        return 0

    each_step(dim, one, 4)


class Share:
    def __init__(self, dim, nm):
        self.dim, self.nm = dim, nm
        self.q = -(-nm * dim.Hd // (8 * dim.S)) * 8
        self.step = math.gcd(self.q, dim.Hd)
        self.shape = (dim.S // 2, dim.D, self.q, dim.H)

    def place(self, m, d, r, me, my):
        p = m * self.dim.Hd + r
        s = p // self.q
        return s & 1, ((s ^ me) >> 1, d ^ my), p % self.q


class Halves:
    def __init__(self, dim):
        self.dim = dim
        self.q = dim.Hd // 2
        self.step = math.gcd(self.q, WIDE)
        self.shape = (dim.D, self.q + SMALL, dim.H)

    def place(self, m, d, r, me, my):
        return r // self.q, (d ^ my,), r % self.q


def weight_grad(dim, share, m, ah, al, bh, bl, tile, keep, send):
    me = lax.axis_index("seq")
    my = lax.axis_index("dp")
    for h0 in range(0, dim.H, WIDE):
        tile[...] = dot3(ah[:, h0 : h0 + WIDE], al[:, h0 : h0 + WIDE], bh[...], bl[...], ((0,), (0,)))

        def put(mine):
            for r0 in range(0, WIDE, share.step):
                h = h0 + r0
                odd, index, off = share.place(m, h // dim.Hd, h % dim.Hd, me, my)
                dst = keep if odd == mine else send
                dst[(*index, slice(off, off + share.step), slice(None))] = tile[r0 : r0 + share.step, :]

        for mine in range(2):
            pl.when(me & 1 == mine)(functools.partial(put, mine))


class Kept:
    def __init__(self, value):
        self.value = value
        self.shape = value.shape


def call(fn, outs, scratch, *args, us=1.0, anywhere=0):
    spaces = [pltpu.HBM] * anywhere + [pltpu.VMEM] * (len(args) - anywhere)

    def placed(x, space):
        if isinstance(x, Kept):
            return pltpu.with_memory_space_constraint(x.value, pltpu.VMEM)
        return pltpu.with_memory_space_constraint(x, pltpu.HBM) if space is pltpu.HBM else x

    values = [placed(x, space) for x, space in zip(args, spaces)]
    room = 10 << 20
    for x in scratch:
        if len(x.shape) > 1:
            room += math.prod(x.shape) * (2 if x.dtype == BF16 else 4)
    results = pl.pallas_call(
        fn,
        out_shape=outs,
        in_specs=[pl.BlockSpec(memory_space=space) for space in spaces],
        out_specs=[pl.BlockSpec(memory_space=pltpu.VMEM)] * len(outs),
        scratch_shapes=scratch,
        compiler_params=pltpu.CompilerParams(vmem_limit_bytes=max(20 << 20, room)),
        cost_estimate=pl.CostEstimate(flops=1, bytes_accessed=int(us * 3.6e6), transcendentals=0),
    )(*values)
    return [x if isinstance(o, jax.ShapeDtypeStruct) else Kept(x) for x, o in zip(results, outs)]


def f32(*shape):
    return jax.ShapeDtypeStruct(shape, F32)


def halves(dim, n):
    return [pltpu.VMEM((dim.T, dim.H), BF16)] * (2 * n) + [pltpu.VMEM((dim.H, dim.H), BF16)] * 2


def prep_kernel(dim, small, table):
    s = small[...]
    nu, theta, gam = s[5:6, : dim.N], s[5:6, dim.N :], s[6:7, : dim.N]
    rate, angle = jnp.exp(nu), jnp.exp(theta)
    mod = jnp.exp(-rate)
    re, im = mod * jnp.cos(angle), mod * jnp.sin(angle)
    gamma = jnp.exp(gam)

    def put(index, a, b):
        table[index : index + 1, : dim.N] = a
        table[index : index + 1, dim.N :] = b

    table[...] = jnp.zeros((TABLE, dim.H), F32)
    table[:5, :] = s[:5]
    put(GAMMA, gamma, gamma)
    put(LAM, re, im)
    put(RATES, rate, angle)
    power = 1
    while power < dim.L:
        re, im = cmul(re, im, re, im)
        power *= 2
    for index in (LAM1, LAM2, LAM4, LAM8):
        put(index, re, im)
        re, im = cmul(re, im, re, im)


def shard_of(sources, name, rows, H):
    layer, m = name
    return sources[(0, 1, 2, 2)[m]].at[layer, rows, pl.ds(H if m == 3 else 0, H)]


def pack_kernel(dim, in_map, out_map, glu, gain, bias, skip, nu, theta, gamma, glu_bias, *refs):
    outs, held, sem = refs[:3], refs[3:-1], refs[-1]
    vectors = (gain, bias, skip, nu, theta, gamma, glu_bias)
    me, my = lax.axis_index("seq"), lax.axis_index("dp")
    start = pl.multiple_of(jnp.minimum(me, dim.used - 1) * dim.q, 16)
    moves = []
    for src, dst in zip(vectors, held):
        moves.append(pltpu.make_async_copy(src, dst, sem.at[len(moves)]))
    gain, bias, skip, nu, theta, gamma, glu_bias = held
    for out, chunk in zip(outs, CHUNKS):
        head = out.shape[0] - len(chunk) * dim.q
        for i, name in enumerate(chunk):
            src = shard_of((in_map, out_map, glu), name, pl.ds(start, dim.q), dim.H)
            dst = out.at[head + i * dim.q : head + (i + 1) * dim.q, :]
            moves.append(pltpu.make_async_copy(src, dst, sem.at[len(moves)]))
    for move in moves:
        move.start()
    for move in moves[: len(held)]:
        move.wait()

    def spread(ref, layer, width):
        vec = ref[layer : layer + 1, :]
        full = jnp.concatenate([vec] * (width // vec.shape[1]), 1)
        lane = lax.broadcasted_iota(jnp.int32, full.shape, 1)
        return jnp.where(lane // vec.shape[1] == my, full, 0.0)

    for layer in range(dim.layers):
        both = spread(glu_bias, layer, 2 * dim.H)
        rows = [spread(ref, layer, dim.H) for ref in (gain, bias, skip)] + [both[:, : dim.H], both[:, dim.H :]]
        rows.append(jnp.concatenate([spread(nu, layer, dim.N), spread(theta, layer, dim.N)], 1))
        rows.append(jnp.concatenate([spread(gamma, layer, dim.N), jnp.zeros((1, dim.N), F32)], 1))
        for i, value in enumerate(rows):
            outs[layer][i : i + 1, :] = value
        outs[layer][7:8, :] = jnp.zeros((1, dim.H), F32)
    for move in moves[len(held) :]:
        move.wait()


class Weight:
    def __init__(self, dim, name, place, sources, own, buf, sem):
        self.dim, self.name, self.place = dim, name, place
        self.sources, self.own, self.buf, self.sem = sources, own, buf, sem
        self.here = False

    def moves(self):
        shard = shard_of(self.sources, self.name, slice(None), self.dim.H)
        yield pltpu.make_async_copy(shard, self.own, self.sem.at[self.dim.S])
        for k, piece in enumerate(self.sources[3:]):
            yield pltpu.make_async_copy(piece.at[self.place], self.buf.at[k], self.sem.at[k])

    def start(self):
        for move in self.moves():
            move.start()

    def fill(self, wh, wl):
        dim, q = self.dim, self.dim.q
        if not self.here:
            for move in self.moves():
                move.wait()
        self.here = True
        me, my = lax.axis_index("seq"), lax.axis_index("dp")

        def put(start, n, value):
            rows = pl.ds(pl.multiple_of(start, 16), n)
            wh[rows, :], wl[rows, :] = split(value)

        def mine(i, _):
            put(my * dim.Hd + i * 32, 32, self.own[pl.ds(pl.multiple_of(i * 32, 32), 32), :])
            return 0

        lax.fori_loop(0, dim.Hd // 32, mine, 0)

        def one(k, _):
            s = k ^ me

            def block():
                for kz in range(1, dim.D):
                    put((kz ^ my) * dim.Hd + s * q, q, self.buf[k, kz - 1])

            if dim.used < dim.S:
                pl.when(s < dim.used)(block)
            else:
                block()
            return 0

        lax.fori_loop(0, dim.S, one, 0)


def weights_in(dim, chunk, names, fn):
    first = 3 + dim.S

    def kernel(*refs):
        spare = refs[len(refs) - 3 * len(names) :]
        weights = [
            Weight(dim, name, CHUNKS[chunk].index(name), refs[:first], *spare[3 * i : 3 * i + 3])
            for i, name in enumerate(names)
        ]
        for w in weights:
            w.start()
        fn(dim, weights, *refs[first : len(refs) - 3 * len(names)])

    scratch = [
        pltpu.VMEM((dim.Hd, dim.H), F32),
        pltpu.VMEM((dim.S, dim.D - 1, dim.q, dim.H), F32),
        pltpu.SemaphoreType.DMA((dim.S + 1,)),
    ] * len(names)
    return kernel, first, scratch


def strided(dim, ref):
    return lambda j, rows: ref[:, j, :]


def plain(ref):
    return lambda j, rows: ref[rows, :]


def k_a0(dim, weights, x, table, xhat, rstd, drive, cf, fin, ah, al, wh, wl):
    front(dim, strided(dim, x), table, weights[0], xhat, rstd, drive, cf, fin, ah, al, wh, wl)


def k_b0(dim, weights, x, t, t1, drive, cf, g, xhat,
         en, states, mixed, active, v, s, act1, xhat1, rstd1, drive1, cf1, fin1, ah, al, wh, wl):
    w_out, w_gv, w_gg, w_in1 = weights
    back(dim, t, drive, cf, g, xhat, w_out, w_gv, w_gg, en, states, mixed, active, v, s, ah, al, wh, wl)
    load = strided(dim, x)

    def residual(j, rows):
        act = load(j, rows) + gate(dim, t, v, s, rows)
        act1[rows, :] = act
        return act

    front(dim, residual, t1, w_in1, xhat1, rstd1, drive1, cf1, fin1, ah, al, wh, wl)


def k_b1(dim, weights, act1, out_grad, t, drive, cf, g, xhat,
         out, en, states, active, dv, dg, dmixed, ds, rcf, rfin, sums, ah, al, bh, bl, wh, wl, mixed, v, s):
    w_out, w_gv, w_gg = weights
    back(dim, t, drive, cf, g, xhat, w_out, w_gv, w_gg, en, states, mixed, active, v, s, ah, al, wh, wl)

    def residual(j, rows, _):
        out[:, j, :] = act1[rows, :] + gate(dim, t, v, s, rows)
        return 0

    each_step(dim, residual, 2)
    sums[...] = jnp.zeros((SMALL, dim.H), F32)
    top(dim, t, strided(dim, out_grad), v, s, mixed, xhat, w_gv, w_gg, w_out, dv, dg, dmixed, ds, rcf, rfin, sums,
        ah, al, bh, bl, wh, wl)


def k_w1(dim, share, active, dv, dg, states, dmixed, keep, send, ah, al, bh, bl, tile):
    split_rows(dim, lambda rows: active[rows, :], ah, al)
    for m, ref in ((0, dv), (1, dg)):
        split_rows(dim, lambda rows: ref[rows, :], bh, bl)
        weight_grad(dim, share, m, ah, al, bh, bl, tile, keep, send)
    split_rows(dim, lambda rows: states[rows, :], ah, al)
    split_rows(dim, lambda rows: dmixed[rows, :], bh, bl)
    weight_grad(dim, share, 2, ah, al, bh, bl, tile, keep, send)


def k_c1(dim, weights, out_grad, t, t0, ds, rcf, gr, states, en, drive, xhat, rstd, dmixed,
         xhat0, mixed0, v0, s0,
         dproj, dmid, dv0, dg0, dmixed0, ds0, rcf0, rfin0, sums1, sums0, ah, al, bh, bl, wh, wl, adj_en):
    w_in, w_gv, w_gg, w_out = weights

    def store(j, rows, value):
        dmid[rows, :] = value

    bottom(dim, t, ds, rcf, gr, states, en, drive, xhat, rstd, dmixed, w_in, strided(dim, out_grad), store,
           dproj, ds0, adj_en, sums1, ah, al, wh, wl)
    sums0[...] = jnp.zeros((SMALL, dim.H), F32)
    top(dim, t0, plain(dmid), v0, s0, mixed0, xhat0, w_gv, w_gg, w_out, dv0, dg0, dmixed0, ds0, rcf0, rfin0,
        sums0, ah, al, bh, bl, wh, wl)


def k_w2(dim, share, active, dv, dg, states, dmixed, xhat1, dproj1, t, keep, send, ah, al, bh, bl, tile):
    k_w1(dim, share, active, dv, dg, states, dmixed, keep, send, ah, al, bh, bl, tile)
    split_rows(dim, lambda rows: xhat1[rows, :] * row(t, GAIN) + row(t, BIAS), ah, al)
    split_rows(dim, lambda rows: dproj1[rows, :], bh, bl)
    weight_grad(dim, share, 3, ah, al, bh, bl, tile, keep, send)


def k_c0(share, dim, weights, t, ds, rcf, gr, states, en, drive, xhat, rstd, dmixed, dmid, sums1a, sums1b, sums0a,
         input_grad, keep, send, ah, al, bh, bl, wh, wl, adj_en, dproj, buf, sums0, tile):
    def store(j, rows, value):
        input_grad[:, j, :] = value

    bottom(dim, t, ds, rcf, gr, states, en, drive, xhat, rstd, dmixed, weights[0], plain(dmid), store, dproj, buf, adj_en,
           sums0, ah, al, wh, wl)
    split_rows(dim, lambda rows: xhat[rows, :] * row(t, GAIN) + row(t, BIAS), bh, bl)
    weight_grad(dim, share, 0, bh, bl, ah, al, tile, keep, send)
    place = lax.broadcasted_iota(jnp.int32, (SMALL, dim.H), 0)
    upper = (place >= SKIP) & (place <= BIAS_G)
    tile[0:SMALL, :] = jnp.where(upper, sums0a[...], sums0[...])
    tile[SMALL : 2 * SMALL, :] = jnp.where(upper, sums1a[...], sums1b[...])
    me = lax.axis_index("seq")

    def put(mine):
        for layer in range(dim.layers):
            dst = keep if layer == mine else send
            for d in range(dim.D):
                dst[d, share.q :, :] = tile[layer * SMALL : (layer + 1) * SMALL, :]

    for mine in range(2):
        pl.when(me & 1 == mine)(functools.partial(put, mine))


def tie(x, others):
    x, *others = lax.optimization_barrier((x, *others))
    return x, others


def swap(x, axis, mask):
    count = lax.axis_size(axis)
    return lax.ppermute(x, axis, [(i, i ^ mask) for i in range(count)])


def chips_gather(dim, x):
    return [x] + [swap(x, "seq", k) for k in range(2, dim.S, 2)]


def cores_gather(pieces):
    return [p for x in pieces for p in (x, swap(x, "seq", 1))]


def plane_gather(dim, x):
    return cores_gather(chips_gather(dim, x))


def tree_sum(parts):
    while len(parts) > 1:
        parts = [a + b for a, b in zip(parts[::2], parts[1::2])]
    return parts[0]


def half_sums(dim, keep, send):
    got = swap(send, "seq", 1)
    return [keep[k] + got[k] for k in range(dim.S // 2)]


def plane_sums(dim, half):
    others = [swap(half[k], "seq", 2 * k) for k in range(1, dim.S // 2)]
    return [sum((o[k] for o in others), half[0][k]) for k in range(dim.D)]


def dp_sum(dim, parts):
    return sum((swap(parts[k], "dp", k) for k in range(1, dim.D)), parts[0])


def unpack_kernel(dim, shares, kinds, last, *refs):
    pieces, (mine, other), outs = refs[: dim.S], refs[dim.S : dim.S + 2], refs[dim.S + 2 :]
    g_gain, g_bias, g_nu, g_theta, g_gamma, g_in, g_out, g_skip, g_glu, g_glu_bias = outs
    me, my = lax.axis_index("seq"), lax.axis_index("dp")

    def place(layer, kind, rows, value):
        if kind == "in":
            g_in[layer, rows, :] = value
        elif kind == "out":
            g_out[layer, rows, :] = value
        elif kind == "gv":
            g_glu[layer, rows, 0 : dim.H] = value
        else:
            g_glu[layer, rows, dim.H : 2 * dim.H] = value

    def put(k, s):
        base = 0
        for share, names in zip(shares, kinds):
            for off in range(0, share.q, share.step):
                p = s * share.q + off
                if p // dim.Hd < share.nm:
                    layer, kind = names[p // dim.Hd]
                    r = p % dim.Hd
                    place(layer, kind, slice(r, r + share.step), pieces[k][base + off : base + off + share.step, :])
            base += share.q

    def vectors(d):
        def own(layer, index, lo, width, out, at=0):
            src = (mine, other)

            def copy(ref):
                start = lo + d * width
                out[layer : layer + 1, :] = ref[last.q + index : last.q + index + 1, start : start + width]

            pl.when(me & 1 == layer)(functools.partial(copy, src[0]))
            pl.when(me & 1 != layer)(functools.partial(copy, src[1]))

        for layer in range(dim.layers):
            for index, out in ((GAIN, g_gain), (BIAS, g_bias), (SKIP, g_skip)):
                own(layer, index, 0, dim.Hd, out)
            n = dim.N // dim.D
            own(layer, 5, 0, n, g_nu)
            own(layer, 5, dim.N, n, g_theta)
            own(layer, 6, 0, n, g_gamma)
            width = 2 * dim.H // dim.D
            index = BIAS_V if d * width < dim.H else BIAS_G
            own(layer, index, 0 if index == BIAS_V else -dim.H, width, g_glu_bias)

    for who in range(dim.S):

        def all_of(who=who):
            for k in range(dim.S):
                put(k, k ^ who)
            half = who & 1
            for ref, part in ((mine, half), (other, 1 - half)):
                place(0, "in", slice(part * last.q, (part + 1) * last.q), ref[: last.q, :])

        pl.when(me == who)(all_of)
    for d in range(dim.D):
        pl.when(my == d)(functools.partial(vectors, d))


def unpack(dim, shares, kinds, last, pieces, mine, other):
    n, l = dim.N // dim.D, dim.layers
    vec, small = f32(l, dim.Hd), f32(l, n)
    mat, wide = f32(l, dim.Hd, dim.H), f32(l, dim.Hd, 2 * dim.H)
    outs = [vec, vec, small, small, small, mat, mat, vec, wide, f32(l, 2 * dim.H // dim.D)]
    return call(functools.partial(unpack_kernel, dim, shares, kinds, last), outs, [], *pieces, mine, other)


def body(inputs, out_grad, ln_gain, ln_bias, nu_log, theta_log, gamma_log, in_map, out_map, skip_gain, glu_weight, glu_bias):
    dim = Dims(inputs, in_map, lax.axis_size("dp"), lax.axis_size("seq"))
    T, H, N, R, B, D, S = dim.T, dim.H, dim.N, dim.R, dim.B, dim.D, dim.S
    me, my = lax.axis_index("seq"), lax.axis_index("dp")
    x = inputs.reshape(R, dim.L, H)
    og = out_grad.reshape(R, dim.L, H)

    heads = [SMALL, SMALL, 0]
    vectors = (ln_gain, ln_bias, skip_gain, nu_log, theta_log, gamma_log, glu_bias)
    messages = call(
        functools.partial(pack_kernel, dim),
        [f32(head + len(chunk) * dim.q, H) for head, chunk in zip(heads, CHUNKS)],
        [pltpu.VMEM(v.shape, F32) for v in vectors] + [pltpu.SemaphoreType.DMA((len(vectors) + sum(map(len, CHUNKS)),))],
        in_map, out_map, glu_weight, *vectors,
        anywhere=3 + len(vectors),
    )
    def stacked(others, head):
        return jnp.stack([other[head:].reshape(-1, dim.q, H) for other in others], 1)

    def along_dp(mine):
        return [swap(mine, "dp", k) for k in range(1, D)]

    def table_of(mine, others, head=SMALL):
        total = mine[:head]
        for other in others:
            total = total + other[:head]
        return call(functools.partial(prep_kernel, dim), [f32(TABLE, H)], [], total)[0]

    mine0, mine1, mine2 = messages
    others0 = along_dp(mine0)
    table0 = table_of(mine0, others0)
    mine1, others0 = tie(mine1, others0)
    others1 = along_dp(mine1)
    table1 = table_of(mine1, others1)
    chips0 = chips_gather(dim, stacked(others0, SMALL))
    joined1, chips0 = tie(stacked(others1, SMALL), chips0)
    pieces0 = cores_gather(chips0)
    chips1 = chips_gather(dim, joined1)
    mine2, (chips1[1],) = tie(mine2, [chips1[1]])
    joined2 = stacked(along_dp(mine2), 0)
    pieces = [pieces0, cores_gather(chips1), None]

    big, ent, fins = pltpu.VMEM((T, H), F32), pltpu.VMEM((R, H), F32), f32(B, H)
    stat = pltpu.VMEM((T, 128), F32)
    vec = pltpu.VMEM((SMALL, H), F32)

    def k(fn, chunk, names, outs, scratch, *args, us):
        kernel, count, own = weights_in(dim, chunk, names, fn)
        sources = [in_map, out_map, glu_weight] + pieces[chunk]
        return call(kernel, outs, scratch + own, *sources, *args, us=us, anywhere=count)

    def carried(fin):
        return lax.all_gather(fin, "seq")

    xhat0, rstd0, drive0, cf0, fin0 = k(
        k_a0, 0, [(0, 0)], [big, stat, big, ent, fins], halves(dim, 1), x, table0, us=3.4
    )
    g0 = carried(fin0)
    joined2, (g0,) = tie(joined2, [g0])
    chips2 = chips_gather(dim, joined2)
    en0, states0, mixed0, active0, v0, s0, act1, xhat1, rstd1, drive1, cf1, fin1 = k(
        k_b0,
        1,
        [(0, 1), (0, 2), (0, 3), (1, 0)],
        [ent, big, big, big, big, big, big, big, stat, big, ent, fins],
        halves(dim, 1),
        x, table0, table1, drive0, cf0, g0, xhat0,
        us=10.0,
    )
    fin1, chips2 = tie(fin1, chips2)
    g1 = carried(fin1)
    pieces[2] = cores_gather(chips2)
    spare = [pltpu.VMEM((T, H), F32)]
    out, en1, states1, active1, dv1, dg1, dmixed1, ds1, rcf1, rfin1, sums1a = k(
        k_b1,
        2,
        [(1, 1), (1, 2), (1, 3)],
        [f32(R, dim.L, H), ent, big, big, big, big, big, big, ent, fins, vec],
        halves(dim, 2) + spare * 3,
        act1, og, table1, drive1, cf1, g1, xhat1,
        us=13.0,
    )
    share1, share2, share3 = Share(dim, 3), Share(dim, 4), Halves(dim)
    tile = [pltpu.VMEM((WIDE, H), F32)]
    pair = [pltpu.VMEM((T, H), BF16)] * 4
    keep1, send1 = call(
        functools.partial(k_w1, dim, share1), [f32(*share1.shape)] * 2, pair + tile,
        active1, dv1, dg1, states1, dmixed1, us=5.0,
    )
    rfin1, (send1,) = tie(rfin1, [send1])
    gr1 = carried(rfin1)
    gr1, half1 = tie(gr1, half_sums(dim, keep1, send1))
    dproj1, dmid, dv0, dg0, dmixed0, ds0, rcf0, rfin0, sums1b, sums0a = k(
        k_c1,
        1,
        [(1, 0), (0, 2), (0, 3), (0, 1)],
        [big, big, big, big, big, big, ent, fins, vec, vec],
        halves(dim, 2) + [pltpu.VMEM((R, H), F32)],
        og, table1, table0, ds1, rcf1, gr1, states1, en1, drive1, xhat1, rstd1, dmixed1,
        xhat0, mixed0, v0, s0,
        us=11.0,
    )
    keep2, send2 = call(
        functools.partial(k_w2, dim, share2), [f32(*share2.shape)] * 2, pair + tile,
        active0, dv0, dg0, states0, dmixed0, xhat1, dproj1, table1, us=6.4,
    )
    rfin0, (send2, *sums1) = tie(rfin0, [send2, *plane_sums(dim, half1)])
    gr0 = carried(rfin0)
    upper1 = dp_sum(dim, sums1)
    gr0, (upper1, *half2) = tie(gr0, [upper1, *half_sums(dim, keep2, send2)])
    input_grad, keep3, send3 = k(
        functools.partial(k_c0, share3),
        0,
        [(0, 0)],
        [f32(R, dim.L, H)] + [f32(*share3.shape)] * 2,
        halves(dim, 2) + [pltpu.VMEM((R, H), F32)] + spare * 2 + [pltpu.VMEM((SMALL, H), F32)] + tile,
        table0, ds0, rcf0, gr0, states0, en0, drive0, xhat0, rstd0, dmixed0, dmid, sums1a, sums1b, sums0a,
        us=7.4,
    )
    sums2 = plane_sums(dim, half2)
    got3 = swap(send3, "seq", 1)
    half3 = [keep3[d] + got3[d] for d in range(D)]
    half3[0], sums2 = tie(half3[0], sums2)
    total3 = tree_sum([half3[0]] + [swap(half3[k], "dp", k) for k in range(1, D)])
    mine3 = tree_sum(chips_gather(dim, total3))
    other3 = swap(mine3, "seq", 1)
    upper = plane_gather(dim, jnp.concatenate([upper1, dp_sum(dim, sums2)], 0))
    kinds = [[(1, "gv"), (1, "gg"), (1, "out")], [(0, "gv"), (0, "gg"), (0, "out"), (1, "in")]]
    grads = unpack(dim, (share1, share2), kinds, share3, upper, mine3, other3)
    return (out.reshape(inputs.shape), input_grad.reshape(inputs.shape), *grads)


def solution(mesh):
    act, vec, mat = P("dp", "seq", None), P(None, "dp"), P(None, "dp", None)
    in_specs = (act, act, vec, vec, vec, vec, vec, mat, mat, vec, mat, vec)
    out_specs = (act, act, vec, vec, vec, vec, vec, mat, mat, vec, mat, vec)
    return jax.shard_map(body, mesh=mesh, in_specs=in_specs, out_specs=out_specs, check_vma=False)
```

```python
import functools
import math

import jax
import jax.numpy as jnp
from jax import lax
from jax.experimental import pallas as pl
from jax.experimental.pallas import tpu as pltpu
from jax.sharding import PartitionSpec as P

NORM_EPS = 1e-05
GROUPS = 8
WIDE = 256
SMALL = 8
TABLE = 16
F32 = jnp.float32
BF16 = jnp.bfloat16
GELU_C = math.sqrt(2.0 / math.pi)

GAIN, BIAS, SKIP, BIAS_V, BIAS_G, GAMMA, LAM, LAM1, LAM2, LAM4, LAM8, RATES = range(12)


CHUNKS = (((0, 0), (1, 0)), ((0, 1), (0, 2), (0, 3)), ((1, 1), (1, 2), (1, 3)))


class Dims:
    def __init__(self, inputs, in_map, dp, seq):
        self.B, self.Tb, self.H = inputs.shape
        self.layers, self.Hd = in_map.shape[:2]
        self.N = self.H // 2
        self.T = self.B * self.Tb
        self.R = self.B * GROUPS
        self.L = self.Tb // GROUPS
        self.D, self.S = dp, seq
        self.q = max(16, self.Hd // seq)
        self.used = self.Hd // self.q


def cmul(ar, ai, br, bi):
    return ar * br - ai * bi, ar * bi + ai * br


def split(x):
    hi = x.astype(BF16)
    return hi, (x - hi.astype(F32)).astype(BF16)


def dot3(ah, al, bh, bl, dims):
    def one(a, b):
        return lax.dot_general(a, b, (dims, ((), ())), preferred_element_type=F32)

    return one(ah, bh) + (one(ah, bl) + one(al, bh))


def product(ah, al, wh, wl, dst, transposed=False, add=False):
    for n in range(dst.shape[1] // WIDE):
        cols = slice(n * WIDE, (n + 1) * WIDE)
        if transposed:
            res = dot3(ah[...], al[...], wh[cols, :], wl[cols, :], ((1,), (1,)))
        else:
            res = dot3(ah[...], al[...], wh[:, cols], wl[:, cols], ((1,), (0,)))
        dst[:, cols] = dst[:, cols] + res if add else res


def each_step(dim, fn, unroll=2, reverse=False, init=0):
    def one(i, carry):
        j = dim.L - 1 - i if reverse else i
        rows = pl.ds(pl.multiple_of(j * dim.R, dim.R), dim.R)
        return fn(j, rows, carry)

    return lax.fori_loop(0, dim.L, one, init, unroll=unroll)


def each_span(dim, fn, init=0, steps=8):
    def one(i, carry):
        rows = pl.ds(pl.multiple_of(i * steps * dim.R, steps * dim.R), steps * dim.R)
        return fn([i * steps + u for u in range(steps)], rows, carry)

    return lax.fori_loop(0, dim.L // steps, one, init)


def fold(x):
    return jnp.sum(x.reshape(x.shape[0] // 8, 8, x.shape[1]), 0)


def row(table, index, n=1):
    return table[index : index + n, :]


def lam_of(dim, table, index, reverse):
    pair = table[index : index + 1, :]
    real, imag = pair[:, : dim.N], pair[:, dim.N :]
    return real, -imag if reverse else imag


def chunk_scan(dim, table, yr, yi, reverse):
    place = lax.broadcasted_iota(jnp.int32, yr.shape, 0)
    for dist, index in ((1, LAM1), (2, LAM2), (4, LAM4)):
        pr, pi = lam_of(dim, table, index, reverse)
        if reverse:
            shift, seen = GROUPS - dist, place < GROUPS - dist
        else:
            shift, seen = dist, place >= dist
        sr = jnp.where(seen, pltpu.roll(yr, shift, 0), 0.0)
        si = jnp.where(seen, pltpu.roll(yi, shift, 0), 0.0)
        mr, mi = cmul(pr, pi, sr, si)
        yr, yi = yr + mr, yi + mi
    return yr, yi


def local_finals(dim, table, drive_ref, cf_ref, f_ref, reverse):
    lr, li = lam_of(dim, table, LAM, reverse)
    lr = jnp.broadcast_to(lr, (dim.R, dim.N))
    li = jnp.broadcast_to(li, (dim.R, dim.N))

    def step(j, rows, carry):
        d = drive_ref[rows, :]
        mr, mi = cmul(lr, li, *carry)
        return mr + d[:, : dim.N], mi + d[:, dim.N :]

    zero = jnp.zeros((dim.R, dim.N), F32)
    fr, fi = each_step(dim, step, 4, reverse, (zero, zero))
    cf_ref[:, : dim.N] = fr
    cf_ref[:, dim.N :] = fi
    last = 0 if reverse else GROUPS - 1
    for b in range(dim.B):
        rows = slice(b * GROUPS, (b + 1) * GROUPS)
        yr, yi = chunk_scan(dim, table, fr[rows], fi[rows], reverse)
        f_ref[b : b + 1, : dim.N] = yr[last : last + 1]
        f_ref[b : b + 1, dim.N :] = yi[last : last + 1]


def entries_of(dim, table, cf_ref, g_ref, en_ref, reverse):
    me = lax.axis_index("seq")
    lr, li = lam_of(dim, table, LAM8, reverse)
    xr = jnp.zeros((dim.B, dim.N), F32)
    xi = xr
    order = reversed(range(dim.S)) if reverse else range(dim.S)
    for other in order:
        ahead = other > me if reverse else other < me
        g = g_ref[other]
        mr, mi = cmul(lr, li, xr, xi)
        xr = jnp.where(ahead, mr + g[:, : dim.N], xr)
        xi = jnp.where(ahead, mi + g[:, dim.N :], xi)
    for b in range(dim.B):
        rows = slice(b * GROUPS, (b + 1) * GROUPS)
        f = cf_ref[rows, :]
        place = lax.broadcasted_iota(jnp.int32, f.shape, 0)
        x = jnp.concatenate([xr[b : b + 1], xi[b : b + 1]], 1)
        if reverse:
            y = jnp.where(place == GROUPS - 1, x, pltpu.roll(f, GROUPS - 1, 0))
        else:
            y = jnp.where(place == 0, x, pltpu.roll(f, 1, 0))
        yr, yi = chunk_scan(dim, table, y[:, : dim.N], y[:, dim.N :], reverse)
        en_ref[rows, : dim.N] = yr
        en_ref[rows, dim.N :] = yi


def norm_step(dim, x, table):
    mean = jnp.mean(x, -1, keepdims=True)
    centred = x - mean
    var = jnp.mean(centred * centred, -1, keepdims=True)
    rstd = lax.rsqrt(var + NORM_EPS)
    xhat = centred * rstd
    return xhat, rstd, xhat * row(table, GAIN) + row(table, BIAS)


def front(dim, load_act, table, w_in, xhat, rstd, drive, cf, fin, ah, al, wh, wl):
    def norm(steps, rows, _):
        xh, rs, normed = norm_step(dim, load_act(steps, rows), table)
        xhat[rows, :] = xh
        rstd[rows, :] = jnp.broadcast_to(rs, (rs.shape[0], 128))
        ah[rows, :], al[rows, :] = split(normed)
        return 0

    each_span(dim, norm)
    w_in.fill(wh, wl)
    product(ah, al, wh, wl, drive)

    def scale(j, rows, _):
        drive[rows, :] = drive[rows, :] * row(table, GAMMA)
        return 0

    each_step(dim, scale, 4)
    local_finals(dim, table, drive, cf, fin, False)


def gelu_parts(m):
    inner = GELU_C * (m + 0.044715 * (m * m * m))
    th = jnp.tanh(inner)
    return th


def back(dim, table, drive, cf, g, xhat, w_out, w_gv, w_gg, en, states, mixed, active, v, s, ah, al, wh, wl):
    entries_of(dim, table, cf, g, en, False)
    lr, li = lam_of(dim, table, LAM, False)
    lr = jnp.broadcast_to(lr, (dim.R, dim.N))
    li = jnp.broadcast_to(li, (dim.R, dim.N))

    def scan(j, rows, carry):
        d = drive[rows, :]
        mr, mi = cmul(lr, li, *carry)
        both = jnp.concatenate([mr + d[:, : dim.N], mi + d[:, dim.N :]], 1)
        states[rows, :] = both
        ah[rows, :], al[rows, :] = split(both)
        return both[:, : dim.N], both[:, dim.N :]

    each_step(dim, scan, 4, False, (en[:, : dim.N], en[:, dim.N :]))
    w_out.fill(wh, wl)
    product(ah, al, wh, wl, mixed)

    def gelu(j, rows, _):
        normed = xhat[rows, :] * row(table, GAIN) + row(table, BIAS)
        m = mixed[rows, :] + row(table, SKIP) * normed
        mixed[rows, :] = m
        a = (0.5 * m) * (1.0 + gelu_parts(m))
        active[rows, :] = a
        ah[rows, :], al[rows, :] = split(a)
        return 0

    each_step(dim, gelu, 4)
    w_gv.fill(wh, wl)
    product(ah, al, wh, wl, v)
    w_gg.fill(wh, wl)
    product(ah, al, wh, wl, s)


def gate(dim, table, v, s, rows):
    vv = v[rows, :] + row(table, BIAS_V)
    ss = jax.nn.sigmoid(s[rows, :] + row(table, BIAS_G))
    v[rows, :] = vv
    s[rows, :] = ss
    return vv * ss


def top(dim, table, load_dact, v, s, mixed, xhat, w_gv, w_gg, w_out, dv, dg, dmixed, ds, rcf, rfin, sums, ah, al, bh, bl, wh, wl):
    def dgate(j, rows, carry):
        dact = load_dact(j, rows)
        ss, vv = s[rows, :], v[rows, :]
        a = dact * ss
        b = a * vv * (1.0 - ss)
        dv[rows, :] = a
        dg[rows, :] = b
        ah[rows, :], al[rows, :] = split(a)
        bh[rows, :], bl[rows, :] = split(b)
        return carry[0] + a, carry[1] + b

    zero = jnp.zeros((dim.R, dim.H), F32)
    sv, sg = each_step(dim, dgate, 2, False, (zero, zero))
    sums[BIAS_V : BIAS_V + 1, :] = jnp.sum(sv, 0, keepdims=True)
    sums[BIAS_G : BIAS_G + 1, :] = jnp.sum(sg, 0, keepdims=True)
    w_gv.fill(wh, wl)
    product(ah, al, wh, wl, dmixed, True)
    w_gg.fill(wh, wl)
    product(bh, bl, wh, wl, dmixed, True, True)

    def dgelu(j, rows, carry):
        m = mixed[rows, :]
        th = gelu_parts(m)
        slope = 0.5 * (1.0 + th) + (0.5 * m) * (1.0 - th * th) * (GELU_C * (1.0 + (3 * 0.044715) * (m * m)))
        d = dmixed[rows, :] * slope
        dmixed[rows, :] = d
        ah[rows, :], al[rows, :] = split(d)
        normed = xhat[rows, :] * row(table, GAIN) + row(table, BIAS)
        return carry + d * normed

    sums[SKIP : SKIP + 1, :] = jnp.sum(each_step(dim, dgelu, 2, False, zero), 0, keepdims=True)
    w_out.fill(wh, wl)
    product(ah, al, wh, wl, ds, True)
    local_finals(dim, table, ds, rcf, rfin, True)


def bottom(dim, table, ds, rcf, gr, states, en, drive, xhat, rstd, dmixed, w_in, load_dact, store, dproj, buf, adj_en, sums, ah, al, wh, wl):
    entries_of(dim, table, rcf, gr, adj_en, True)
    lr, li = lam_of(dim, table, LAM, True)
    lr = jnp.broadcast_to(lr, (dim.R, dim.N))
    li = jnp.broadcast_to(li, (dim.R, dim.N))
    zero = jnp.zeros((dim.R, dim.N), F32)

    def scan(j, rows, carry):
        ar, ai, dr, di, dgam = carry
        d = ds[rows, :]
        mr, mi = cmul(lr, li, ar, ai)
        ar, ai = mr + d[:, : dim.N], mi + d[:, dim.N :]
        earlier = pl.ds(pl.multiple_of(jnp.maximum(j - 1, 0) * dim.R, dim.R), dim.R)
        before = jnp.where(j == 0, en[...], states[earlier, :])
        br, bi = before[:, : dim.N], before[:, dim.N :]
        dr = dr + (ar * br + ai * bi)
        di = di + (ai * br - ar * bi)
        u = drive[rows, :]
        dgam = dgam + (ar * u[:, : dim.N] + ai * u[:, dim.N :])
        dp = jnp.concatenate([ar, ai], 1) * row(table, GAMMA)
        dproj[rows, :] = dp
        ah[rows, :], al[rows, :] = split(dp)
        return ar, ai, dr, di, dgam

    start = (adj_en[:, : dim.N], adj_en[:, dim.N :], zero, zero, zero)
    _, _, dr, di, dgam = each_step(dim, scan, 2, True, start)
    dr, di, dgam = (jnp.sum(x, 0, keepdims=True) for x in (dr, di, dgam))
    fr, fi = lam_of(dim, table, LAM, False)
    rates = row(table, RATES)
    rate, angle = rates[:, : dim.N], rates[:, dim.N :]
    sums[5:6, : dim.N] = -rate * (dr * fr + di * fi)
    sums[5:6, dim.N :] = angle * (di * fr - dr * fi)
    sums[6:7, : dim.N] = dgam
    sums[6:7, dim.N :] = jnp.zeros_like(dgam)
    sums[7:8, :] = jnp.zeros((1, dim.H), F32)

    w_in.fill(wh, wl)
    product(ah, al, wh, wl, buf, True)
    wide = jnp.zeros((8, dim.H), F32)

    def dnorm(steps, rows, carry):
        dn = buf[rows, :] + dmixed[rows, :] * row(table, SKIP)
        xh = xhat[rows, :]
        dx = dn * row(table, GAIN)
        m1 = jnp.mean(dx, -1, keepdims=True)
        m2 = jnp.mean(dx * xh, -1, keepdims=True)
        store(steps, rows, load_dact(steps, rows) + rstd[rows, 0:1] * (dx - m1 - xh * m2))
        return carry[0] + fold(dn * xh), carry[1] + fold(dn)

    sgain, sbias = each_span(dim, dnorm, (wide, wide))
    sums[GAIN : GAIN + 1, :] = jnp.sum(sgain, 0, keepdims=True)
    sums[BIAS : BIAS + 1, :] = jnp.sum(sbias, 0, keepdims=True)


def split_rows(dim, load, xh, xl):
    def one(j, rows, _):
        xh[rows, :], xl[rows, :] = split(load(rows))
        return 0

    each_step(dim, one, 4)


class Share:
    def __init__(self, dim, nm):
        self.dim, self.nm = dim, nm
        self.q = -(-nm * dim.Hd // (8 * dim.S)) * 8
        self.step = math.gcd(self.q, dim.Hd)
        self.shape = (dim.S // 2, dim.D, self.q, dim.H)

    def place(self, m, d, r, me, my):
        p = m * self.dim.Hd + r
        s = p // self.q
        return s & 1, ((s ^ me) >> 1, d ^ my), p % self.q


class Halves:
    def __init__(self, dim):
        self.dim = dim
        self.q = dim.Hd // 2
        self.step = math.gcd(self.q, WIDE)
        self.shape = (dim.D, self.q + SMALL, dim.H)

    def place(self, m, d, r, me, my):
        return r // self.q, (d ^ my,), r % self.q


def weight_grad(dim, share, m, ah, al, bh, bl, tile, keep, send):
    me = lax.axis_index("seq")
    my = lax.axis_index("dp")
    for h0 in range(0, dim.H, WIDE):
        tile[...] = dot3(ah[:, h0 : h0 + WIDE], al[:, h0 : h0 + WIDE], bh[...], bl[...], ((0,), (0,)))

        def put(mine):
            for r0 in range(0, WIDE, share.step):
                h = h0 + r0
                odd, index, off = share.place(m, h // dim.Hd, h % dim.Hd, me, my)
                dst = keep if odd == mine else send
                dst[(*index, slice(off, off + share.step), slice(None))] = tile[r0 : r0 + share.step, :]

        for mine in range(2):
            pl.when(me & 1 == mine)(functools.partial(put, mine))


class Kept:
    def __init__(self, value):
        self.value = value
        self.shape = value.shape


def call(fn, outs, scratch, *args, us=1.0, anywhere=0):
    spaces = [pltpu.HBM] * anywhere + [pltpu.VMEM] * (len(args) - anywhere)

    def placed(x, space):
        if isinstance(x, Kept):
            return pltpu.with_memory_space_constraint(x.value, pltpu.VMEM)
        return pltpu.with_memory_space_constraint(x, pltpu.HBM) if space is pltpu.HBM else x

    values = [placed(x, space) for x, space in zip(args, spaces)]
    room = 10 << 20
    for x in scratch:
        if len(x.shape) > 1:
            room += math.prod(x.shape) * (2 if x.dtype == BF16 else 4)
    results = pl.pallas_call(
        fn,
        out_shape=outs,
        in_specs=[pl.BlockSpec(memory_space=space) for space in spaces],
        out_specs=[pl.BlockSpec(memory_space=pltpu.VMEM)] * len(outs),
        scratch_shapes=scratch,
        compiler_params=pltpu.CompilerParams(vmem_limit_bytes=max(20 << 20, room)),
        cost_estimate=pl.CostEstimate(flops=1, bytes_accessed=int(us * 3.6e6), transcendentals=0),
    )(*values)
    return [x if isinstance(o, jax.ShapeDtypeStruct) else Kept(x) for x, o in zip(results, outs)]


def f32(*shape):
    return jax.ShapeDtypeStruct(shape, F32)


def halves(dim, n):
    return [pltpu.VMEM((dim.T, dim.H), BF16)] * (2 * n) + [pltpu.VMEM((dim.H, dim.H), BF16)] * 2


def prep_kernel(dim, small, table):
    s = small[...]
    nu, theta, gam = s[5:6, : dim.N], s[5:6, dim.N :], s[6:7, : dim.N]
    rate, angle = jnp.exp(nu), jnp.exp(theta)
    mod = jnp.exp(-rate)
    re, im = mod * jnp.cos(angle), mod * jnp.sin(angle)
    gamma = jnp.exp(gam)

    def put(index, a, b):
        table[index : index + 1, : dim.N] = a
        table[index : index + 1, dim.N :] = b

    table[...] = jnp.zeros((TABLE, dim.H), F32)
    table[:5, :] = s[:5]
    put(GAMMA, gamma, gamma)
    put(LAM, re, im)
    put(RATES, rate, angle)
    power = 1
    while power < dim.L:
        re, im = cmul(re, im, re, im)
        power *= 2
    for index in (LAM1, LAM2, LAM4, LAM8):
        put(index, re, im)
        re, im = cmul(re, im, re, im)


def shard_of(sources, name, rows, H):
    layer, m = name
    return sources[(0, 1, 2, 2)[m]].at[layer, rows, pl.ds(H if m == 3 else 0, H)]


def pack_kernel(dim, in_map, out_map, glu, gain, bias, skip, nu, theta, gamma, glu_bias, *refs):
    outs, held, sem = refs[:2], refs[2:-1], refs[-1]
    vectors = (gain, bias, skip, nu, theta, gamma, glu_bias)
    me, my = lax.axis_index("seq"), lax.axis_index("dp")
    start = pl.multiple_of(jnp.minimum(me, dim.used - 1) * dim.q, 16)
    moves = []
    for src, dst in zip(vectors, held):
        moves.append(pltpu.make_async_copy(src, dst, sem.at[len(moves)]))
    gain, bias, skip, nu, theta, gamma, glu_bias = held
    for out, chunk in zip(outs, (CHUNKS[0], CHUNKS[1] + CHUNKS[2])):
        head = out.shape[0] - len(chunk) * dim.q
        for i, name in enumerate(chunk):
            src = shard_of((in_map, out_map, glu), name, pl.ds(start, dim.q), dim.H)
            dst = out.at[head + i * dim.q : head + (i + 1) * dim.q, :]
            moves.append(pltpu.make_async_copy(src, dst, sem.at[len(moves)]))
    for move in moves:
        move.start()
    for move in moves[: len(held)]:
        move.wait()

    def spread(ref, layer, width):
        vec = ref[layer : layer + 1, :]
        full = jnp.concatenate([vec] * (width // vec.shape[1]), 1)
        lane = lax.broadcasted_iota(jnp.int32, full.shape, 1)
        return jnp.where(lane // vec.shape[1] == my, full, 0.0)

    for layer in range(dim.layers):
        both = spread(glu_bias, layer, 2 * dim.H)
        rows = [spread(ref, layer, dim.H) for ref in (gain, bias, skip)] + [both[:, : dim.H], both[:, dim.H :]]
        rows.append(jnp.concatenate([spread(nu, layer, dim.N), spread(theta, layer, dim.N)], 1))
        rows.append(jnp.concatenate([spread(gamma, layer, dim.N), jnp.zeros((1, dim.N), F32)], 1))
        for i, value in enumerate(rows):
            outs[layer][i : i + 1, :] = value
        outs[layer][7:8, :] = jnp.zeros((1, dim.H), F32)
    for move in moves[len(held) :]:
        move.wait()


class Weight:
    def __init__(self, dim, name, place, sources, own, buf, sem):
        self.dim, self.name, self.place = dim, name, place
        self.sources, self.own, self.buf, self.sem = sources, own, buf, sem
        self.here = False

    def moves(self):
        shard = shard_of(self.sources, self.name, slice(None), self.dim.H)
        yield pltpu.make_async_copy(shard, self.own, self.sem.at[self.dim.S])
        for k, piece in enumerate(self.sources[3:]):
            yield pltpu.make_async_copy(piece.at[self.place], self.buf.at[k], self.sem.at[k])

    def start(self):
        for move in self.moves():
            move.start()

    def fill(self, wh, wl):
        dim, q = self.dim, self.dim.q
        if not self.here:
            for move in self.moves():
                move.wait()
        self.here = True
        me, my = lax.axis_index("seq"), lax.axis_index("dp")

        def put(start, n, value):
            rows = pl.ds(pl.multiple_of(start, 16), n)
            wh[rows, :], wl[rows, :] = split(value)

        def mine(i, _):
            put(my * dim.Hd + i * 32, 32, self.own[pl.ds(pl.multiple_of(i * 32, 32), 32), :])
            return 0

        lax.fori_loop(0, dim.Hd // 32, mine, 0)

        def one(k, _):
            s = k ^ me

            def block():
                for kz in range(1, dim.D):
                    put((kz ^ my) * dim.Hd + s * q, q, self.buf[k, kz - 1])

            if dim.used < dim.S:
                pl.when(s < dim.used)(block)
            else:
                block()
            return 0

        lax.fori_loop(0, dim.S, one, 0)


def weights_in(dim, chunks, names, fn):
    first = 3 + len(chunks) * dim.S

    def kernel(*refs):
        spare = refs[len(refs) - 3 * len(names) :]
        weights = []
        for i, name in enumerate(names):
            (n,) = [n for n, c in enumerate(chunks) if name in CHUNKS[c]]
            sources = refs[:3] + refs[3 + n * dim.S : 3 + (n + 1) * dim.S]
            place = CHUNKS[chunks[n]].index(name)
            weights.append(Weight(dim, name, place, sources, *spare[3 * i : 3 * i + 3]))
        for w in weights:
            w.start()
        fn(dim, weights, *refs[first : len(refs) - 3 * len(names)])

    scratch = [
        pltpu.VMEM((dim.Hd, dim.H), F32),
        pltpu.VMEM((dim.S, dim.D - 1, dim.q, dim.H), F32),
        pltpu.SemaphoreType.DMA((dim.S + 1,)),
    ] * len(names)
    return kernel, first, scratch


def strided(dim, ref):
    def load(steps, rows):
        if isinstance(steps, list):
            return jnp.concatenate([ref[:, j, :] for j in steps], 0)
        return ref[:, steps, :]

    return load


def plain(ref):
    return lambda j, rows: ref[rows, :]


def k_a0(dim, weights, x, table, xhat, rstd, drive, cf, fin, ah, al, wh, wl):
    front(dim, strided(dim, x), table, weights[0], xhat, rstd, drive, cf, fin, ah, al, wh, wl)


def k_b0(dim, weights, x, t, t1, drive, cf, g, xhat,
         en, states, mixed, active, v, s, act1, xhat1, rstd1, drive1, cf1, fin1, ah, al, wh, wl):
    w_out, w_gv, w_gg, w_in1 = weights
    back(dim, t, drive, cf, g, xhat, w_out, w_gv, w_gg, en, states, mixed, active, v, s, ah, al, wh, wl)
    load = strided(dim, x)

    def residual(steps, rows):
        act = load(steps, rows) + gate(dim, t, v, s, rows)
        act1[rows, :] = act
        return act

    front(dim, residual, t1, w_in1, xhat1, rstd1, drive1, cf1, fin1, ah, al, wh, wl)


def k_b1(dim, weights, act1, out_grad, t, drive, cf, g, xhat,
         out, en, states, active, dv, dg, dmixed, ds, rcf, rfin, sums, ah, al, bh, bl, wh, wl, mixed, v, s):
    w_out, w_gv, w_gg = weights
    back(dim, t, drive, cf, g, xhat, w_out, w_gv, w_gg, en, states, mixed, active, v, s, ah, al, wh, wl)

    def residual(j, rows, _):
        out[:, j, :] = act1[rows, :] + gate(dim, t, v, s, rows)
        return 0

    each_step(dim, residual, 2)
    sums[...] = jnp.zeros((SMALL, dim.H), F32)
    top(dim, t, strided(dim, out_grad), v, s, mixed, xhat, w_gv, w_gg, w_out, dv, dg, dmixed, ds, rcf, rfin, sums,
        ah, al, bh, bl, wh, wl)


def k_w1(dim, share, active, dv, dg, states, dmixed, keep, send, ah, al, bh, bl, tile):
    split_rows(dim, lambda rows: active[rows, :], ah, al)
    for m, ref in ((0, dv), (1, dg)):
        split_rows(dim, lambda rows: ref[rows, :], bh, bl)
        weight_grad(dim, share, m, ah, al, bh, bl, tile, keep, send)
    split_rows(dim, lambda rows: states[rows, :], ah, al)
    split_rows(dim, lambda rows: dmixed[rows, :], bh, bl)
    weight_grad(dim, share, 2, ah, al, bh, bl, tile, keep, send)


def k_c1(dim, weights, out_grad, t, t0, ds, rcf, gr, states, en, drive, xhat, rstd, dmixed,
         xhat0, mixed0, v0, s0,
         dproj, dmid, dv0, dg0, dmixed0, ds0, rcf0, rfin0, sums1, sums0, ah, al, bh, bl, wh, wl, adj_en):
    w_in, w_gv, w_gg, w_out = weights

    def store(j, rows, value):
        dmid[rows, :] = value

    bottom(dim, t, ds, rcf, gr, states, en, drive, xhat, rstd, dmixed, w_in, strided(dim, out_grad), store,
           dproj, ds0, adj_en, sums1, ah, al, wh, wl)
    sums0[...] = jnp.zeros((SMALL, dim.H), F32)
    top(dim, t0, plain(dmid), v0, s0, mixed0, xhat0, w_gv, w_gg, w_out, dv0, dg0, dmixed0, ds0, rcf0, rfin0,
        sums0, ah, al, bh, bl, wh, wl)


def k_w2(dim, share, active, dv, dg, states, dmixed, xhat1, dproj1, t, keep, send, ah, al, bh, bl, tile):
    k_w1(dim, share, active, dv, dg, states, dmixed, keep, send, ah, al, bh, bl, tile)
    split_rows(dim, lambda rows: xhat1[rows, :] * row(t, GAIN) + row(t, BIAS), ah, al)
    split_rows(dim, lambda rows: dproj1[rows, :], bh, bl)
    weight_grad(dim, share, 3, ah, al, bh, bl, tile, keep, send)


def k_c0(share, dim, weights, t, ds, rcf, gr, states, en, drive, xhat, rstd, dmixed, dmid, sums1a, sums1b, sums0a,
         input_grad, keep, send, ah, al, bh, bl, wh, wl, adj_en, dproj, buf, sums0, tile):
    def store(steps, rows, value):
        for u, j in enumerate(steps):
            input_grad[:, j, :] = value[u * dim.R : (u + 1) * dim.R, :]

    bottom(dim, t, ds, rcf, gr, states, en, drive, xhat, rstd, dmixed, weights[0], plain(dmid), store, dproj, buf, adj_en,
           sums0, ah, al, wh, wl)
    split_rows(dim, lambda rows: xhat[rows, :] * row(t, GAIN) + row(t, BIAS), bh, bl)
    weight_grad(dim, share, 0, bh, bl, ah, al, tile, keep, send)
    place = lax.broadcasted_iota(jnp.int32, (SMALL, dim.H), 0)
    upper = (place >= SKIP) & (place <= BIAS_G)
    tile[0:SMALL, :] = jnp.where(upper, sums0a[...], sums0[...])
    tile[SMALL : 2 * SMALL, :] = jnp.where(upper, sums1a[...], sums1b[...])
    me = lax.axis_index("seq")

    def put(mine):
        for layer in range(dim.layers):
            dst = keep if layer == mine else send
            for d in range(dim.D):
                dst[d, share.q :, :] = tile[layer * SMALL : (layer + 1) * SMALL, :]

    for mine in range(2):
        pl.when(me & 1 == mine)(functools.partial(put, mine))


def tie(x, others):
    x, *others = lax.optimization_barrier((x, *others))
    return x, others


def swap(x, axis, mask):
    count = lax.axis_size(axis)
    return lax.ppermute(x, axis, [(i, i ^ mask) for i in range(count)])


def chips_gather(dim, x):
    return [x] + [swap(x, "seq", k) for k in range(2, dim.S, 2)]


def cores_gather(pieces):
    return [p for x in pieces for p in (x, swap(x, "seq", 1))]


def plane_gather(dim, x):
    return cores_gather(chips_gather(dim, x))


def tree_sum(parts):
    while len(parts) > 1:
        parts = [a + b for a, b in zip(parts[::2], parts[1::2])]
    return parts[0]


def half_sums(dim, keep, send):
    got = swap(send, "seq", 1)
    return [keep[k] + got[k] for k in range(dim.S // 2)]


def plane_sums(dim, half):
    others = [swap(half[k], "seq", 2 * k) for k in range(1, dim.S // 2)]
    return [sum((o[k] for o in others), half[0][k]) for k in range(dim.D)]


def dp_sum(dim, parts):
    return sum((swap(parts[k], "dp", k) for k in range(1, dim.D)), parts[0])


def unpack_kernel(dim, shares, kinds, last, *refs):
    pieces, (mine, other), outs = refs[: dim.S], refs[dim.S : dim.S + 2], refs[dim.S + 2 :]
    g_gain, g_bias, g_nu, g_theta, g_gamma, g_in, g_out, g_skip, g_glu, g_glu_bias = outs
    me, my = lax.axis_index("seq"), lax.axis_index("dp")

    def place(layer, kind, rows, value):
        if kind == "in":
            g_in[layer, rows, :] = value
        elif kind == "out":
            g_out[layer, rows, :] = value
        elif kind == "gv":
            g_glu[layer, rows, 0 : dim.H] = value
        else:
            g_glu[layer, rows, dim.H : 2 * dim.H] = value

    def put(k, s):
        base = 0
        for share, names in zip(shares, kinds):
            for off in range(0, share.q, share.step):
                p = s * share.q + off
                if p // dim.Hd < share.nm:
                    layer, kind = names[p // dim.Hd]
                    r = p % dim.Hd
                    place(layer, kind, slice(r, r + share.step), pieces[k][base + off : base + off + share.step, :])
            base += share.q

    def vectors(d):
        def own(layer, index, lo, width, out, at=0):
            src = (mine, other)

            def copy(ref):
                start = lo + d * width
                out[layer : layer + 1, :] = ref[last.q + index : last.q + index + 1, start : start + width]

            pl.when(me & 1 == layer)(functools.partial(copy, src[0]))
            pl.when(me & 1 != layer)(functools.partial(copy, src[1]))

        for layer in range(dim.layers):
            for index, out in ((GAIN, g_gain), (BIAS, g_bias), (SKIP, g_skip)):
                own(layer, index, 0, dim.Hd, out)
            n = dim.N // dim.D
            own(layer, 5, 0, n, g_nu)
            own(layer, 5, dim.N, n, g_theta)
            own(layer, 6, 0, n, g_gamma)
            width = 2 * dim.H // dim.D
            index = BIAS_V if d * width < dim.H else BIAS_G
            own(layer, index, 0 if index == BIAS_V else -dim.H, width, g_glu_bias)

    for who in range(dim.S):

        def all_of(who=who):
            for k in range(dim.S):
                put(k, k ^ who)
            half = who & 1
            for ref, part in ((mine, half), (other, 1 - half)):
                place(0, "in", slice(part * last.q, (part + 1) * last.q), ref[: last.q, :])

        pl.when(me == who)(all_of)
    for d in range(dim.D):
        pl.when(my == d)(functools.partial(vectors, d))


def unpack(dim, shares, kinds, last, pieces, mine, other):
    n, l = dim.N // dim.D, dim.layers
    vec, small = f32(l, dim.Hd), f32(l, n)
    mat, wide = f32(l, dim.Hd, dim.H), f32(l, dim.Hd, 2 * dim.H)
    outs = [vec, vec, small, small, small, mat, mat, vec, wide, f32(l, 2 * dim.H // dim.D)]
    return call(functools.partial(unpack_kernel, dim, shares, kinds, last), outs, [], *pieces, mine, other)


def body(inputs, out_grad, ln_gain, ln_bias, nu_log, theta_log, gamma_log, in_map, out_map, skip_gain, glu_weight, glu_bias):
    dim = Dims(inputs, in_map, lax.axis_size("dp"), lax.axis_size("seq"))
    T, H, N, R, B, D, S = dim.T, dim.H, dim.N, dim.R, dim.B, dim.D, dim.S
    me, my = lax.axis_index("seq"), lax.axis_index("dp")
    x = inputs.reshape(R, dim.L, H)
    og = out_grad.reshape(R, dim.L, H)

    heads = [SMALL, SMALL]
    sends = [CHUNKS[0], CHUNKS[1] + CHUNKS[2]]
    vectors = (ln_gain, ln_bias, skip_gain, nu_log, theta_log, gamma_log, glu_bias)
    messages = call(
        functools.partial(pack_kernel, dim),
        [f32(head + len(chunk) * dim.q, H) for head, chunk in zip(heads, sends)],
        [pltpu.VMEM(v.shape, F32) for v in vectors] + [pltpu.SemaphoreType.DMA((len(vectors) + sum(map(len, CHUNKS)),))],
        in_map, out_map, glu_weight, *vectors,
        anywhere=3 + len(vectors),
    )
    def stacked(others, head):
        return jnp.stack([other[head:].reshape(-1, dim.q, H) for other in others], 1)

    def along_dp(mine):
        return [swap(mine, "dp", k) for k in range(1, D)]

    def table_of(mine, others, head=SMALL):
        total = mine[:head]
        for other in others:
            total = total + other[:head]
        return call(functools.partial(prep_kernel, dim), [f32(TABLE, H)], [], total)[0]

    mine0, mine1 = messages
    others0 = along_dp(mine0)
    table0 = table_of(mine0, others0)
    mine1, others0 = tie(mine1, others0)
    others1 = along_dp(mine1)
    table1 = table_of(mine1, others1)
    chips0 = chips_gather(dim, stacked(others0, SMALL))
    cut = SMALL + len(CHUNKS[1]) * dim.q
    joined1, chips0 = tie(stacked([o[:cut] for o in others1], SMALL), chips0)
    joined2 = stacked(others1, cut)
    pieces0 = cores_gather(chips0)
    chips1 = chips_gather(dim, joined1)
    pieces = [pieces0, cores_gather(chips1), None]

    big, ent, fins = pltpu.VMEM((T, H), F32), pltpu.VMEM((R, H), F32), f32(B, H)
    stat = pltpu.VMEM((T, 128), F32)
    vec = pltpu.VMEM((SMALL, H), F32)

    def k(fn, names, outs, scratch, *args, us):
        chunks = [c for c, chunk in enumerate(CHUNKS) if set(chunk) & set(names)]
        kernel, count, own = weights_in(dim, chunks, names, fn)
        sources = [in_map, out_map, glu_weight] + [p for c in chunks for p in pieces[c]]
        return call(kernel, outs, scratch + own, *sources, *args, us=us, anywhere=count)

    def carried(fin):
        return lax.all_gather(fin, "seq")

    xhat0, rstd0, drive0, cf0, fin0 = k(
        k_a0, [(0, 0)], [big, stat, big, ent, fins], halves(dim, 1), x, table0, us=3.4
    )
    g0 = carried(fin0)
    joined2, (g0,) = tie(joined2, [g0])
    chips2 = chips_gather(dim, joined2)
    en0, states0, mixed0, active0, v0, s0, act1, xhat1, rstd1, drive1, cf1, fin1 = k(
        k_b0,
        [(0, 1), (0, 2), (0, 3), (1, 0)],
        [ent, big, big, big, big, big, big, big, stat, big, ent, fins],
        halves(dim, 1),
        x, table0, table1, drive0, cf0, g0, xhat0,
        us=10.0,
    )
    fin1, chips2 = tie(fin1, chips2)
    g1 = carried(fin1)
    pieces[2] = cores_gather(chips2)
    spare = [pltpu.VMEM((T, H), F32)]
    out, en1, states1, active1, dv1, dg1, dmixed1, ds1, rcf1, rfin1, sums1a = k(
        k_b1,
        [(1, 1), (1, 2), (1, 3)],
        [f32(R, dim.L, H), ent, big, big, big, big, big, big, ent, fins, vec],
        halves(dim, 2) + spare * 3,
        act1, og, table1, drive1, cf1, g1, xhat1,
        us=13.0,
    )
    share1, share2, share3 = Share(dim, 3), Share(dim, 4), Halves(dim)
    tile = [pltpu.VMEM((WIDE, H), F32)]
    pair = [pltpu.VMEM((T, H), BF16)] * 4
    keep1, send1 = call(
        functools.partial(k_w1, dim, share1), [f32(*share1.shape)] * 2, pair + tile,
        active1, dv1, dg1, states1, dmixed1, us=5.0,
    )
    rfin1, (send1,) = tie(rfin1, [send1])
    gr1 = carried(rfin1)
    gr1, half1 = tie(gr1, half_sums(dim, keep1, send1))
    dproj1, dmid, dv0, dg0, dmixed0, ds0, rcf0, rfin0, sums1b, sums0a = k(
        k_c1,
        [(1, 0), (0, 2), (0, 3), (0, 1)],
        [big, big, big, big, big, big, ent, fins, vec, vec],
        halves(dim, 2) + [pltpu.VMEM((R, H), F32)],
        og, table1, table0, ds1, rcf1, gr1, states1, en1, drive1, xhat1, rstd1, dmixed1,
        xhat0, mixed0, v0, s0,
        us=11.0,
    )
    keep2, send2 = call(
        functools.partial(k_w2, dim, share2), [f32(*share2.shape)] * 2, pair + tile,
        active0, dv0, dg0, states0, dmixed0, xhat1, dproj1, table1, us=6.4,
    )
    rfin0, (send2, *sums1) = tie(rfin0, [send2, *plane_sums(dim, half1)])
    gr0 = carried(rfin0)
    upper1 = dp_sum(dim, sums1)
    gr0, (upper1, *half2) = tie(gr0, [upper1, *half_sums(dim, keep2, send2)])
    input_grad, keep3, send3 = k(
        functools.partial(k_c0, share3),
        [(0, 0)],
        [f32(R, dim.L, H)] + [f32(*share3.shape)] * 2,
        halves(dim, 2) + [pltpu.VMEM((R, H), F32)] + spare * 2 + [pltpu.VMEM((SMALL, H), F32)] + tile,
        table0, ds0, rcf0, gr0, states0, en0, drive0, xhat0, rstd0, dmixed0, dmid, sums1a, sums1b, sums0a,
        us=7.4,
    )
    sums2 = plane_sums(dim, half2)
    got3 = swap(send3, "seq", 1)
    half3 = [keep3[d] + got3[d] for d in range(D)]
    total3 = tree_sum([half3[0]] + [swap(half3[k], "dp", k) for k in range(1, D)])
    mine3 = tree_sum(chips_gather(dim, total3))
    joint, (mine3,) = tie(jnp.concatenate([upper1, dp_sum(dim, sums2)], 0), [mine3])
    upper = plane_gather(dim, joint)
    other3 = swap(mine3, "seq", 1)
    kinds = [[(1, "gv"), (1, "gg"), (1, "out")], [(0, "gv"), (0, "gg"), (0, "out"), (1, "in")]]
    grads = unpack(dim, (share1, share2), kinds, share3, upper, mine3, other3)
    return (out.reshape(inputs.shape), input_grad.reshape(inputs.shape), *grads)


def solution(mesh):
    act, vec, mat = P("dp", "seq", None), P(None, "dp"), P(None, "dp", None)
    in_specs = (act, act, vec, vec, vec, vec, vec, mat, mat, vec, mat, vec)
    out_specs = (act, act, vec, vec, vec, vec, vec, mat, mat, vec, mat, vec)
    return jax.shard_map(body, mesh=mesh, in_specs=in_specs, out_specs=out_specs, check_vma=False)
```

```python
import functools
import math

import jax
import jax.numpy as jnp
from jax import lax
from jax.experimental import pallas as pl
from jax.experimental.pallas import tpu as pltpu
from jax.sharding import PartitionSpec as P

NORM_EPS = 1e-05
GROUPS = 8
WIDE = 256
SMALL = 8
TABLE = 16
F32 = jnp.float32
BF16 = jnp.bfloat16
GELU_C = math.sqrt(2.0 / math.pi)

GAIN, BIAS, SKIP, BIAS_V, BIAS_G, GAMMA, LAM, LAM1, LAM2, LAM4, LAM8, RATES = range(12)


CHUNKS = (((0, 0), (1, 0)), ((0, 1), (0, 2), (0, 3)), ((1, 1), (1, 2), (1, 3)))


class Dims:
    def __init__(self, inputs, in_map, dp, seq):
        self.B, self.Tb, self.H = inputs.shape
        self.layers, self.Hd = in_map.shape[:2]
        self.N = self.H // 2
        self.T = self.B * self.Tb
        self.R = self.B * GROUPS
        self.L = self.Tb // GROUPS
        self.D, self.S = dp, seq
        self.q = max(16, self.Hd // seq)
        self.used = self.Hd // self.q


def cmul(ar, ai, br, bi):
    return ar * br - ai * bi, ar * bi + ai * br


def split(x):
    hi = x.astype(BF16)
    return hi, (x - hi.astype(F32)).astype(BF16)


def dot3(ah, al, bh, bl, dims):
    def one(a, b):
        return lax.dot_general(a, b, (dims, ((), ())), preferred_element_type=F32)

    return one(ah, bh) + (one(ah, bl) + one(al, bh))


def product(ah, al, wh, wl, dst, transposed=False, add=False):
    for n in range(dst.shape[1] // WIDE):
        cols = slice(n * WIDE, (n + 1) * WIDE)
        if transposed:
            res = dot3(ah[...], al[...], wh[cols, :], wl[cols, :], ((1,), (1,)))
        else:
            res = dot3(ah[...], al[...], wh[:, cols], wl[:, cols], ((1,), (0,)))
        dst[:, cols] = dst[:, cols] + res if add else res


def each_step(dim, fn, unroll=2, reverse=False, init=0):
    def one(i, carry):
        j = dim.L - 1 - i if reverse else i
        rows = pl.ds(pl.multiple_of(j * dim.R, dim.R), dim.R)
        return fn(j, rows, carry)

    return lax.fori_loop(0, dim.L, one, init, unroll=unroll)


def each_span(dim, fn, init=0, steps=8):
    def one(i, carry):
        rows = pl.ds(pl.multiple_of(i * steps * dim.R, steps * dim.R), steps * dim.R)
        return fn([i * steps + u for u in range(steps)], rows, carry)

    return lax.fori_loop(0, dim.L // steps, one, init)


def fold(x):
    return jnp.sum(x.reshape(x.shape[0] // 8, 8, x.shape[1]), 0)


def row(table, index, n=1):
    return table[index : index + n, :]


def lam_of(dim, table, index, reverse):
    pair = table[index : index + 1, :]
    real, imag = pair[:, : dim.N], pair[:, dim.N :]
    return real, -imag if reverse else imag


def chunk_scan(dim, table, yr, yi, reverse):
    place = lax.broadcasted_iota(jnp.int32, yr.shape, 0)
    for dist, index in ((1, LAM1), (2, LAM2), (4, LAM4)):
        pr, pi = lam_of(dim, table, index, reverse)
        if reverse:
            shift, seen = GROUPS - dist, place < GROUPS - dist
        else:
            shift, seen = dist, place >= dist
        sr = jnp.where(seen, pltpu.roll(yr, shift, 0), 0.0)
        si = jnp.where(seen, pltpu.roll(yi, shift, 0), 0.0)
        mr, mi = cmul(pr, pi, sr, si)
        yr, yi = yr + mr, yi + mi
    return yr, yi


def local_finals(dim, table, drive_ref, cf_ref, f_ref, reverse):
    lr, li = lam_of(dim, table, LAM, reverse)
    lr = jnp.broadcast_to(lr, (dim.R, dim.N))
    li = jnp.broadcast_to(li, (dim.R, dim.N))

    def step(j, rows, carry):
        d = drive_ref[rows, :]
        mr, mi = cmul(lr, li, *carry)
        return mr + d[:, : dim.N], mi + d[:, dim.N :]

    zero = jnp.zeros((dim.R, dim.N), F32)
    fr, fi = each_step(dim, step, 4, reverse, (zero, zero))
    cf_ref[:, : dim.N] = fr
    cf_ref[:, dim.N :] = fi
    last = 0 if reverse else GROUPS - 1
    for b in range(dim.B):
        rows = slice(b * GROUPS, (b + 1) * GROUPS)
        yr, yi = chunk_scan(dim, table, fr[rows], fi[rows], reverse)
        f_ref[b : b + 1, : dim.N] = yr[last : last + 1]
        f_ref[b : b + 1, dim.N :] = yi[last : last + 1]


def entries_of(dim, table, cf_ref, g_ref, en_ref, reverse):
    me = lax.axis_index("seq")
    lr, li = lam_of(dim, table, LAM8, reverse)
    xr = jnp.zeros((dim.B, dim.N), F32)
    xi = xr
    order = reversed(range(dim.S)) if reverse else range(dim.S)
    for other in order:
        ahead = other > me if reverse else other < me
        g = g_ref[other]
        mr, mi = cmul(lr, li, xr, xi)
        xr = jnp.where(ahead, mr + g[:, : dim.N], xr)
        xi = jnp.where(ahead, mi + g[:, dim.N :], xi)
    for b in range(dim.B):
        rows = slice(b * GROUPS, (b + 1) * GROUPS)
        f = cf_ref[rows, :]
        place = lax.broadcasted_iota(jnp.int32, f.shape, 0)
        x = jnp.concatenate([xr[b : b + 1], xi[b : b + 1]], 1)
        if reverse:
            y = jnp.where(place == GROUPS - 1, x, pltpu.roll(f, GROUPS - 1, 0))
        else:
            y = jnp.where(place == 0, x, pltpu.roll(f, 1, 0))
        yr, yi = chunk_scan(dim, table, y[:, : dim.N], y[:, dim.N :], reverse)
        en_ref[rows, : dim.N] = yr
        en_ref[rows, dim.N :] = yi


def norm_step(dim, x, table):
    mean = jnp.mean(x, -1, keepdims=True)
    centred = x - mean
    var = jnp.mean(centred * centred, -1, keepdims=True)
    rstd = lax.rsqrt(var + NORM_EPS)
    xhat = centred * rstd
    return xhat, rstd, xhat * row(table, GAIN) + row(table, BIAS)


def front(dim, load_act, table, w_in, xhat, rstd, drive, cf, fin, ah, al, wh, wl):
    def norm(steps, rows, _):
        xh, rs, normed = norm_step(dim, load_act(steps, rows), table)
        xhat[rows, :] = xh
        rstd[rows, :] = jnp.broadcast_to(rs, (rs.shape[0], 128))
        ah[rows, :], al[rows, :] = split(normed)
        return 0

    each_span(dim, norm)
    w_in.fill(wh, wl)
    product(ah, al, wh, wl, drive)

    def scale(j, rows, _):
        drive[rows, :] = drive[rows, :] * row(table, GAMMA)
        return 0

    each_step(dim, scale, 4)
    local_finals(dim, table, drive, cf, fin, False)


def gelu_parts(m):
    inner = GELU_C * (m + 0.044715 * (m * m * m))
    th = jnp.tanh(inner)
    return th


def back(dim, table, drive, cf, g, xhat, w_out, w_gv, w_gg, en, states, mixed, active, v, s, ah, al, wh, wl):
    entries_of(dim, table, cf, g, en, False)
    lr, li = lam_of(dim, table, LAM, False)
    lr = jnp.broadcast_to(lr, (dim.R, dim.N))
    li = jnp.broadcast_to(li, (dim.R, dim.N))

    def scan(j, rows, carry):
        d = drive[rows, :]
        mr, mi = cmul(lr, li, *carry)
        both = jnp.concatenate([mr + d[:, : dim.N], mi + d[:, dim.N :]], 1)
        states[rows, :] = both
        ah[rows, :], al[rows, :] = split(both)
        return both[:, : dim.N], both[:, dim.N :]

    each_step(dim, scan, 4, False, (en[:, : dim.N], en[:, dim.N :]))
    w_out.fill(wh, wl)
    product(ah, al, wh, wl, mixed)

    def gelu(j, rows, _):
        normed = xhat[rows, :] * row(table, GAIN) + row(table, BIAS)
        m = mixed[rows, :] + row(table, SKIP) * normed
        mixed[rows, :] = m
        a = (0.5 * m) * (1.0 + gelu_parts(m))
        active[rows, :] = a
        ah[rows, :], al[rows, :] = split(a)
        return 0

    each_step(dim, gelu, 4)
    w_gv.fill(wh, wl)
    product(ah, al, wh, wl, v)
    w_gg.fill(wh, wl)
    product(ah, al, wh, wl, s)


def gate(dim, table, v, s, rows):
    vv = v[rows, :] + row(table, BIAS_V)
    ss = jax.nn.sigmoid(s[rows, :] + row(table, BIAS_G))
    v[rows, :] = vv
    s[rows, :] = ss
    return vv * ss


def top(dim, table, load_dact, v, s, mixed, xhat, w_gv, w_gg, w_out, dv, dg, dmixed, ds, rcf, rfin, sums, ah, al, bh, bl, wh, wl):
    def dgate(j, rows, carry):
        dact = load_dact(j, rows)
        ss, vv = s[rows, :], v[rows, :]
        a = dact * ss
        b = a * vv * (1.0 - ss)
        dv[rows, :] = a
        dg[rows, :] = b
        ah[rows, :], al[rows, :] = split(a)
        bh[rows, :], bl[rows, :] = split(b)
        return carry[0] + a, carry[1] + b

    zero = jnp.zeros((dim.R, dim.H), F32)
    sv, sg = each_step(dim, dgate, 2, False, (zero, zero))
    sums[BIAS_V : BIAS_V + 1, :] = jnp.sum(sv, 0, keepdims=True)
    sums[BIAS_G : BIAS_G + 1, :] = jnp.sum(sg, 0, keepdims=True)
    w_gv.fill(wh, wl)
    product(ah, al, wh, wl, dmixed, True)
    w_gg.fill(wh, wl)
    product(bh, bl, wh, wl, dmixed, True, True)

    def dgelu(j, rows, carry):
        m = mixed[rows, :]
        th = gelu_parts(m)
        slope = 0.5 * (1.0 + th) + (0.5 * m) * (1.0 - th * th) * (GELU_C * (1.0 + (3 * 0.044715) * (m * m)))
        d = dmixed[rows, :] * slope
        dmixed[rows, :] = d
        ah[rows, :], al[rows, :] = split(d)
        normed = xhat[rows, :] * row(table, GAIN) + row(table, BIAS)
        return carry + d * normed

    sums[SKIP : SKIP + 1, :] = jnp.sum(each_step(dim, dgelu, 2, False, zero), 0, keepdims=True)
    w_out.fill(wh, wl)
    product(ah, al, wh, wl, ds, True)
    local_finals(dim, table, ds, rcf, rfin, True)


def bottom(dim, table, ds, rcf, gr, states, en, drive, xhat, rstd, dmixed, w_in, load_dact, store, dproj, buf, adj_en, sums, ah, al, wh, wl):
    entries_of(dim, table, rcf, gr, adj_en, True)
    lr, li = lam_of(dim, table, LAM, True)
    lr = jnp.broadcast_to(lr, (dim.R, dim.N))
    li = jnp.broadcast_to(li, (dim.R, dim.N))
    zero = jnp.zeros((dim.R, dim.N), F32)

    def scan(j, rows, carry):
        ar, ai, dr, di, dgam = carry
        d = ds[rows, :]
        mr, mi = cmul(lr, li, ar, ai)
        ar, ai = mr + d[:, : dim.N], mi + d[:, dim.N :]
        earlier = pl.ds(pl.multiple_of(jnp.maximum(j - 1, 0) * dim.R, dim.R), dim.R)
        before = jnp.where(j == 0, en[...], states[earlier, :])
        br, bi = before[:, : dim.N], before[:, dim.N :]
        dr = dr + (ar * br + ai * bi)
        di = di + (ai * br - ar * bi)
        u = drive[rows, :]
        dgam = dgam + (ar * u[:, : dim.N] + ai * u[:, dim.N :])
        dp = jnp.concatenate([ar, ai], 1) * row(table, GAMMA)
        dproj[rows, :] = dp
        ah[rows, :], al[rows, :] = split(dp)
        return ar, ai, dr, di, dgam

    start = (adj_en[:, : dim.N], adj_en[:, dim.N :], zero, zero, zero)
    _, _, dr, di, dgam = each_step(dim, scan, 2, True, start)
    dr, di, dgam = (jnp.sum(x, 0, keepdims=True) for x in (dr, di, dgam))
    fr, fi = lam_of(dim, table, LAM, False)
    rates = row(table, RATES)
    rate, angle = rates[:, : dim.N], rates[:, dim.N :]
    sums[5:6, : dim.N] = -rate * (dr * fr + di * fi)
    sums[5:6, dim.N :] = angle * (di * fr - dr * fi)
    sums[6:7, : dim.N] = dgam
    sums[6:7, dim.N :] = jnp.zeros_like(dgam)
    sums[7:8, :] = jnp.zeros((1, dim.H), F32)

    w_in.fill(wh, wl)
    product(ah, al, wh, wl, buf, True)
    wide = jnp.zeros((8, dim.H), F32)

    def dnorm(steps, rows, carry):
        dn = buf[rows, :] + dmixed[rows, :] * row(table, SKIP)
        xh = xhat[rows, :]
        dx = dn * row(table, GAIN)
        m1 = jnp.mean(dx, -1, keepdims=True)
        m2 = jnp.mean(dx * xh, -1, keepdims=True)
        store(steps, rows, load_dact(steps, rows) + rstd[rows, 0:1] * (dx - m1 - xh * m2))
        return carry[0] + fold(dn * xh), carry[1] + fold(dn)

    sgain, sbias = each_span(dim, dnorm, (wide, wide))
    sums[GAIN : GAIN + 1, :] = jnp.sum(sgain, 0, keepdims=True)
    sums[BIAS : BIAS + 1, :] = jnp.sum(sbias, 0, keepdims=True)


def split_rows(dim, load, xh, xl):
    def one(j, rows, _):
        xh[rows, :], xl[rows, :] = split(load(rows))
        return 0

    each_step(dim, one, 4)


class Share:
    def __init__(self, dim, nm):
        self.dim, self.nm = dim, nm
        self.q = -(-nm * dim.Hd // (8 * dim.S)) * 8
        self.step = math.gcd(self.q, dim.Hd)
        self.shape = (dim.S // 2, dim.D, self.q, dim.H)

    def place(self, m, d, r, me, my):
        p = m * self.dim.Hd + r
        s = p // self.q
        return s & 1, ((s ^ me) >> 1, d ^ my), p % self.q


class Halves:
    def __init__(self, dim):
        self.dim = dim
        self.q = dim.Hd // 2
        self.step = math.gcd(self.q, WIDE)
        self.shape = (dim.D, self.q + SMALL, dim.H)

    def place(self, m, d, r, me, my):
        return r // self.q, (d ^ my,), r % self.q


def weight_grad(dim, share, m, ah, al, bh, bl, tile, keep, send):
    me = lax.axis_index("seq")
    my = lax.axis_index("dp")
    for h0 in range(0, dim.H, WIDE):
        tile[...] = dot3(ah[:, h0 : h0 + WIDE], al[:, h0 : h0 + WIDE], bh[...], bl[...], ((0,), (0,)))

        def put(mine):
            for r0 in range(0, WIDE, share.step):
                h = h0 + r0
                odd, index, off = share.place(m, h // dim.Hd, h % dim.Hd, me, my)
                dst = keep if odd == mine else send
                dst[(*index, slice(off, off + share.step), slice(None))] = tile[r0 : r0 + share.step, :]

        for mine in range(2):
            pl.when(me & 1 == mine)(functools.partial(put, mine))


class Kept:
    def __init__(self, value):
        self.value = value
        self.shape = value.shape


def call(fn, outs, scratch, *args, us=1.0, anywhere=0):
    spaces = [pltpu.HBM] * anywhere + [pltpu.VMEM] * (len(args) - anywhere)

    def placed(x, space):
        if isinstance(x, Kept):
            return pltpu.with_memory_space_constraint(x.value, pltpu.VMEM)
        return pltpu.with_memory_space_constraint(x, pltpu.HBM) if space is pltpu.HBM else x

    values = [placed(x, space) for x, space in zip(args, spaces)]
    room = 10 << 20
    for x in scratch:
        if len(x.shape) > 1:
            room += math.prod(x.shape) * (2 if x.dtype == BF16 else 4)
    results = pl.pallas_call(
        fn,
        out_shape=outs,
        in_specs=[pl.BlockSpec(memory_space=space) for space in spaces],
        out_specs=[pl.BlockSpec(memory_space=pltpu.VMEM)] * len(outs),
        scratch_shapes=scratch,
        compiler_params=pltpu.CompilerParams(vmem_limit_bytes=max(20 << 20, room)),
        cost_estimate=pl.CostEstimate(flops=1, bytes_accessed=int(us * 3.6e6), transcendentals=0),
    )(*values)
    return [x if isinstance(o, jax.ShapeDtypeStruct) else Kept(x) for x, o in zip(results, outs)]


def f32(*shape):
    return jax.ShapeDtypeStruct(shape, F32)


def halves(dim, n):
    return [pltpu.VMEM((dim.T, dim.H), BF16)] * (2 * n) + [pltpu.VMEM((dim.H, dim.H), BF16)] * 2


def prep_kernel(dim, small, table):
    s = small[...]
    nu, theta, gam = s[5:6, : dim.N], s[5:6, dim.N :], s[6:7, : dim.N]
    rate, angle = jnp.exp(nu), jnp.exp(theta)
    mod = jnp.exp(-rate)
    re, im = mod * jnp.cos(angle), mod * jnp.sin(angle)
    gamma = jnp.exp(gam)

    def put(index, a, b):
        table[index : index + 1, : dim.N] = a
        table[index : index + 1, dim.N :] = b

    table[...] = jnp.zeros((TABLE, dim.H), F32)
    table[:5, :] = s[:5]
    put(GAMMA, gamma, gamma)
    put(LAM, re, im)
    put(RATES, rate, angle)
    power = 1
    while power < dim.L:
        re, im = cmul(re, im, re, im)
        power *= 2
    for index in (LAM1, LAM2, LAM4, LAM8):
        put(index, re, im)
        re, im = cmul(re, im, re, im)


def shard_of(sources, name, rows, H):
    layer, m = name
    return sources[(0, 1, 2, 2)[m]].at[layer, rows, pl.ds(H if m == 3 else 0, H)]


def pack_kernel(dim, in_map, out_map, glu, gain, bias, skip, nu, theta, gamma, glu_bias, *refs):
    outs, held, sem = refs[:3], refs[3:-1], refs[-1]
    vectors = (gain, bias, skip, nu, theta, gamma, glu_bias)
    me, my = lax.axis_index("seq"), lax.axis_index("dp")
    start = pl.multiple_of(jnp.minimum(me, dim.used - 1) * dim.q, 16)
    moves = []
    for src, dst in zip(vectors, held):
        moves.append(pltpu.make_async_copy(src, dst, sem.at[len(moves)]))
    gain, bias, skip, nu, theta, gamma, glu_bias = held
    for out, chunk in zip(outs, CHUNKS):
        head = out.shape[0] - len(chunk) * dim.q
        for i, name in enumerate(chunk):
            src = shard_of((in_map, out_map, glu), name, pl.ds(start, dim.q), dim.H)
            dst = out.at[head + i * dim.q : head + (i + 1) * dim.q, :]
            moves.append(pltpu.make_async_copy(src, dst, sem.at[len(moves)]))
    for move in moves:
        move.start()
    for move in moves[: len(held)]:
        move.wait()

    def spread(ref, layer, width):
        vec = ref[layer : layer + 1, :]
        full = jnp.concatenate([vec] * (width // vec.shape[1]), 1)
        lane = lax.broadcasted_iota(jnp.int32, full.shape, 1)
        return jnp.where(lane // vec.shape[1] == my, full, 0.0)

    for layer in range(dim.layers):
        both = spread(glu_bias, layer, 2 * dim.H)
        rows = [spread(ref, layer, dim.H) for ref in (gain, bias, skip)] + [both[:, : dim.H], both[:, dim.H :]]
        rows.append(jnp.concatenate([spread(nu, layer, dim.N), spread(theta, layer, dim.N)], 1))
        rows.append(jnp.concatenate([spread(gamma, layer, dim.N), jnp.zeros((1, dim.N), F32)], 1))
        for i, value in enumerate(rows):
            outs[layer][i : i + 1, :] = value
        outs[layer][7:8, :] = jnp.zeros((1, dim.H), F32)
    for move in moves[len(held) :]:
        move.wait()


class Weight:
    def __init__(self, dim, name, place, sources, own, buf, sem):
        self.dim, self.name, self.place = dim, name, place
        self.sources, self.own, self.buf, self.sem = sources, own, buf, sem
        self.here = False

    def moves(self):
        shard = shard_of(self.sources, self.name, slice(None), self.dim.H)
        yield pltpu.make_async_copy(shard, self.own, self.sem.at[self.dim.S])
        for k, piece in enumerate(self.sources[3:]):
            yield pltpu.make_async_copy(piece.at[self.place], self.buf.at[k], self.sem.at[k])

    def start(self):
        for move in self.moves():
            move.start()

    def fill(self, wh, wl):
        dim, q = self.dim, self.dim.q
        if not self.here:
            for move in self.moves():
                move.wait()
        self.here = True
        me, my = lax.axis_index("seq"), lax.axis_index("dp")

        def put(start, n, value):
            rows = pl.ds(pl.multiple_of(start, 16), n)
            wh[rows, :], wl[rows, :] = split(value)

        def mine(i, _):
            put(my * dim.Hd + i * 32, 32, self.own[pl.ds(pl.multiple_of(i * 32, 32), 32), :])
            return 0

        lax.fori_loop(0, dim.Hd // 32, mine, 0)

        def one(k, _):
            s = k ^ me

            def block():
                for kz in range(1, dim.D):
                    put((kz ^ my) * dim.Hd + s * q, q, self.buf[k, kz - 1])

            if dim.used < dim.S:
                pl.when(s < dim.used)(block)
            else:
                block()
            return 0

        lax.fori_loop(0, dim.S, one, 0)


def weights_in(dim, chunks, names, fn):
    first = 3 + len(chunks) * dim.S

    def kernel(*refs):
        spare = refs[len(refs) - 3 * len(names) :]
        weights = []
        for i, name in enumerate(names):
            (n,) = [n for n, c in enumerate(chunks) if name in CHUNKS[c]]
            sources = refs[:3] + refs[3 + n * dim.S : 3 + (n + 1) * dim.S]
            place = CHUNKS[chunks[n]].index(name)
            weights.append(Weight(dim, name, place, sources, *spare[3 * i : 3 * i + 3]))
        for w in weights:
            w.start()
        fn(dim, weights, *refs[first : len(refs) - 3 * len(names)])

    scratch = [
        pltpu.VMEM((dim.Hd, dim.H), F32),
        pltpu.VMEM((dim.S, dim.D - 1, dim.q, dim.H), F32),
        pltpu.SemaphoreType.DMA((dim.S + 1,)),
    ] * len(names)
    return kernel, first, scratch


def strided(dim, ref):
    def load(steps, rows):
        if isinstance(steps, list):
            return jnp.concatenate([ref[:, j, :] for j in steps], 0)
        return ref[:, steps, :]

    return load


def plain(ref):
    return lambda j, rows: ref[rows, :]


def k_a0(dim, weights, x, table, xhat, rstd, drive, cf, fin, ah, al, wh, wl):
    front(dim, strided(dim, x), table, weights[0], xhat, rstd, drive, cf, fin, ah, al, wh, wl)


def k_b0(dim, weights, x, t, t1, drive, cf, g, xhat,
         en, states, mixed, active, v, s, act1, xhat1, rstd1, drive1, cf1, fin1, ah, al, wh, wl):
    w_out, w_gv, w_gg, w_in1 = weights
    back(dim, t, drive, cf, g, xhat, w_out, w_gv, w_gg, en, states, mixed, active, v, s, ah, al, wh, wl)
    load = strided(dim, x)

    def residual(steps, rows):
        act = load(steps, rows) + gate(dim, t, v, s, rows)
        act1[rows, :] = act
        return act

    front(dim, residual, t1, w_in1, xhat1, rstd1, drive1, cf1, fin1, ah, al, wh, wl)


def k_b1(dim, weights, act1, out_grad, t, drive, cf, g, xhat,
         out, en, states, active, dv, dg, dmixed, ds, rcf, rfin, sums, ah, al, bh, bl, wh, wl, mixed, v, s):
    w_out, w_gv, w_gg = weights
    back(dim, t, drive, cf, g, xhat, w_out, w_gv, w_gg, en, states, mixed, active, v, s, ah, al, wh, wl)

    def residual(j, rows, _):
        out[:, j, :] = act1[rows, :] + gate(dim, t, v, s, rows)
        return 0

    each_step(dim, residual, 2)
    sums[...] = jnp.zeros((SMALL, dim.H), F32)
    top(dim, t, strided(dim, out_grad), v, s, mixed, xhat, w_gv, w_gg, w_out, dv, dg, dmixed, ds, rcf, rfin, sums,
        ah, al, bh, bl, wh, wl)


def k_w1(dim, share, active, dv, dg, states, dmixed, keep, send, ah, al, bh, bl, tile):
    split_rows(dim, lambda rows: active[rows, :], ah, al)
    for m, ref in ((0, dv), (1, dg)):
        split_rows(dim, lambda rows: ref[rows, :], bh, bl)
        weight_grad(dim, share, m, ah, al, bh, bl, tile, keep, send)
    split_rows(dim, lambda rows: states[rows, :], ah, al)
    split_rows(dim, lambda rows: dmixed[rows, :], bh, bl)
    weight_grad(dim, share, 2, ah, al, bh, bl, tile, keep, send)


def k_c1(dim, weights, out_grad, t, t0, ds, rcf, gr, states, en, drive, xhat, rstd, dmixed,
         xhat0, mixed0, v0, s0,
         dproj, dmid, dv0, dg0, dmixed0, ds0, rcf0, rfin0, sums1, sums0, ah, al, bh, bl, wh, wl, adj_en):
    w_in, w_gv, w_gg, w_out = weights

    def store(j, rows, value):
        dmid[rows, :] = value

    bottom(dim, t, ds, rcf, gr, states, en, drive, xhat, rstd, dmixed, w_in, strided(dim, out_grad), store,
           dproj, ds0, adj_en, sums1, ah, al, wh, wl)
    sums0[...] = jnp.zeros((SMALL, dim.H), F32)
    top(dim, t0, plain(dmid), v0, s0, mixed0, xhat0, w_gv, w_gg, w_out, dv0, dg0, dmixed0, ds0, rcf0, rfin0,
        sums0, ah, al, bh, bl, wh, wl)


def k_w2(dim, share, active, dv, dg, states, dmixed, xhat1, dproj1, t, keep, send, ah, al, bh, bl, tile):
    k_w1(dim, share, active, dv, dg, states, dmixed, keep, send, ah, al, bh, bl, tile)
    split_rows(dim, lambda rows: xhat1[rows, :] * row(t, GAIN) + row(t, BIAS), ah, al)
    split_rows(dim, lambda rows: dproj1[rows, :], bh, bl)
    weight_grad(dim, share, 3, ah, al, bh, bl, tile, keep, send)


def k_c0(share, dim, weights, t, ds, rcf, gr, states, en, drive, xhat, rstd, dmixed, dmid, sums1a, sums1b, sums0a,
         input_grad, keep, send, ah, al, bh, bl, wh, wl, adj_en, dproj, buf, sums0, tile):
    def store(steps, rows, value):
        for u, j in enumerate(steps):
            input_grad[:, j, :] = value[u * dim.R : (u + 1) * dim.R, :]

    bottom(dim, t, ds, rcf, gr, states, en, drive, xhat, rstd, dmixed, weights[0], plain(dmid), store, dproj, buf, adj_en,
           sums0, ah, al, wh, wl)
    split_rows(dim, lambda rows: xhat[rows, :] * row(t, GAIN) + row(t, BIAS), bh, bl)
    weight_grad(dim, share, 0, bh, bl, ah, al, tile, keep, send)
    place = lax.broadcasted_iota(jnp.int32, (SMALL, dim.H), 0)
    upper = (place >= SKIP) & (place <= BIAS_G)
    tile[0:SMALL, :] = jnp.where(upper, sums0a[...], sums0[...])
    tile[SMALL : 2 * SMALL, :] = jnp.where(upper, sums1a[...], sums1b[...])
    me = lax.axis_index("seq")

    def put(mine):
        for layer in range(dim.layers):
            dst = keep if layer == mine else send
            for d in range(dim.D):
                dst[d, share.q :, :] = tile[layer * SMALL : (layer + 1) * SMALL, :]

    for mine in range(2):
        pl.when(me & 1 == mine)(functools.partial(put, mine))


def tie(x, others):
    x, *others = lax.optimization_barrier((x, *others))
    return x, others


def swap(x, axis, mask):
    count = lax.axis_size(axis)
    return lax.ppermute(x, axis, [(i, i ^ mask) for i in range(count)])


def chips_gather(dim, x):
    return [x] + [swap(x, "seq", k) for k in range(2, dim.S, 2)]


def cores_gather(pieces):
    return [p for x in pieces for p in (x, swap(x, "seq", 1))]


def plane_gather(dim, x):
    return cores_gather(chips_gather(dim, x))


def tree_sum(parts):
    while len(parts) > 1:
        parts = [a + b for a, b in zip(parts[::2], parts[1::2])]
    return parts[0]


def half_sums(dim, keep, send):
    got = swap(send, "seq", 1)
    return [keep[k] + got[k] for k in range(dim.S // 2)]


def plane_sums(dim, half):
    others = [swap(half[k], "seq", 2 * k) for k in range(1, dim.S // 2)]
    return [sum((o[k] for o in others), half[0][k]) for k in range(dim.D)]


def dp_sum(dim, parts):
    return sum((swap(parts[k], "dp", k) for k in range(1, dim.D)), parts[0])


def unpack_kernel(dim, shares, kinds, last, *refs):
    lower, upper, outs, (mine, other) = refs[: dim.S], refs[dim.S : 2 * dim.S], refs[2 * dim.S : -2], refs[-2:]
    head = last.q + SMALL
    for dst, first in ((mine, 0), (other, 1)):
        dst[...] = tree_sum([lower[k][:head, :] for k in range(first, dim.S, 2)])
    g_gain, g_bias, g_nu, g_theta, g_gamma, g_in, g_out, g_skip, g_glu, g_glu_bias = outs
    me, my = lax.axis_index("seq"), lax.axis_index("dp")

    def place(layer, kind, rows, value):
        if kind == "in":
            g_in[layer, rows, :] = value
        elif kind == "out":
            g_out[layer, rows, :] = value
        elif kind == "gv":
            g_glu[layer, rows, 0 : dim.H] = value
        else:
            g_glu[layer, rows, dim.H : 2 * dim.H] = value

    def put(k, s):
        for share, names, src, base in zip(shares, kinds, (lower[k], upper[k]), (head, 0)):
            for off in range(0, share.q, share.step):
                p = s * share.q + off
                if p // dim.Hd < share.nm:
                    layer, kind = names[p // dim.Hd]
                    r = p % dim.Hd
                    place(layer, kind, slice(r, r + share.step), src[base + off : base + off + share.step, :])

    def vectors(d):
        def own(layer, index, lo, width, out, at=0):
            src = (mine, other)

            def copy(ref):
                start = lo + d * width
                out[layer : layer + 1, :] = ref[last.q + index : last.q + index + 1, start : start + width]

            pl.when(me & 1 == layer)(functools.partial(copy, src[0]))
            pl.when(me & 1 != layer)(functools.partial(copy, src[1]))

        for layer in range(dim.layers):
            for index, out in ((GAIN, g_gain), (BIAS, g_bias), (SKIP, g_skip)):
                own(layer, index, 0, dim.Hd, out)
            n = dim.N // dim.D
            own(layer, 5, 0, n, g_nu)
            own(layer, 5, dim.N, n, g_theta)
            own(layer, 6, 0, n, g_gamma)
            width = 2 * dim.H // dim.D
            index = BIAS_V if d * width < dim.H else BIAS_G
            own(layer, index, 0 if index == BIAS_V else -dim.H, width, g_glu_bias)

    for who in range(dim.S):

        def all_of(who=who):
            for k in range(dim.S):
                put(k, k ^ who)
            half = who & 1
            for ref, part in ((mine, half), (other, 1 - half)):
                place(0, "in", slice(part * last.q, (part + 1) * last.q), ref[: last.q, :])

        pl.when(me == who)(all_of)
    for d in range(dim.D):
        pl.when(my == d)(functools.partial(vectors, d))


def unpack(dim, shares, kinds, last, lower, upper):
    n, l = dim.N // dim.D, dim.layers
    vec, small = f32(l, dim.Hd), f32(l, n)
    mat, wide = f32(l, dim.Hd, dim.H), f32(l, dim.Hd, 2 * dim.H)
    outs = [vec, vec, small, small, small, mat, mat, vec, wide, f32(l, 2 * dim.H // dim.D)]
    return call(functools.partial(unpack_kernel, dim, shares, kinds, last), outs, [pltpu.VMEM((last.q + SMALL, dim.H), F32)] * 2, *lower, *upper)


def body(inputs, out_grad, ln_gain, ln_bias, nu_log, theta_log, gamma_log, in_map, out_map, skip_gain, glu_weight, glu_bias):
    dim = Dims(inputs, in_map, lax.axis_size("dp"), lax.axis_size("seq"))
    T, H, N, R, B, D, S = dim.T, dim.H, dim.N, dim.R, dim.B, dim.D, dim.S
    me, my = lax.axis_index("seq"), lax.axis_index("dp")
    x = inputs.reshape(R, dim.L, H)
    og = out_grad.reshape(R, dim.L, H)

    heads = [SMALL, SMALL, 0]
    vectors = (ln_gain, ln_bias, skip_gain, nu_log, theta_log, gamma_log, glu_bias)
    messages = call(
        functools.partial(pack_kernel, dim),
        [f32(head + len(chunk) * dim.q, H) for head, chunk in zip(heads, CHUNKS)],
        [pltpu.VMEM(v.shape, F32) for v in vectors] + [pltpu.SemaphoreType.DMA((len(vectors) + sum(map(len, CHUNKS)),))],
        in_map, out_map, glu_weight, *vectors,
        anywhere=3 + len(vectors),
    )
    def stacked(others, head):
        return jnp.stack([other[head:].reshape(-1, dim.q, H) for other in others], 1)

    def along_dp(mine):
        return [swap(mine, "dp", k) for k in range(1, D)]

    def table_of(mine, others, head=SMALL):
        total = mine[:head]
        for other in others:
            total = total + other[:head]
        return call(functools.partial(prep_kernel, dim), [f32(TABLE, H)], [], total)[0]

    mine0, mine1, mine2 = messages
    others0 = along_dp(mine0)
    table0 = table_of(mine0, others0)
    mine1, others0 = tie(mine1, others0)
    others1 = along_dp(mine1)
    table1 = table_of(mine1, others1)
    chips0 = chips_gather(dim, stacked(others0, SMALL))
    joined1, chips0 = tie(stacked(others1, SMALL), chips0)
    pieces0 = cores_gather(chips0)
    mine2, (joined1,) = tie(mine2, [joined1])
    chips1 = chips_gather(dim, joined1)
    blocks = mine2[None]
    while blocks.shape[0] < D:
        blocks = jnp.concatenate([blocks, swap(blocks, "dp", blocks.shape[0])], 0)
    joined2 = stacked([blocks[k] for k in range(1, D)], 0)
    pieces = [pieces0, cores_gather(chips1), None]

    big, ent, fins = pltpu.VMEM((T, H), F32), pltpu.VMEM((R, H), F32), f32(B, H)
    stat = pltpu.VMEM((T, 128), F32)
    vec = pltpu.VMEM((SMALL, H), F32)

    def k(fn, names, outs, scratch, *args, us):
        chunks = [c for c, chunk in enumerate(CHUNKS) if set(chunk) & set(names)]
        kernel, count, own = weights_in(dim, chunks, names, fn)
        sources = [in_map, out_map, glu_weight] + [p for c in chunks for p in pieces[c]]
        return call(kernel, outs, scratch + own, *sources, *args, us=us, anywhere=count)

    def carried(fin):
        return lax.all_gather(fin, "seq")

    xhat0, rstd0, drive0, cf0, fin0 = k(
        k_a0, [(0, 0)], [big, stat, big, ent, fins], halves(dim, 1), x, table0, us=3.4
    )
    g0 = carried(fin0)
    joined2, (g0,) = tie(joined2, [g0])
    chips2 = chips_gather(dim, joined2)
    en0, states0, mixed0, active0, v0, s0, act1, xhat1, rstd1, drive1, cf1, fin1 = k(
        k_b0,
        [(0, 1), (0, 2), (0, 3), (1, 0)],
        [ent, big, big, big, big, big, big, big, stat, big, ent, fins],
        halves(dim, 1),
        x, table0, table1, drive0, cf0, g0, xhat0,
        us=10.0,
    )
    fin1, chips2 = tie(fin1, chips2)
    g1 = carried(fin1)
    pieces[2] = cores_gather(chips2)
    spare = [pltpu.VMEM((T, H), F32)]
    out, en1, states1, active1, dv1, dg1, dmixed1, ds1, rcf1, rfin1, sums1a = k(
        k_b1,
        [(1, 1), (1, 2), (1, 3)],
        [f32(R, dim.L, H), ent, big, big, big, big, big, big, ent, fins, vec],
        halves(dim, 2) + spare * 3,
        act1, og, table1, drive1, cf1, g1, xhat1,
        us=13.0,
    )
    share1, share2, share3 = Share(dim, 3), Share(dim, 4), Halves(dim)
    tile = [pltpu.VMEM((WIDE, H), F32)]
    pair = [pltpu.VMEM((T, H), BF16)] * 4
    keep1, send1 = call(
        functools.partial(k_w1, dim, share1), [f32(*share1.shape)] * 2, pair + tile,
        active1, dv1, dg1, states1, dmixed1, us=5.0,
    )
    rfin1, (send1,) = tie(rfin1, [send1])
    gr1 = carried(rfin1)
    gr1, half1 = tie(gr1, half_sums(dim, keep1, send1))
    dproj1, dmid, dv0, dg0, dmixed0, ds0, rcf0, rfin0, sums1b, sums0a = k(
        k_c1,
        [(1, 0), (0, 2), (0, 3), (0, 1)],
        [big, big, big, big, big, big, ent, fins, vec, vec],
        halves(dim, 2) + [pltpu.VMEM((R, H), F32)],
        og, table1, table0, ds1, rcf1, gr1, states1, en1, drive1, xhat1, rstd1, dmixed1,
        xhat0, mixed0, v0, s0,
        us=11.0,
    )
    keep2, send2 = call(
        functools.partial(k_w2, dim, share2), [f32(*share2.shape)] * 2, pair + tile,
        active0, dv0, dg0, states0, dmixed0, xhat1, dproj1, table1, us=6.4,
    )
    rfin0, (send2, *sums1) = tie(rfin0, [send2, *plane_sums(dim, half1)])
    gr0 = carried(rfin0)
    gr0, half2 = tie(gr0, half_sums(dim, keep2, send2))
    input_grad, keep3, send3 = k(
        functools.partial(k_c0, share3),
        [(0, 0)],
        [f32(R, dim.L, H)] + [f32(*share3.shape)] * 2,
        halves(dim, 2) + [pltpu.VMEM((R, H), F32)] + spare * 2 + [pltpu.VMEM((SMALL, H), F32)] + tile,
        table0, ds0, rcf0, gr0, states0, en0, drive0, xhat0, rstd0, dmixed0, dmid, sums1a, sums1b, sums0a,
        us=7.4,
    )
    sums2 = plane_sums(dim, half2)
    got3 = swap(send3, "seq", 1)
    half3 = [jnp.concatenate([keep3[d] + got3[d], sums1[d]], 0) for d in range(D)]
    total3 = tree_sum([half3[0]] + [swap(half3[k], "dp", k) for k in range(1, D)])
    chips3 = chips_gather(dim, total3)
    joint, chips3 = tie(dp_sum(dim, sums2), chips3)
    last = cores_gather(chips3)
    upper = plane_gather(dim, joint)
    kinds = [[(1, "gv"), (1, "gg"), (1, "out")], [(0, "gv"), (0, "gg"), (0, "out"), (1, "in")]]
    grads = unpack(dim, (share1, share2), kinds, share3, last, upper)
    return (out.reshape(inputs.shape), input_grad.reshape(inputs.shape), *grads)


def solution(mesh):
    act, vec, mat = P("dp", "seq", None), P(None, "dp"), P(None, "dp", None)
    in_specs = (act, act, vec, vec, vec, vec, vec, mat, mat, vec, mat, vec)
    out_specs = (act, act, vec, vec, vec, vec, vec, mat, mat, vec, mat, vec)
    return jax.shard_map(body, mesh=mesh, in_specs=in_specs, out_specs=out_specs, check_vma=False)
```

```python
import functools
import math

import jax
import jax.numpy as jnp
from jax import lax
from jax.experimental import pallas as pl
from jax.experimental.pallas import tpu as pltpu
from jax.sharding import PartitionSpec as P

NORM_EPS = 1e-05
GROUPS = 8
WIDE = 256
SMALL = 8
TABLE = 16
F32 = jnp.float32
BF16 = jnp.bfloat16
GELU_C = math.sqrt(2.0 / math.pi)

GAIN, BIAS, SKIP, BIAS_V, BIAS_G, GAMMA, LAM, LAM1, LAM2, LAM4, LAM8, RATES = range(12)


CHUNKS = (((0, 0), (1, 0)), ((0, 1), (0, 2), (0, 3)), ((1, 1), (1, 2), (1, 3)))


class Dims:
    def __init__(self, inputs, in_map, dp, seq):
        self.B, self.Tb, self.H = inputs.shape
        self.layers, self.Hd = in_map.shape[:2]
        self.N = self.H // 2
        self.T = self.B * self.Tb
        self.R = self.B * GROUPS
        self.L = self.Tb // GROUPS
        self.D, self.S = dp, seq
        self.q = max(16, self.Hd // seq)
        self.used = self.Hd // self.q


def cmul(ar, ai, br, bi):
    return ar * br - ai * bi, ar * bi + ai * br


def split(x):
    hi = x.astype(BF16)
    return hi, (x - hi.astype(F32)).astype(BF16)


def dot3(ah, al, bh, bl, dims):
    def one(a, b):
        return lax.dot_general(a, b, (dims, ((), ())), preferred_element_type=F32)

    return one(ah, bh) + (one(ah, bl) + one(al, bh))


def product(ah, al, wh, wl, dst, transposed=False, add=False):
    for n in range(dst.shape[1] // WIDE):
        cols = slice(n * WIDE, (n + 1) * WIDE)
        if transposed:
            res = dot3(ah[...], al[...], wh[cols, :], wl[cols, :], ((1,), (1,)))
        else:
            res = dot3(ah[...], al[...], wh[:, cols], wl[:, cols], ((1,), (0,)))
        dst[:, cols] = dst[:, cols] + res if add else res


def each_step(dim, fn, unroll=2, reverse=False, init=0):
    def one(i, carry):
        j = dim.L - 1 - i if reverse else i
        rows = pl.ds(pl.multiple_of(j * dim.R, dim.R), dim.R)
        return fn(j, rows, carry)

    return lax.fori_loop(0, dim.L, one, init, unroll=unroll)


def each_span(dim, fn, init=0, steps=8):
    def one(i, carry):
        rows = pl.ds(pl.multiple_of(i * steps * dim.R, steps * dim.R), steps * dim.R)
        return fn([i * steps + u for u in range(steps)], rows, carry)

    return lax.fori_loop(0, dim.L // steps, one, init)


def fold(x):
    return jnp.sum(x.reshape(x.shape[0] // 8, 8, x.shape[1]), 0)


def row(table, index, n=1):
    return table[index : index + n, :]


def lam_of(dim, table, index, reverse):
    pair = table[index : index + 1, :]
    real, imag = pair[:, : dim.N], pair[:, dim.N :]
    return real, -imag if reverse else imag


def chunk_scan(dim, table, yr, yi, reverse):
    place = lax.broadcasted_iota(jnp.int32, yr.shape, 0)
    for dist, index in ((1, LAM1), (2, LAM2), (4, LAM4)):
        pr, pi = lam_of(dim, table, index, reverse)
        if reverse:
            shift, seen = GROUPS - dist, place < GROUPS - dist
        else:
            shift, seen = dist, place >= dist
        sr = jnp.where(seen, pltpu.roll(yr, shift, 0), 0.0)
        si = jnp.where(seen, pltpu.roll(yi, shift, 0), 0.0)
        mr, mi = cmul(pr, pi, sr, si)
        yr, yi = yr + mr, yi + mi
    return yr, yi


def local_finals(dim, table, drive_ref, cf_ref, f_ref, reverse):
    lr, li = lam_of(dim, table, LAM, reverse)
    lr = jnp.broadcast_to(lr, (dim.R, dim.N))
    li = jnp.broadcast_to(li, (dim.R, dim.N))

    def step(j, rows, carry):
        d = drive_ref[rows, :]
        mr, mi = cmul(lr, li, *carry)
        return mr + d[:, : dim.N], mi + d[:, dim.N :]

    zero = jnp.zeros((dim.R, dim.N), F32)
    fr, fi = each_step(dim, step, 4, reverse, (zero, zero))
    cf_ref[:, : dim.N] = fr
    cf_ref[:, dim.N :] = fi
    last = 0 if reverse else GROUPS - 1
    for b in range(dim.B):
        rows = slice(b * GROUPS, (b + 1) * GROUPS)
        yr, yi = chunk_scan(dim, table, fr[rows], fi[rows], reverse)
        f_ref[b : b + 1, : dim.N] = yr[last : last + 1]
        f_ref[b : b + 1, dim.N :] = yi[last : last + 1]


def entries_of(dim, table, cf_ref, g_ref, en_ref, reverse):
    me = lax.axis_index("seq")
    lr, li = lam_of(dim, table, LAM8, reverse)
    xr = jnp.zeros((dim.B, dim.N), F32)
    xi = xr
    order = reversed(range(dim.S)) if reverse else range(dim.S)
    for other in order:
        ahead = other > me if reverse else other < me
        g = g_ref[other]
        mr, mi = cmul(lr, li, xr, xi)
        xr = jnp.where(ahead, mr + g[:, : dim.N], xr)
        xi = jnp.where(ahead, mi + g[:, dim.N :], xi)
    for b in range(dim.B):
        rows = slice(b * GROUPS, (b + 1) * GROUPS)
        f = cf_ref[rows, :]
        place = lax.broadcasted_iota(jnp.int32, f.shape, 0)
        x = jnp.concatenate([xr[b : b + 1], xi[b : b + 1]], 1)
        if reverse:
            y = jnp.where(place == GROUPS - 1, x, pltpu.roll(f, GROUPS - 1, 0))
        else:
            y = jnp.where(place == 0, x, pltpu.roll(f, 1, 0))
        yr, yi = chunk_scan(dim, table, y[:, : dim.N], y[:, dim.N :], reverse)
        en_ref[rows, : dim.N] = yr
        en_ref[rows, dim.N :] = yi


def norm_step(dim, x, table):
    mean = jnp.mean(x, -1, keepdims=True)
    centred = x - mean
    var = jnp.mean(centred * centred, -1, keepdims=True)
    rstd = lax.rsqrt(var + NORM_EPS)
    xhat = centred * rstd
    return xhat, rstd, xhat * row(table, GAIN) + row(table, BIAS)


def front(dim, load_act, table, w_in, xhat, rstd, drive, cf, fin, ah, al, wh, wl):
    def norm(steps, rows, _):
        xh, rs, normed = norm_step(dim, load_act(steps, rows), table)
        xhat[rows, :] = xh
        rstd[rows, :] = jnp.broadcast_to(rs, (rs.shape[0], 128))
        ah[rows, :], al[rows, :] = split(normed)
        return 0

    each_span(dim, norm)
    w_in.fill(wh, wl)
    product(ah, al, wh, wl, drive)

    def scale(j, rows, _):
        drive[rows, :] = drive[rows, :] * row(table, GAMMA)
        return 0

    each_step(dim, scale, 4)
    local_finals(dim, table, drive, cf, fin, False)


def gelu_parts(m):
    inner = GELU_C * (m + 0.044715 * (m * m * m))
    th = jnp.tanh(inner)
    return th


def back(dim, table, drive, cf, g, xhat, w_out, w_gv, w_gg, en, states, mixed, active, v, s, ah, al, wh, wl):
    entries_of(dim, table, cf, g, en, False)
    lr, li = lam_of(dim, table, LAM, False)
    lr = jnp.broadcast_to(lr, (dim.R, dim.N))
    li = jnp.broadcast_to(li, (dim.R, dim.N))

    def scan(j, rows, carry):
        d = drive[rows, :]
        mr, mi = cmul(lr, li, *carry)
        both = jnp.concatenate([mr + d[:, : dim.N], mi + d[:, dim.N :]], 1)
        states[rows, :] = both
        ah[rows, :], al[rows, :] = split(both)
        return both[:, : dim.N], both[:, dim.N :]

    each_step(dim, scan, 4, False, (en[:, : dim.N], en[:, dim.N :]))
    w_out.fill(wh, wl)
    product(ah, al, wh, wl, mixed)

    def gelu(j, rows, _):
        normed = xhat[rows, :] * row(table, GAIN) + row(table, BIAS)
        m = mixed[rows, :] + row(table, SKIP) * normed
        mixed[rows, :] = m
        a = (0.5 * m) * (1.0 + gelu_parts(m))
        active[rows, :] = a
        ah[rows, :], al[rows, :] = split(a)
        return 0

    each_step(dim, gelu, 4)
    w_gv.fill(wh, wl)
    product(ah, al, wh, wl, v)
    w_gg.fill(wh, wl)
    product(ah, al, wh, wl, s)


def gate(dim, table, v, s, rows):
    vv = v[rows, :] + row(table, BIAS_V)
    ss = jax.nn.sigmoid(s[rows, :] + row(table, BIAS_G))
    v[rows, :] = vv
    s[rows, :] = ss
    return vv * ss


def top(dim, table, load_dact, v, s, mixed, xhat, w_gv, w_gg, w_out, dv, dg, dmixed, ds, rcf, rfin, sums, ah, al, bh, bl, wh, wl):
    def dgate(j, rows, carry):
        dact = load_dact(j, rows)
        ss, vv = s[rows, :], v[rows, :]
        a = dact * ss
        b = a * vv * (1.0 - ss)
        dv[rows, :] = a
        dg[rows, :] = b
        ah[rows, :], al[rows, :] = split(a)
        bh[rows, :], bl[rows, :] = split(b)
        return carry[0] + a, carry[1] + b

    zero = jnp.zeros((dim.R, dim.H), F32)
    sv, sg = each_step(dim, dgate, 2, False, (zero, zero))
    sums[BIAS_V : BIAS_V + 1, :] = jnp.sum(sv, 0, keepdims=True)
    sums[BIAS_G : BIAS_G + 1, :] = jnp.sum(sg, 0, keepdims=True)
    w_gv.fill(wh, wl)
    product(ah, al, wh, wl, dmixed, True)
    w_gg.fill(wh, wl)
    product(bh, bl, wh, wl, dmixed, True, True)

    def dgelu(j, rows, carry):
        m = mixed[rows, :]
        th = gelu_parts(m)
        slope = 0.5 * (1.0 + th) + (0.5 * m) * (1.0 - th * th) * (GELU_C * (1.0 + (3 * 0.044715) * (m * m)))
        d = dmixed[rows, :] * slope
        dmixed[rows, :] = d
        ah[rows, :], al[rows, :] = split(d)
        normed = xhat[rows, :] * row(table, GAIN) + row(table, BIAS)
        return carry + d * normed

    sums[SKIP : SKIP + 1, :] = jnp.sum(each_step(dim, dgelu, 2, False, zero), 0, keepdims=True)
    w_out.fill(wh, wl)
    product(ah, al, wh, wl, ds, True)
    local_finals(dim, table, ds, rcf, rfin, True)


def bottom(dim, table, ds, rcf, gr, states, en, drive, xhat, rstd, dmixed, w_in, load_dact, store, dproj, buf, adj_en, sums, ah, al, wh, wl):
    entries_of(dim, table, rcf, gr, adj_en, True)
    lr, li = lam_of(dim, table, LAM, True)
    lr = jnp.broadcast_to(lr, (dim.R, dim.N))
    li = jnp.broadcast_to(li, (dim.R, dim.N))
    zero = jnp.zeros((dim.R, dim.N), F32)

    def scan(j, rows, carry):
        ar, ai, dr, di, dgam = carry
        d = ds[rows, :]
        mr, mi = cmul(lr, li, ar, ai)
        ar, ai = mr + d[:, : dim.N], mi + d[:, dim.N :]
        earlier = pl.ds(pl.multiple_of(jnp.maximum(j - 1, 0) * dim.R, dim.R), dim.R)
        before = jnp.where(j == 0, en[...], states[earlier, :])
        br, bi = before[:, : dim.N], before[:, dim.N :]
        dr = dr + (ar * br + ai * bi)
        di = di + (ai * br - ar * bi)
        u = drive[rows, :]
        dgam = dgam + (ar * u[:, : dim.N] + ai * u[:, dim.N :])
        dp = jnp.concatenate([ar, ai], 1) * row(table, GAMMA)
        dproj[rows, :] = dp
        ah[rows, :], al[rows, :] = split(dp)
        return ar, ai, dr, di, dgam

    start = (adj_en[:, : dim.N], adj_en[:, dim.N :], zero, zero, zero)
    _, _, dr, di, dgam = each_step(dim, scan, 2, True, start)
    dr, di, dgam = (jnp.sum(x, 0, keepdims=True) for x in (dr, di, dgam))
    fr, fi = lam_of(dim, table, LAM, False)
    rates = row(table, RATES)
    rate, angle = rates[:, : dim.N], rates[:, dim.N :]
    sums[5:6, : dim.N] = -rate * (dr * fr + di * fi)
    sums[5:6, dim.N :] = angle * (di * fr - dr * fi)
    sums[6:7, : dim.N] = dgam
    sums[6:7, dim.N :] = jnp.zeros_like(dgam)
    sums[7:8, :] = jnp.zeros((1, dim.H), F32)

    w_in.fill(wh, wl)
    product(ah, al, wh, wl, buf, True)
    wide = jnp.zeros((8, dim.H), F32)

    def dnorm(steps, rows, carry):
        dn = buf[rows, :] + dmixed[rows, :] * row(table, SKIP)
        xh = xhat[rows, :]
        dx = dn * row(table, GAIN)
        m1 = jnp.mean(dx, -1, keepdims=True)
        m2 = jnp.mean(dx * xh, -1, keepdims=True)
        store(steps, rows, load_dact(steps, rows) + rstd[rows, 0:1] * (dx - m1 - xh * m2))
        return carry[0] + fold(dn * xh), carry[1] + fold(dn)

    sgain, sbias = each_span(dim, dnorm, (wide, wide))
    sums[GAIN : GAIN + 1, :] = jnp.sum(sgain, 0, keepdims=True)
    sums[BIAS : BIAS + 1, :] = jnp.sum(sbias, 0, keepdims=True)


def split_rows(dim, load, xh, xl):
    def one(j, rows, _):
        xh[rows, :], xl[rows, :] = split(load(rows))
        return 0

    each_step(dim, one, 4)


class Share:
    def __init__(self, dim, nm):
        self.dim, self.nm = dim, nm
        self.q = -(-nm * dim.Hd // (8 * dim.S)) * 8
        self.step = math.gcd(self.q, dim.Hd)
        self.shape = (dim.S // 2, dim.D, self.q, dim.H)

    def place(self, m, d, r, me, my):
        p = m * self.dim.Hd + r
        s = p // self.q
        return s & 1, ((s ^ me) >> 1, d ^ my), p % self.q


class Halves:
    def __init__(self, dim):
        self.dim = dim
        self.q = dim.Hd // 2
        self.step = math.gcd(self.q, WIDE)
        self.shape = (dim.D, self.q + SMALL, dim.H)

    def place(self, m, d, r, me, my):
        return r // self.q, (d ^ my,), r % self.q


def weight_grad(dim, share, m, ah, al, bh, bl, tile, keep, send):
    for h0 in range(0, dim.H, WIDE):
        tile[...] = dot3(ah[:, h0 : h0 + WIDE], al[:, h0 : h0 + WIDE], bh[...], bl[...], ((0,), (0,)))
        put_rows(dim, share, m, h0, tile, keep, send)


def put_rows(dim, share, m, h0, tile, keep, send):
    me = lax.axis_index("seq")
    my = lax.axis_index("dp")

    def put(mine):
        for r0 in range(0, WIDE, share.step):
            h = h0 + r0
            odd, index, off = share.place(m, h // dim.Hd, h % dim.Hd, me, my)
            dst = keep if odd == mine else send
            dst[(*index, slice(off, off + share.step), slice(None))] = tile[r0 : r0 + share.step, :]

    for mine in range(2):
        pl.when(me & 1 == mine)(functools.partial(put, mine))


class Kept:
    def __init__(self, value):
        self.value = value
        self.shape = value.shape


class Moved:
    def __init__(self, far, near, sem):
        self.far, self.near, self.sem, self.copies = far, near, sem, []

    def fetch(self):
        self.copies.append(pltpu.make_async_copy(self.far, self.near, self.sem.at[0]))
        self.copies[0].start()

    def flush(self, *index):
        sem = self.sem.at[len(self.copies)]
        near, far = (self.near.at[index], self.far.at[index]) if index else (self.near, self.far)
        self.copies.append(pltpu.make_async_copy(near, far, sem))
        self.copies[-1].start()

    def get(self):
        for copy in self.copies:
            copy.wait()
        return self.near


def call(fn, outs, scratch, *args, us=1.0, anywhere=0, late=(), sinks=()):
    scratch = list(scratch)
    first, total = len(args), len(args) + len(outs)
    moved = list(late) + [first + i for i in sinks]
    if moved:
        inner = fn
        for i in moved:
            shape = args[i].shape if i < first else outs[i - first].shape
            scratch += [pltpu.VMEM(shape, F32), pltpu.SemaphoreType.DMA((8,))]

        def fn(*refs):
            refs, spare = list(refs[: -2 * len(moved)]), refs[-2 * len(moved) :]
            for n, i in enumerate(moved):
                refs[i] = Moved(refs[i], *spare[2 * n : 2 * n + 2])
                if i < first:
                    refs[i].fetch()
            inner(*refs)
            for i in moved:
                if i >= first:
                    refs[i].get()

    spaces = [pltpu.HBM if i < anywhere or i in late else pltpu.VMEM for i in range(first)]

    def placed(x, space):
        if isinstance(x, Kept):
            return pltpu.with_memory_space_constraint(x.value, pltpu.VMEM)
        return pltpu.with_memory_space_constraint(x, pltpu.HBM) if space is pltpu.HBM else x

    values = [placed(x, space) for x, space in zip(args, spaces)]
    room = 10 << 20
    for x in scratch:
        if len(x.shape) > 1:
            room += math.prod(x.shape) * (2 if x.dtype == BF16 else 4)
    results = pl.pallas_call(
        fn,
        out_shape=outs,
        in_specs=[pl.BlockSpec(memory_space=space) for space in spaces],
        out_specs=[pl.BlockSpec(memory_space=pl.ANY if i in sinks else pltpu.VMEM) for i in range(len(outs))],
        scratch_shapes=scratch,
        compiler_params=pltpu.CompilerParams(vmem_limit_bytes=max(20 << 20, room)),
        cost_estimate=pl.CostEstimate(flops=1, bytes_accessed=int(us * 3.6e6), transcendentals=0),
    )(*values)
    return [x if isinstance(o, jax.ShapeDtypeStruct) else Kept(x) for x, o in zip(results, outs)]


def f32(*shape):
    return jax.ShapeDtypeStruct(shape, F32)


def halves(dim, n):
    return [pltpu.VMEM((dim.T, dim.H), BF16)] * (2 * n) + [pltpu.VMEM((dim.H, dim.H), BF16)] * 2


def prep_kernel(dim, small, table):
    s = small[...]
    nu, theta, gam = s[5:6, : dim.N], s[5:6, dim.N :], s[6:7, : dim.N]
    rate, angle = jnp.exp(nu), jnp.exp(theta)
    mod = jnp.exp(-rate)
    re, im = mod * jnp.cos(angle), mod * jnp.sin(angle)
    gamma = jnp.exp(gam)

    def put(index, a, b):
        table[index : index + 1, : dim.N] = a
        table[index : index + 1, dim.N :] = b

    table[...] = jnp.zeros((TABLE, dim.H), F32)
    table[:5, :] = s[:5]
    put(GAMMA, gamma, gamma)
    put(LAM, re, im)
    put(RATES, rate, angle)
    power = 1
    while power < dim.L:
        re, im = cmul(re, im, re, im)
        power *= 2
    for index in (LAM1, LAM2, LAM4, LAM8):
        put(index, re, im)
        re, im = cmul(re, im, re, im)


def shard_of(sources, name, rows, H):
    layer, m = name
    return sources[(0, 1, 2, 2)[m]].at[layer, rows, pl.ds(H if m == 3 else 0, H)]


def pack_kernel(dim, in_map, out_map, glu, gain, bias, skip, nu, theta, gamma, glu_bias, *refs):
    outs, held, sem = refs[:3], refs[3:-1], refs[-1]
    vectors = (gain, bias, skip, nu, theta, gamma, glu_bias)
    me, my = lax.axis_index("seq"), lax.axis_index("dp")
    start = pl.multiple_of(jnp.minimum(me, dim.used - 1) * dim.q, 16)
    moves = []
    for src, dst in zip(vectors, held):
        moves.append(pltpu.make_async_copy(src, dst, sem.at[len(moves)]))
    gain, bias, skip, nu, theta, gamma, glu_bias = held
    for out, chunk in zip(outs, CHUNKS):
        head = out.shape[0] - len(chunk) * dim.q
        for i, name in enumerate(chunk):
            src = shard_of((in_map, out_map, glu), name, pl.ds(start, dim.q), dim.H)
            dst = out.at[head + i * dim.q : head + (i + 1) * dim.q, :]
            moves.append(pltpu.make_async_copy(src, dst, sem.at[len(moves)]))
    for move in moves:
        move.start()
    for move in moves[: len(held)]:
        move.wait()

    def spread(ref, layer, width):
        vec = ref[layer : layer + 1, :]
        full = jnp.concatenate([vec] * (width // vec.shape[1]), 1)
        lane = lax.broadcasted_iota(jnp.int32, full.shape, 1)
        return jnp.where(lane // vec.shape[1] == my, full, 0.0)

    for layer in range(dim.layers):
        both = spread(glu_bias, layer, 2 * dim.H)
        rows = [spread(ref, layer, dim.H) for ref in (gain, bias, skip)] + [both[:, : dim.H], both[:, dim.H :]]
        rows.append(jnp.concatenate([spread(nu, layer, dim.N), spread(theta, layer, dim.N)], 1))
        rows.append(jnp.concatenate([spread(gamma, layer, dim.N), jnp.zeros((1, dim.N), F32)], 1))
        for i, value in enumerate(rows):
            outs[layer][i : i + 1, :] = value
        outs[layer][7:8, :] = jnp.zeros((1, dim.H), F32)
    for move in moves[len(held) :]:
        move.wait()


class Weight:
    def __init__(self, dim, name, place, sources, own, buf, sem):
        self.dim, self.name, self.place = dim, name, place
        self.sources, self.own, self.buf, self.sem = sources, own, buf, sem
        self.here = False

    def moves(self):
        shard = shard_of(self.sources, self.name, slice(None), self.dim.H)
        yield pltpu.make_async_copy(shard, self.own, self.sem.at[self.dim.S])
        for k, piece in enumerate(self.sources[3:]):
            yield pltpu.make_async_copy(piece.at[self.place], self.buf.at[k], self.sem.at[k])

    def start(self):
        for move in self.moves():
            move.start()

    def fill(self, wh, wl):
        dim, q = self.dim, self.dim.q
        if not self.here:
            for move in self.moves():
                move.wait()
        self.here = True
        me, my = lax.axis_index("seq"), lax.axis_index("dp")

        def put(start, n, value):
            rows = pl.ds(pl.multiple_of(start, 16), n)
            wh[rows, :], wl[rows, :] = split(value)

        def mine(i, _):
            put(my * dim.Hd + i * 32, 32, self.own[pl.ds(pl.multiple_of(i * 32, 32), 32), :])
            return 0

        lax.fori_loop(0, dim.Hd // 32, mine, 0)

        def one(k, _):
            s = k ^ me

            def block():
                for kz in range(1, dim.D):
                    put((kz ^ my) * dim.Hd + s * q, q, self.buf[k, kz - 1])

            if dim.used < dim.S:
                pl.when(s < dim.used)(block)
            else:
                block()
            return 0

        lax.fori_loop(0, dim.S, one, 0)


def weights_in(dim, chunks, names, fn):
    first = 3 + len(chunks) * dim.S

    def kernel(*refs):
        spare = refs[len(refs) - 3 * len(names) :]
        weights = []
        for i, name in enumerate(names):
            (n,) = [n for n, c in enumerate(chunks) if name in CHUNKS[c]]
            sources = refs[:3] + refs[3 + n * dim.S : 3 + (n + 1) * dim.S]
            place = CHUNKS[chunks[n]].index(name)
            weights.append(Weight(dim, name, place, sources, *spare[3 * i : 3 * i + 3]))
        for w in weights:
            w.start()
        fn(dim, weights, *refs[first : len(refs) - 3 * len(names)])

    scratch = [
        pltpu.VMEM((dim.Hd, dim.H), F32),
        pltpu.VMEM((dim.S, dim.D - 1, dim.q, dim.H), F32),
        pltpu.SemaphoreType.DMA((dim.S + 1,)),
    ] * len(names)
    return kernel, first, scratch


def strided(dim, ref):
    def load(steps, rows):
        if isinstance(steps, list):
            return jnp.concatenate([ref[:, j, :] for j in steps], 0)
        return ref[:, steps, :]

    return load


def plain(ref):
    return lambda j, rows: ref[rows, :]


def k_a0(dim, weights, x, table, xhat, rstd, drive, cf, fin, ah, al, wh, wl):
    front(dim, strided(dim, x), table, weights[0], xhat, rstd, drive, cf, fin, ah, al, wh, wl)


def k_b0(dim, weights, x, t, t1, drive, cf, g, xhat,
         en, states, mixed, active, v, s, act1, xhat1, rstd1, drive1, cf1, fin1, ah, al, wh, wl):
    w_out, w_gv, w_gg, w_in1 = weights
    back(dim, t, drive, cf, g, xhat, w_out, w_gv, w_gg, en, states, mixed, active, v, s, ah, al, wh, wl)
    load = strided(dim, x)

    def residual(steps, rows):
        act = load(steps, rows) + gate(dim, t, v, s, rows)
        act1[rows, :] = act
        return act

    front(dim, residual, t1, w_in1, xhat1, rstd1, drive1, cf1, fin1, ah, al, wh, wl)


def k_b1(dim, weights, act1, out_grad, t, drive, cf, g, xhat,
         out, en, states, active, dv, dg, dmixed, ds, rcf, rfin, sums, ah, al, bh, bl, wh, wl, mixed, v, s):
    w_out, w_gv, w_gg = weights
    back(dim, t, drive, cf, g, xhat, w_out, w_gv, w_gg, en, states, mixed, active, v, s, ah, al, wh, wl)

    def residual(j, rows, _):
        out.near[:, j, :] = act1[rows, :] + gate(dim, t, v, s, rows)
        return 0

    each_step(dim, residual, 2)
    out.flush()
    sums[...] = jnp.zeros((SMALL, dim.H), F32)
    top(dim, t, strided(dim, out_grad), v, s, mixed, xhat, w_gv, w_gg, w_out, dv, dg, dmixed, ds, rcf, rfin, sums,
        ah, al, bh, bl, wh, wl)


def k_w1(dim, share, active, dv, dg, states, dmixed, keep, send, ah, al, bh, bl, tile):
    split_rows(dim, lambda rows: active[rows, :], ah, al)
    for m, ref in ((0, dv), (1, dg)):
        split_rows(dim, lambda rows: ref[rows, :], bh, bl)
        weight_grad(dim, share, m, ah, al, bh, bl, tile, keep, send)
    split_rows(dim, lambda rows: states[rows, :], ah, al)
    split_rows(dim, lambda rows: dmixed[rows, :], bh, bl)
    weight_grad(dim, share, 2, ah, al, bh, bl, tile, keep, send)


def k_w2(dim, share, active, dv, dg, states, dmixed, xhat1, dproj1, t, keep, send, ah, al, bh, bl, tile):
    k_w1(dim, share, active, dv, dg, states, dmixed, keep, send, ah, al, bh, bl, tile)
    split_rows(dim, lambda rows: xhat1[rows, :] * row(t, GAIN) + row(t, BIAS), ah, al)
    split_rows(dim, lambda rows: dproj1[rows, :], bh, bl)
    weight_grad(dim, share, 3, ah, al, bh, bl, tile, keep, send)


def k_c1(dim, weights, out_grad, t, t0, ds, rcf, gr, states, en, drive, xhat, rstd, dmixed,
         xhat0, mixed0, v0, s0,
         dproj, dmid, dv0, dg0, dmixed0, ds0, rcf0, rfin0, sums1, sums0, ah, al, bh, bl, wh, wl, adj_en):
    w_in, w_gv, w_gg, w_out = weights

    def store(j, rows, value):
        dmid[rows, :] = value

    bottom(dim, t, ds, rcf, gr, states, en, drive, xhat, rstd, dmixed, w_in, strided(dim, out_grad), store,
           dproj, ds0, adj_en, sums1, ah, al, wh, wl)
    sums0[...] = jnp.zeros((SMALL, dim.H), F32)
    top(dim, t0, plain(dmid), v0, s0, mixed0, xhat0, w_gv, w_gg, w_out, dv0, dg0, dmixed0, ds0, rcf0, rfin0,
        sums0, ah, al, bh, bl, wh, wl)


def k_c0(share, dim, weights, t, ds, rcf, gr, states, en, drive, xhat, rstd, dmixed, dmid, sums1a, sums1b, sums0a,
         input_grad, keep, send, ah, al, bh, bl, wh, wl, adj_en, dproj, buf, sums0, tile):
    def store(steps, rows, value):
        for u, j in enumerate(steps):
            input_grad.near[:, j, :] = value[u * dim.R : (u + 1) * dim.R, :]

    bottom(dim, t, ds, rcf, gr, states, en, drive, xhat, rstd, dmixed, weights[0], plain(dmid), store, dproj, buf, adj_en,
           sums0, ah, al, wh, wl)
    input_grad.flush()
    split_rows(dim, lambda rows: xhat[rows, :] * row(t, GAIN) + row(t, BIAS), bh, bl)
    weight_grad(dim, share, 0, bh, bl, ah, al, tile, keep, send)
    place = lax.broadcasted_iota(jnp.int32, (SMALL, dim.H), 0)
    upper = (place >= SKIP) & (place <= BIAS_G)
    tile[0:SMALL, :] = jnp.where(upper, sums0a[...], sums0[...])
    tile[SMALL : 2 * SMALL, :] = jnp.where(upper, sums1a[...], sums1b[...])
    me = lax.axis_index("seq")

    def put(mine):
        for layer in range(dim.layers):
            dst = keep if layer == mine else send
            for d in range(dim.D):
                dst[d, share.q :, :] = tile[layer * SMALL : (layer + 1) * SMALL, :]

    for mine in range(2):
        pl.when(me & 1 == mine)(functools.partial(put, mine))


def tie(x, others):
    x, *others = lax.optimization_barrier((x, *others))
    return x, others


def swap(x, axis, mask):
    count = lax.axis_size(axis)
    return lax.ppermute(x, axis, [(i, i ^ mask) for i in range(count)])


def chips_gather(dim, x):
    return [x] + [swap(x, "seq", k) for k in range(2, dim.S, 2)]


def cores_gather(pieces):
    return [p for x in pieces for p in (x, swap(x, "seq", 1))]


def plane_gather(dim, x):
    return cores_gather(chips_gather(dim, x))


def tree_sum(parts):
    while len(parts) > 1:
        parts = [a + b for a, b in zip(parts[::2], parts[1::2])]
    return parts[0]


def half_sums(dim, keep, send):
    got = swap(send, "seq", 1)
    return [keep[k] + got[k] for k in range(dim.S // 2)]


def plane_sums(dim, half):
    others = [swap(half[k], "seq", 2 * k) for k in range(1, dim.S // 2)]
    return [sum((o[k] for o in others), half[0][k]) for k in range(dim.D)]


def split_half(dim, half):
    cut = dim.D // 2
    a, b = [h[:cut] for h in half], [h[cut:] for h in half]
    return [jnp.stack([a[1], a[3]]), jnp.stack([b[2], b[3]]), a[0], a[2], b[0], b[1]]


def two_step_sums(dim, parts):
    send_a, send_b, a0, a2, b0, b1 = parts
    got_a, got_b = swap(send_a, "seq", 2), swap(send_b, "seq", 4)
    far_a, far_b = swap(a2 + got_a[1], "seq", 4), swap(b1 + got_b[1], "seq", 2)
    a, b = a0 + got_a[0] + far_a, b0 + got_b[0] + far_b
    cut = dim.D // 2
    return [a[d] for d in range(cut)] + [b[d] for d in range(dim.D - cut)]


def dp_sum_halving(dim, parts):
    n = dim.D
    while n > 1:
        n //= 2
        got = swap(jnp.stack(parts[n:]), "dp", n)
        parts = [parts[k] + got[k] for k in range(n)]
    return parts[0]


def dp_sum(dim, parts):
    return sum((swap(parts[k], "dp", k) for k in range(1, dim.D)), parts[0])


def unpack_kernel(dim, shares, kinds, last, *refs):
    lower, upper, outs, (mine, other) = refs[: dim.S], refs[dim.S : 2 * dim.S], refs[2 * dim.S : -2], refs[-2:]
    head = last.q + SMALL
    for dst, first in ((mine, 0), (other, 1)):
        dst[...] = tree_sum([lower[k][:head, :] for k in range(first, dim.S, 2)])
    g_gain, g_bias, g_nu, g_theta, g_gamma, g_in, g_out, g_skip, g_glu, g_glu_bias = outs
    me, my = lax.axis_index("seq"), lax.axis_index("dp")

    def place(layer, kind, rows, value):
        if kind == "in":
            g_in[layer, rows, :] = value
        elif kind == "out":
            g_out[layer, rows, :] = value
        elif kind == "gv":
            g_glu[layer, rows, 0 : dim.H] = value
        else:
            g_glu[layer, rows, dim.H : 2 * dim.H] = value

    def put(k, s):
        for share, names, src, base in zip(shares, kinds, (lower[k], upper[k]), (head, 0)):
            for off in range(0, share.q, share.step):
                p = s * share.q + off
                if p // dim.Hd < share.nm:
                    layer, kind = names[p // dim.Hd]
                    r = p % dim.Hd
                    place(layer, kind, slice(r, r + share.step), src[base + off : base + off + share.step, :])

    def vectors(d):
        def own(layer, index, lo, width, out, at=0):
            src = (mine, other)

            def copy(ref):
                start = lo + d * width
                out[layer : layer + 1, :] = ref[last.q + index : last.q + index + 1, start : start + width]

            pl.when(me & 1 == layer)(functools.partial(copy, src[0]))
            pl.when(me & 1 != layer)(functools.partial(copy, src[1]))

        for layer in range(dim.layers):
            for index, out in ((GAIN, g_gain), (BIAS, g_bias), (SKIP, g_skip)):
                own(layer, index, 0, dim.Hd, out)
            n = dim.N // dim.D
            own(layer, 5, 0, n, g_nu)
            own(layer, 5, dim.N, n, g_theta)
            own(layer, 6, 0, n, g_gamma)
            width = 2 * dim.H // dim.D
            index = BIAS_V if d * width < dim.H else BIAS_G
            own(layer, index, 0 if index == BIAS_V else -dim.H, width, g_glu_bias)

    for who in range(dim.S):

        def all_of(who=who):
            for k in range(dim.S):
                put(k, k ^ who)
            half = who & 1
            for ref, part in ((mine, half), (other, 1 - half)):
                place(0, "in", slice(part * last.q, (part + 1) * last.q), ref[: last.q, :])

        pl.when(me == who)(all_of)
    for d in range(dim.D):
        pl.when(my == d)(functools.partial(vectors, d))


def unpack(dim, shares, kinds, last, lower, upper):
    n, l = dim.N // dim.D, dim.layers
    vec, small = f32(l, dim.Hd), f32(l, n)
    mat, wide = f32(l, dim.Hd, dim.H), f32(l, dim.Hd, 2 * dim.H)
    outs = [vec, vec, small, small, small, mat, mat, vec, wide, f32(l, 2 * dim.H // dim.D)]
    return call(functools.partial(unpack_kernel, dim, shares, kinds, last), outs, [pltpu.VMEM((last.q + SMALL, dim.H), F32)] * 2, *lower, *upper)


def body(inputs, out_grad, ln_gain, ln_bias, nu_log, theta_log, gamma_log, in_map, out_map, skip_gain, glu_weight, glu_bias):
    dim = Dims(inputs, in_map, lax.axis_size("dp"), lax.axis_size("seq"))
    T, H, N, R, B, D, S = dim.T, dim.H, dim.N, dim.R, dim.B, dim.D, dim.S
    me, my = lax.axis_index("seq"), lax.axis_index("dp")
    x = inputs.reshape(R, dim.L, H)
    og = out_grad.reshape(R, dim.L, H)

    heads = [SMALL, SMALL, 0]
    vectors = (ln_gain, ln_bias, skip_gain, nu_log, theta_log, gamma_log, glu_bias)
    messages = call(
        functools.partial(pack_kernel, dim),
        [f32(head + len(chunk) * dim.q, H) for head, chunk in zip(heads, CHUNKS)],
        [pltpu.VMEM(v.shape, F32) for v in vectors] + [pltpu.SemaphoreType.DMA((len(vectors) + sum(map(len, CHUNKS)),))],
        in_map, out_map, glu_weight, *vectors,
        anywhere=3 + len(vectors),
    )
    def stacked(others, head):
        return jnp.stack([other[head:].reshape(-1, dim.q, H) for other in others], 1)

    def along_dp(mine):
        return [swap(mine, "dp", k) for k in range(1, D)]

    def table_of(mine, others, head=SMALL):
        total = mine[:head]
        for other in others:
            total = total + other[:head]
        return call(functools.partial(prep_kernel, dim), [f32(TABLE, H)], [], total)[0]

    mine0, mine1, mine2 = messages
    others0 = along_dp(mine0)
    table0 = table_of(mine0, others0)
    mine1, others0 = tie(mine1, others0)
    others1 = along_dp(mine1)
    table1 = table_of(mine1, others1)
    chips0 = chips_gather(dim, stacked(others0, SMALL))
    joined1, chips0 = tie(stacked(others1, SMALL), chips0)
    pieces0 = cores_gather(chips0)
    mine2, (joined1,) = tie(mine2, [joined1])
    chips1 = chips_gather(dim, joined1)
    blocks = mine2[None]
    while blocks.shape[0] < D:
        blocks = jnp.concatenate([blocks, swap(blocks, "dp", blocks.shape[0])], 0)
    joined2 = stacked([blocks[k] for k in range(1, D)], 0)
    pieces = [pieces0, cores_gather(chips1), None]

    big, ent, fins = pltpu.VMEM((T, H), F32), pltpu.VMEM((R, H), F32), f32(B, H)
    stat = pltpu.VMEM((T, 128), F32)
    vec = pltpu.VMEM((SMALL, H), F32)

    def k(fn, names, outs, scratch, *args, us, late=(), sinks=()):
        chunks = [c for c, chunk in enumerate(CHUNKS) if set(chunk) & set(names)]
        kernel, count, own = weights_in(dim, chunks, names, fn)
        sources = [in_map, out_map, glu_weight] + [p for c in chunks for p in pieces[c]]
        late = [count + i for i in late]
        return call(kernel, outs, scratch + own, *sources, *args, us=us, anywhere=count, late=late, sinks=sinks)

    def carried(fin):
        return lax.all_gather(fin, "seq")

    xhat0, rstd0, drive0, cf0, fin0 = k(
        k_a0, [(0, 0)], [big, stat, big, ent, fins], halves(dim, 1), x, table0, us=3.4
    )
    g0 = carried(fin0)
    joined2, (g0,) = tie(joined2, [g0])
    chips2 = chips_gather(dim, joined2)
    en0, states0, mixed0, active0, v0, s0, act1, xhat1, rstd1, drive1, cf1, fin1 = k(
        k_b0,
        [(0, 1), (0, 2), (0, 3), (1, 0)],
        [ent, big, big, big, big, big, big, big, stat, big, ent, fins],
        halves(dim, 1),
        x, table0, table1, drive0, cf0, g0, xhat0,
        us=9.0,
    )
    fin1, chips2 = tie(fin1, chips2)
    g1 = carried(fin1)
    pieces[2] = cores_gather(chips2)
    spare = [pltpu.VMEM((T, H), F32)]
    out, en1, states1, active1, dv1, dg1, dmixed1, ds1, rcf1, rfin1, sums1a = k(
        k_b1,
        [(1, 1), (1, 2), (1, 3)],
        [f32(R, dim.L, H), ent, big, big, big, big, big, big, ent, fins, vec],
        halves(dim, 2) + spare * 3,
        act1, og, table1, drive1, cf1, g1, xhat1,
        us=12.5, sinks=[0],
    )
    share1, share2, share3 = Share(dim, 3), Share(dim, 4), Halves(dim)
    tile = [pltpu.VMEM((WIDE, H), F32)]
    pair = [pltpu.VMEM((T, H), BF16)] * 4
    keep1, send1 = call(
        functools.partial(k_w1, dim, share1), [f32(*share1.shape)] * 2, pair + tile,
        active1, dv1, dg1, states1, dmixed1, us=5.0,
    )
    rfin1, (send1,) = tie(rfin1, [send1])
    gr1 = carried(rfin1)
    gr1, half1 = tie(gr1, half_sums(dim, keep1, send1))
    dproj1, dmid, dv0, dg0, dmixed0, ds0, rcf0, rfin0, sums1b, sums0a = k(
        k_c1,
        [(1, 0), (0, 2), (0, 3), (0, 1)],
        [big, big, big, big, big, big, ent, fins, vec, vec],
        halves(dim, 2) + [pltpu.VMEM((R, H), F32)],
        og, table1, table0, ds1, rcf1, gr1, states1, en1, drive1, xhat1, rstd1, dmixed1,
        xhat0, mixed0, v0, s0,
        us=9.5,
    )
    keep2, send2 = call(
        functools.partial(k_w2, dim, share2), [f32(*share2.shape)] * 2, pair + tile,
        active0, dv0, dg0, states0, dmixed0, xhat1, dproj1, table1, us=6.4,
    )
    rfin0, (send2, *sums1) = tie(rfin0, [send2, *plane_sums(dim, half1)])
    gr0 = carried(rfin0)
    half2 = half_sums(dim, keep2, send2)
    two_steps = S == 8
    gr0, half2 = tie(gr0, split_half(dim, half2) if two_steps else half2)
    input_grad, keep3, send3 = k(
        functools.partial(k_c0, share3),
        [(0, 0)],
        [f32(R, dim.L, H)] + [f32(*share3.shape)] * 2,
        halves(dim, 2) + [pltpu.VMEM((R, H), F32)] + spare * 2 + [pltpu.VMEM((SMALL, H), F32)] + tile,
        table0, ds0, rcf0, gr0, states0, en0, drive0, xhat0, rstd0, dmixed0, dmid, sums1a, sums1b, sums0a,
        us=6.0, sinks=[0],
    )
    sums2 = two_step_sums(dim, half2) if two_steps else plane_sums(dim, half2)
    got3 = swap(send3, "seq", 1)
    half3 = [keep3[d] + got3[d] for d in range(D)]
    total3 = tree_sum([half3[0]] + [swap(half3[k], "dp", k) for k in range(1, D)])
    upper1 = dp_sum(dim, sums1)
    chips3 = chips_gather(dim, jnp.concatenate([total3, upper1], 0))
    last = cores_gather(chips3)
    upper = plane_gather(dim, dp_sum(dim, sums2))
    kinds = [[(1, "gv"), (1, "gg"), (1, "out")], [(0, "gv"), (0, "gg"), (0, "out"), (1, "in")]]
    grads = unpack(dim, (share1, share2), kinds, share3, last, upper)
    return (out.reshape(inputs.shape), input_grad.reshape(inputs.shape), *grads)


def solution(mesh):
    act, vec, mat = P("dp", "seq", None), P(None, "dp"), P(None, "dp", None)
    in_specs = (act, act, vec, vec, vec, vec, vec, mat, mat, vec, mat, vec)
    out_specs = (act, act, vec, vec, vec, vec, vec, mat, mat, vec, mat, vec)
    return jax.shard_map(body, mesh=mesh, in_specs=in_specs, out_specs=out_specs, check_vma=False)
```

```python
import functools
import math

import jax
import jax.numpy as jnp
from jax import lax
from jax.experimental import pallas as pl
from jax.experimental.pallas import tpu as pltpu
from jax.sharding import PartitionSpec as P

NORM_EPS = 1e-05
GROUPS = 8
WIDE = 256
SMALL = 8
TABLE = 16
F32 = jnp.float32
BF16 = jnp.bfloat16
GELU_C = math.sqrt(2.0 / math.pi)

GAIN, BIAS, SKIP, BIAS_V, BIAS_G, GAMMA, LAM, LAM1, LAM2, LAM4, LAM8, RATES = range(12)


CHUNKS = (((0, 0), (1, 0)), ((0, 1), (0, 2), (0, 3)), ((1, 1), (1, 2), (1, 3)))


class Dims:
    def __init__(self, inputs, in_map, dp, seq):
        self.B, self.Tb, self.H = inputs.shape
        self.layers, self.Hd = in_map.shape[:2]
        self.N = self.H // 2
        self.T = self.B * self.Tb
        self.R = self.B * GROUPS
        self.L = self.Tb // GROUPS
        self.D, self.S = dp, seq
        self.q = max(16, self.Hd // seq)
        self.used = self.Hd // self.q


def cmul(ar, ai, br, bi):
    return ar * br - ai * bi, ar * bi + ai * br


def split(x):
    hi = x.astype(BF16)
    return hi, (x - hi.astype(F32)).astype(BF16)


def dot3(ah, al, bh, bl, dims):
    def one(a, b):
        return lax.dot_general(a, b, (dims, ((), ())), preferred_element_type=F32)

    return one(ah, bh) + (one(ah, bl) + one(al, bh))


def product(ah, al, wh, wl, dst, transposed=False, add=False):
    for n in range(dst.shape[1] // WIDE):
        cols = slice(n * WIDE, (n + 1) * WIDE)
        if transposed:
            res = dot3(ah[...], al[...], wh[cols, :], wl[cols, :], ((1,), (1,)))
        else:
            res = dot3(ah[...], al[...], wh[:, cols], wl[:, cols], ((1,), (0,)))
        dst[:, cols] = dst[:, cols] + res if add else res


def each_step(dim, fn, unroll=2, reverse=False, init=0):
    def one(i, carry):
        j = dim.L - 1 - i if reverse else i
        rows = pl.ds(pl.multiple_of(j * dim.R, dim.R), dim.R)
        return fn(j, rows, carry)

    return lax.fori_loop(0, dim.L, one, init, unroll=unroll)


def each_span(dim, fn, init=0, steps=8):
    def one(i, carry):
        rows = pl.ds(pl.multiple_of(i * steps * dim.R, steps * dim.R), steps * dim.R)
        return fn([i * steps + u for u in range(steps)], rows, carry)

    return lax.fori_loop(0, dim.L // steps, one, init)


def fold(x):
    return jnp.sum(x.reshape(x.shape[0] // 8, 8, x.shape[1]), 0)


def row(table, index, n=1):
    return table[index : index + n, :]


def lam_of(dim, table, index, reverse):
    pair = table[index : index + 1, :]
    real, imag = pair[:, : dim.N], pair[:, dim.N :]
    return real, -imag if reverse else imag


def chunk_scan(dim, table, yr, yi, reverse):
    place = lax.broadcasted_iota(jnp.int32, yr.shape, 0)
    for dist, index in ((1, LAM1), (2, LAM2), (4, LAM4)):
        pr, pi = lam_of(dim, table, index, reverse)
        if reverse:
            shift, seen = GROUPS - dist, place < GROUPS - dist
        else:
            shift, seen = dist, place >= dist
        sr = jnp.where(seen, pltpu.roll(yr, shift, 0), 0.0)
        si = jnp.where(seen, pltpu.roll(yi, shift, 0), 0.0)
        mr, mi = cmul(pr, pi, sr, si)
        yr, yi = yr + mr, yi + mi
    return yr, yi


def local_finals(dim, table, drive_ref, cf_ref, f_ref, reverse):
    lr, li = lam_of(dim, table, LAM, reverse)
    lr = jnp.broadcast_to(lr, (dim.R, dim.N))
    li = jnp.broadcast_to(li, (dim.R, dim.N))

    def step(j, rows, carry):
        d = drive_ref[rows, :]
        mr, mi = cmul(lr, li, *carry)
        return mr + d[:, : dim.N], mi + d[:, dim.N :]

    zero = jnp.zeros((dim.R, dim.N), F32)
    fr, fi = each_step(dim, step, 4, reverse, (zero, zero))
    cf_ref[:, : dim.N] = fr
    cf_ref[:, dim.N :] = fi
    last = 0 if reverse else GROUPS - 1
    for b in range(dim.B):
        rows = slice(b * GROUPS, (b + 1) * GROUPS)
        yr, yi = chunk_scan(dim, table, fr[rows], fi[rows], reverse)
        f_ref[b : b + 1, : dim.N] = yr[last : last + 1]
        f_ref[b : b + 1, dim.N :] = yi[last : last + 1]


def entries_of(dim, table, cf_ref, g_ref, en_ref, reverse):
    me = lax.axis_index("seq")
    lr, li = lam_of(dim, table, LAM8, reverse)
    xr = jnp.zeros((dim.B, dim.N), F32)
    xi = xr
    order = reversed(range(dim.S)) if reverse else range(dim.S)
    for other in order:
        ahead = other > me if reverse else other < me
        g = g_ref[other]
        mr, mi = cmul(lr, li, xr, xi)
        xr = jnp.where(ahead, mr + g[:, : dim.N], xr)
        xi = jnp.where(ahead, mi + g[:, dim.N :], xi)
    for b in range(dim.B):
        rows = slice(b * GROUPS, (b + 1) * GROUPS)
        f = cf_ref[rows, :]
        place = lax.broadcasted_iota(jnp.int32, f.shape, 0)
        x = jnp.concatenate([xr[b : b + 1], xi[b : b + 1]], 1)
        if reverse:
            y = jnp.where(place == GROUPS - 1, x, pltpu.roll(f, GROUPS - 1, 0))
        else:
            y = jnp.where(place == 0, x, pltpu.roll(f, 1, 0))
        yr, yi = chunk_scan(dim, table, y[:, : dim.N], y[:, dim.N :], reverse)
        en_ref[rows, : dim.N] = yr
        en_ref[rows, dim.N :] = yi


def norm_step(dim, x, table):
    mean = jnp.mean(x, -1, keepdims=True)
    centred = x - mean
    var = jnp.mean(centred * centred, -1, keepdims=True)
    rstd = lax.rsqrt(var + NORM_EPS)
    xhat = centred * rstd
    return xhat, rstd, xhat * row(table, GAIN) + row(table, BIAS)


def front(dim, load_act, table, w_in, xhat, rstd, drive, cf, fin, ah, al, wh, wl):
    def norm(steps, rows, _):
        xh, rs, normed = norm_step(dim, load_act(steps, rows), table)
        xhat[rows, :] = xh
        rstd[rows, :] = jnp.broadcast_to(rs, (rs.shape[0], 128))
        ah[rows, :], al[rows, :] = split(normed)
        return 0

    each_span(dim, norm)
    w_in.fill(wh, wl)
    product(ah, al, wh, wl, drive)

    def scale(j, rows, _):
        drive[rows, :] = drive[rows, :] * row(table, GAMMA)
        return 0

    each_step(dim, scale, 4)
    local_finals(dim, table, drive, cf, fin, False)


def gelu_parts(m):
    inner = GELU_C * (m + 0.044715 * (m * m * m))
    th = jnp.tanh(inner)
    return th


def back(dim, table, drive, cf, g, xhat, w_out, w_gv, w_gg, en, states, mixed, v, s, sh, sl, ch, cl, wh, wl):
    entries_of(dim, table, cf, g, en, False)
    lr, li = lam_of(dim, table, LAM, False)
    lr = jnp.broadcast_to(lr, (dim.R, dim.N))
    li = jnp.broadcast_to(li, (dim.R, dim.N))

    def scan(j, rows, carry):
        d = drive[rows, :]
        mr, mi = cmul(lr, li, *carry)
        both = jnp.concatenate([mr + d[:, : dim.N], mi + d[:, dim.N :]], 1)
        states[rows, :] = both
        sh[rows, :], sl[rows, :] = split(both)
        return both[:, : dim.N], both[:, dim.N :]

    each_step(dim, scan, 4, False, (en[:, : dim.N], en[:, dim.N :]))
    w_out.fill(wh, wl)
    product(sh, sl, wh, wl, mixed)

    def gelu(j, rows, _):
        normed = xhat[rows, :] * row(table, GAIN) + row(table, BIAS)
        m = mixed[rows, :] + row(table, SKIP) * normed
        mixed[rows, :] = m
        a = (0.5 * m) * (1.0 + gelu_parts(m))
        ch[rows, :], cl[rows, :] = split(a)
        return 0

    each_step(dim, gelu, 4)
    w_gv.fill(wh, wl)
    product(ch, cl, wh, wl, v)
    w_gg.fill(wh, wl)
    product(ch, cl, wh, wl, s)


def gate(dim, table, v, s, rows):
    vv = v[rows, :] + row(table, BIAS_V)
    ss = jax.nn.sigmoid(s[rows, :] + row(table, BIAS_G))
    v[rows, :] = vv
    s[rows, :] = ss
    return vv * ss


def top(dim, table, load_dact, v, s, mixed, xhat, w_gv, w_gg, w_out, dmixed, ds, rcf, rfin, sums, ah, al, bh, bl, mh, ml, wh, wl):
    def dgate(j, rows, carry):
        dact = load_dact(j, rows)
        ss, vv = s[rows, :], v[rows, :]
        a = dact * ss
        b = a * vv * (1.0 - ss)
        ah[rows, :], al[rows, :] = split(a)
        bh[rows, :], bl[rows, :] = split(b)
        return carry[0] + a, carry[1] + b

    zero = jnp.zeros((dim.R, dim.H), F32)
    sv, sg = each_step(dim, dgate, 2, False, (zero, zero))
    sums[BIAS_V : BIAS_V + 1, :] = jnp.sum(sv, 0, keepdims=True)
    sums[BIAS_G : BIAS_G + 1, :] = jnp.sum(sg, 0, keepdims=True)
    w_gv.fill(wh, wl)
    product(ah, al, wh, wl, dmixed, True)
    w_gg.fill(wh, wl)
    product(bh, bl, wh, wl, dmixed, True, True)

    def dgelu(j, rows, carry):
        m = mixed[rows, :]
        th = gelu_parts(m)
        slope = 0.5 * (1.0 + th) + (0.5 * m) * (1.0 - th * th) * (GELU_C * (1.0 + (3 * 0.044715) * (m * m)))
        d = dmixed[rows, :] * slope
        dmixed[rows, :] = d
        mh[rows, :], ml[rows, :] = split(d)
        normed = xhat[rows, :] * row(table, GAIN) + row(table, BIAS)
        return carry + d * normed

    sums[SKIP : SKIP + 1, :] = jnp.sum(each_step(dim, dgelu, 2, False, zero), 0, keepdims=True)
    w_out.fill(wh, wl)
    product(mh, ml, wh, wl, ds, True)
    local_finals(dim, table, ds, rcf, rfin, True)


def bottom(dim, table, ds, rcf, gr, states, en, drive, xhat, rstd, dmixed, w_in, load_dact, store, buf, adj_en, sums, ah, al, wh, wl):
    entries_of(dim, table, rcf, gr, adj_en, True)
    lr, li = lam_of(dim, table, LAM, True)
    lr = jnp.broadcast_to(lr, (dim.R, dim.N))
    li = jnp.broadcast_to(li, (dim.R, dim.N))
    zero = jnp.zeros((dim.R, dim.N), F32)

    def scan(j, rows, carry):
        ar, ai, dr, di, dgam = carry
        d = ds[rows, :]
        mr, mi = cmul(lr, li, ar, ai)
        ar, ai = mr + d[:, : dim.N], mi + d[:, dim.N :]
        earlier = pl.ds(pl.multiple_of(jnp.maximum(j - 1, 0) * dim.R, dim.R), dim.R)
        before = jnp.where(j == 0, en[...], states[earlier, :])
        br, bi = before[:, : dim.N], before[:, dim.N :]
        dr = dr + (ar * br + ai * bi)
        di = di + (ai * br - ar * bi)
        u = drive[rows, :]
        dgam = dgam + (ar * u[:, : dim.N] + ai * u[:, dim.N :])
        dp = jnp.concatenate([ar, ai], 1) * row(table, GAMMA)
        ah[rows, :], al[rows, :] = split(dp)
        return ar, ai, dr, di, dgam

    start = (adj_en[:, : dim.N], adj_en[:, dim.N :], zero, zero, zero)
    _, _, dr, di, dgam = each_step(dim, scan, 2, True, start)
    dr, di, dgam = (jnp.sum(x, 0, keepdims=True) for x in (dr, di, dgam))
    fr, fi = lam_of(dim, table, LAM, False)
    rates = row(table, RATES)
    rate, angle = rates[:, : dim.N], rates[:, dim.N :]
    sums[5:6, : dim.N] = -rate * (dr * fr + di * fi)
    sums[5:6, dim.N :] = angle * (di * fr - dr * fi)
    sums[6:7, : dim.N] = dgam
    sums[6:7, dim.N :] = jnp.zeros_like(dgam)
    sums[7:8, :] = jnp.zeros((1, dim.H), F32)

    w_in.fill(wh, wl)
    product(ah, al, wh, wl, buf, True)
    wide = jnp.zeros((8, dim.H), F32)

    def dnorm(steps, rows, carry):
        dn = buf[rows, :] + dmixed[rows, :] * row(table, SKIP)
        xh = xhat[rows, :]
        dx = dn * row(table, GAIN)
        m1 = jnp.mean(dx, -1, keepdims=True)
        m2 = jnp.mean(dx * xh, -1, keepdims=True)
        store(steps, rows, load_dact(steps, rows) + rstd[rows, 0:1] * (dx - m1 - xh * m2))
        return carry[0] + fold(dn * xh), carry[1] + fold(dn)

    sgain, sbias = each_span(dim, dnorm, (wide, wide))
    sums[GAIN : GAIN + 1, :] = jnp.sum(sgain, 0, keepdims=True)
    sums[BIAS : BIAS + 1, :] = jnp.sum(sbias, 0, keepdims=True)


def split_rows(dim, load, xh, xl):
    def one(j, rows, _):
        xh[rows, :], xl[rows, :] = split(load(rows))
        return 0

    each_step(dim, one, 4)


class Share:
    def __init__(self, dim, nm):
        self.dim, self.nm = dim, nm
        self.q = -(-nm * dim.Hd // (8 * dim.S)) * 8
        self.step = math.gcd(self.q, dim.Hd)
        self.shape = (dim.S // 2, dim.D, self.q, dim.H)

    def place(self, m, d, r, me, my):
        p = m * self.dim.Hd + r
        s = p // self.q
        return s & 1, ((s ^ me) >> 1, d ^ my), p % self.q


class Halves:
    def __init__(self, dim):
        self.dim = dim
        self.q = dim.Hd // 2
        self.step = math.gcd(self.q, WIDE)
        self.shape = (dim.D, self.q + SMALL, dim.H)

    def place(self, m, d, r, me, my):
        return r // self.q, (d ^ my,), r % self.q


def weight_grad(dim, share, m, ah, al, bh, bl, tile, keep, send):
    for h0 in range(0, dim.H, WIDE):
        tile[...] = dot3(ah[:, h0 : h0 + WIDE], al[:, h0 : h0 + WIDE], bh[...], bl[...], ((0,), (0,)))
        put_rows(dim, share, m, h0, tile, keep, send)


def put_rows(dim, share, m, h0, tile, keep, send):
    me = lax.axis_index("seq")
    my = lax.axis_index("dp")

    def put(mine):
        for r0 in range(0, WIDE, share.step):
            h = h0 + r0
            odd, index, off = share.place(m, h // dim.Hd, h % dim.Hd, me, my)
            dst = keep if odd == mine else send
            dst[(*index, slice(off, off + share.step), slice(None))] = tile[r0 : r0 + share.step, :]

    for mine in range(2):
        pl.when(me & 1 == mine)(functools.partial(put, mine))


class Kept:
    def __init__(self, value):
        self.value = value
        self.shape = value.shape


class Moved:
    def __init__(self, far, near, sem):
        self.far, self.near, self.sem, self.copies = far, near, sem, []

    def fetch(self):
        self.copies.append(pltpu.make_async_copy(self.far, self.near, self.sem.at[0]))
        self.copies[0].start()

    def flush(self, *index):
        sem = self.sem.at[len(self.copies)]
        near, far = (self.near.at[index], self.far.at[index]) if index else (self.near, self.far)
        self.copies.append(pltpu.make_async_copy(near, far, sem))
        self.copies[-1].start()

    def get(self):
        for copy in self.copies:
            copy.wait()
        return self.near


def call(fn, outs, scratch, *args, us=1.0, anywhere=0, late=(), sinks=()):
    scratch = list(scratch)
    first, total = len(args), len(args) + len(outs)
    moved = list(late) + [first + i for i in sinks]
    if moved:
        inner = fn
        for i in moved:
            shape = args[i].shape if i < first else outs[i - first].shape
            scratch += [pltpu.VMEM(shape, F32), pltpu.SemaphoreType.DMA((8,))]

        def fn(*refs):
            refs, spare = list(refs[: -2 * len(moved)]), refs[-2 * len(moved) :]
            for n, i in enumerate(moved):
                refs[i] = Moved(refs[i], *spare[2 * n : 2 * n + 2])
                if i < first:
                    refs[i].fetch()
            inner(*refs)
            for i in moved:
                if i >= first:
                    refs[i].get()

    spaces = [pltpu.HBM if i < anywhere or i in late else pltpu.VMEM for i in range(first)]

    def placed(x, space):
        if isinstance(x, Kept):
            return pltpu.with_memory_space_constraint(x.value, pltpu.VMEM)
        return pltpu.with_memory_space_constraint(x, pltpu.HBM) if space is pltpu.HBM else x

    values = [placed(x, space) for x, space in zip(args, spaces)]
    room = 10 << 20
    for x in scratch:
        if len(x.shape) > 1:
            room += math.prod(x.shape) * (2 if x.dtype == BF16 else 4)
    results = pl.pallas_call(
        fn,
        out_shape=outs,
        in_specs=[pl.BlockSpec(memory_space=space) for space in spaces],
        out_specs=[pl.BlockSpec(memory_space=pl.ANY if i in sinks else pltpu.VMEM) for i in range(len(outs))],
        scratch_shapes=scratch,
        compiler_params=pltpu.CompilerParams(vmem_limit_bytes=max(20 << 20, room)),
        cost_estimate=pl.CostEstimate(flops=1, bytes_accessed=int(us * 3.6e6), transcendentals=0),
    )(*values)
    return [x if isinstance(o, jax.ShapeDtypeStruct) else Kept(x) for x, o in zip(results, outs)]


def f32(*shape):
    return jax.ShapeDtypeStruct(shape, F32)


def prep_kernel(dim, small, table):
    s = small[...]
    nu, theta, gam = s[5:6, : dim.N], s[5:6, dim.N :], s[6:7, : dim.N]
    rate, angle = jnp.exp(nu), jnp.exp(theta)
    mod = jnp.exp(-rate)
    re, im = mod * jnp.cos(angle), mod * jnp.sin(angle)
    gamma = jnp.exp(gam)

    def put(index, a, b):
        table[index : index + 1, : dim.N] = a
        table[index : index + 1, dim.N :] = b

    table[...] = jnp.zeros((TABLE, dim.H), F32)
    table[:5, :] = s[:5]
    put(GAMMA, gamma, gamma)
    put(LAM, re, im)
    put(RATES, rate, angle)
    power = 1
    while power < dim.L:
        re, im = cmul(re, im, re, im)
        power *= 2
    for index in (LAM1, LAM2, LAM4, LAM8):
        put(index, re, im)
        re, im = cmul(re, im, re, im)


def shard_of(sources, name, rows, H):
    layer, m = name
    return sources[(0, 1, 2, 2)[m]].at[layer, rows, pl.ds(H if m == 3 else 0, H)]


def pack_kernel(dim, in_map, out_map, glu, gain, bias, skip, nu, theta, gamma, glu_bias, *refs):
    outs, held, sem = refs[:3], refs[3:-1], refs[-1]
    vectors = (gain, bias, skip, nu, theta, gamma, glu_bias)
    me, my = lax.axis_index("seq"), lax.axis_index("dp")
    start = pl.multiple_of(jnp.minimum(me, dim.used - 1) * dim.q, 16)
    moves = []
    for src, dst in zip(vectors, held):
        moves.append(pltpu.make_async_copy(src, dst, sem.at[len(moves)]))
    gain, bias, skip, nu, theta, gamma, glu_bias = held
    for out, chunk in zip(outs, CHUNKS):
        head = out.shape[0] - len(chunk) * dim.q
        for i, name in enumerate(chunk):
            src = shard_of((in_map, out_map, glu), name, pl.ds(start, dim.q), dim.H)
            dst = out.at[head + i * dim.q : head + (i + 1) * dim.q, :]
            moves.append(pltpu.make_async_copy(src, dst, sem.at[len(moves)]))
    for move in moves:
        move.start()
    for move in moves[: len(held)]:
        move.wait()

    def spread(ref, layer, width):
        vec = ref[layer : layer + 1, :]
        full = jnp.concatenate([vec] * (width // vec.shape[1]), 1)
        lane = lax.broadcasted_iota(jnp.int32, full.shape, 1)
        return jnp.where(lane // vec.shape[1] == my, full, 0.0)

    for layer in range(dim.layers):
        both = spread(glu_bias, layer, 2 * dim.H)
        rows = [spread(ref, layer, dim.H) for ref in (gain, bias, skip)] + [both[:, : dim.H], both[:, dim.H :]]
        rows.append(jnp.concatenate([spread(nu, layer, dim.N), spread(theta, layer, dim.N)], 1))
        rows.append(jnp.concatenate([spread(gamma, layer, dim.N), jnp.zeros((1, dim.N), F32)], 1))
        for i, value in enumerate(rows):
            outs[layer][i : i + 1, :] = value
        outs[layer][7:8, :] = jnp.zeros((1, dim.H), F32)
    for move in moves[len(held) :]:
        move.wait()


class Weight:
    def __init__(self, dim, name, place, sources, own, buf, sem):
        self.dim, self.name, self.place = dim, name, place
        self.sources, self.own, self.buf, self.sem = sources, own, buf, sem
        self.here = False

    def moves(self):
        shard = shard_of(self.sources, self.name, slice(None), self.dim.H)
        yield pltpu.make_async_copy(shard, self.own, self.sem.at[self.dim.S])
        for k, piece in enumerate(self.sources[3:]):
            yield pltpu.make_async_copy(piece.at[self.place], self.buf.at[k], self.sem.at[k])

    def start(self):
        for move in self.moves():
            move.start()

    def fill(self, wh, wl):
        dim, q = self.dim, self.dim.q
        if not self.here:
            for move in self.moves():
                move.wait()
        self.here = True
        me, my = lax.axis_index("seq"), lax.axis_index("dp")

        def put(start, n, value):
            rows = pl.ds(pl.multiple_of(start, 16), n)
            wh[rows, :], wl[rows, :] = split(value)

        def mine(i, _):
            put(my * dim.Hd + i * 32, 32, self.own[pl.ds(pl.multiple_of(i * 32, 32), 32), :])
            return 0

        lax.fori_loop(0, dim.Hd // 32, mine, 0)

        def one(k, _):
            s = k ^ me

            def block():
                for kz in range(1, dim.D):
                    put((kz ^ my) * dim.Hd + s * q, q, self.buf[k, kz - 1])

            if dim.used < dim.S:
                pl.when(s < dim.used)(block)
            else:
                block()
            return 0

        lax.fori_loop(0, dim.S, one, 0)


def weights_in(dim, chunks, names, fn):
    first = 3 + len(chunks) * dim.S

    def kernel(*refs):
        spare = refs[len(refs) - 3 * len(names) :]
        weights = []
        for i, name in enumerate(names):
            (n,) = [n for n, c in enumerate(chunks) if name in CHUNKS[c]]
            sources = refs[:3] + refs[3 + n * dim.S : 3 + (n + 1) * dim.S]
            place = CHUNKS[chunks[n]].index(name)
            weights.append(Weight(dim, name, place, sources, *spare[3 * i : 3 * i + 3]))
        for w in weights:
            w.start()
        fn(dim, weights, *refs[first : len(refs) - 3 * len(names)])

    scratch = [
        pltpu.VMEM((dim.Hd, dim.H), F32),
        pltpu.VMEM((dim.S, dim.D - 1, dim.q, dim.H), F32),
        pltpu.SemaphoreType.DMA((dim.S + 1,)),
    ] * len(names)
    return kernel, first, scratch


def strided(dim, ref):
    def load(steps, rows):
        if isinstance(steps, list):
            return jnp.concatenate([ref[:, j, :] for j in steps], 0)
        return ref[:, steps, :]

    return load


def plain(ref):
    return lambda j, rows: ref[rows, :]


def k_a0(dim, weights, x, table, xhat, rstd, drive, cf, fin, nh, nl, wh, wl):
    front(dim, strided(dim, x), table, weights[0], xhat, rstd, drive, cf, fin, nh, nl, wh, wl)


def k_b0(dim, weights, x, t, t1, drive, cf, g, xhat,
         en, states, mixed, v, s, sh, sl, ch, cl, act1, xhat1, rstd1, drive1, cf1, fin1, nh, nl, wh, wl):
    w_out, w_gv, w_gg, w_in1 = weights
    back(dim, t, drive, cf, g, xhat, w_out, w_gv, w_gg, en, states, mixed, v, s, sh, sl, ch, cl, wh, wl)
    load = strided(dim, x)

    def residual(steps, rows):
        act = load(steps, rows) + gate(dim, t, v, s, rows)
        act1[rows, :] = act
        return act

    front(dim, residual, t1, w_in1, xhat1, rstd1, drive1, cf1, fin1, nh, nl, wh, wl)


def k_b1(dim, weights, act1, out_grad, t, drive, cf, g, xhat,
         out, en, states, dmixed, ds, rcf, rfin, sums, sh, sl, ch, cl, dvh, dvl, dgh, dgl, mh, ml, wh, wl, mixed, v, s):
    w_out, w_gv, w_gg = weights
    back(dim, t, drive, cf, g, xhat, w_out, w_gv, w_gg, en, states, mixed, v, s, sh, sl, ch, cl, wh, wl)

    def residual(j, rows, _):
        out.near[:, j, :] = act1[rows, :] + gate(dim, t, v, s, rows)
        return 0

    each_step(dim, residual, 2)
    out.flush()
    sums[...] = jnp.zeros((SMALL, dim.H), F32)
    top(dim, t, strided(dim, out_grad), v, s, mixed, xhat, w_gv, w_gg, w_out, dmixed, ds, rcf, rfin, sums,
        dvh, dvl, dgh, dgl, mh, ml, wh, wl)


def k_w1(dim, share, ch, cl, dvh, dvl, dgh, dgl, sh, sl, mh, ml, keep, send, tile):
    for m, (ah, al, bh, bl) in enumerate(((ch, cl, dvh, dvl), (ch, cl, dgh, dgl), (sh, sl, mh, ml))):
        weight_grad(dim, share, m, ah, al, bh, bl, tile, keep, send)


def k_w2(dim, share, ch, cl, dvh, dvl, dgh, dgl, sh, sl, mh, ml, nh, nl, dph, dpl, keep, send, tile):
    k_w1(dim, share, ch, cl, dvh, dvl, dgh, dgl, sh, sl, mh, ml, keep, send, tile)
    weight_grad(dim, share, 3, nh, nl, dph, dpl, tile, keep, send)


def k_c1(dim, weights, out_grad, t, t0, ds, rcf, gr, states, en, drive, xhat, rstd, dmixed,
         xhat0, mixed0, v0, s0,
         dmid, dmixed0, ds0, rcf0, rfin0, sums1, sums0, dph, dpl, dvh, dvl, dgh, dgl, mh, ml, wh, wl, adj_en):
    w_in, w_gv, w_gg, w_out = weights

    def store(j, rows, value):
        dmid[rows, :] = value

    bottom(dim, t, ds, rcf, gr, states, en, drive, xhat, rstd, dmixed, w_in, strided(dim, out_grad), store,
           ds0, adj_en, sums1, dph, dpl, wh, wl)
    sums0[...] = jnp.zeros((SMALL, dim.H), F32)
    top(dim, t0, plain(dmid), v0, s0, mixed0, xhat0, w_gv, w_gg, w_out, dmixed0, ds0, rcf0, rfin0,
        sums0, dvh, dvl, dgh, dgl, mh, ml, wh, wl)


def k_c0(share, dim, weights, t, ds, rcf, gr, states, en, drive, xhat, rstd, dmixed, dmid, sums1a, sums1b, sums0a, nh, nl,
         input_grad, keep, send, ah, al, wh, wl, adj_en, buf, sums0, tile):
    def store(steps, rows, value):
        for u, j in enumerate(steps):
            input_grad.near[:, j, :] = value[u * dim.R : (u + 1) * dim.R, :]

    bottom(dim, t, ds, rcf, gr, states, en, drive, xhat, rstd, dmixed, weights[0], plain(dmid), store, buf, adj_en,
           sums0, ah, al, wh, wl)
    input_grad.flush()
    weight_grad(dim, share, 0, nh, nl, ah, al, tile, keep, send)
    place = lax.broadcasted_iota(jnp.int32, (SMALL, dim.H), 0)
    upper = (place >= SKIP) & (place <= BIAS_G)
    tile[0:SMALL, :] = jnp.where(upper, sums0a[...], sums0[...])
    tile[SMALL : 2 * SMALL, :] = jnp.where(upper, sums1a[...], sums1b[...])
    me = lax.axis_index("seq")

    def put(mine):
        for layer in range(dim.layers):
            dst = keep if layer == mine else send
            for d in range(dim.D):
                dst[d, share.q :, :] = tile[layer * SMALL : (layer + 1) * SMALL, :]

    for mine in range(2):
        pl.when(me & 1 == mine)(functools.partial(put, mine))


def tie(x, others):
    x, *others = lax.optimization_barrier((x, *others))
    return x, others


def swap(x, axis, mask):
    count = lax.axis_size(axis)
    return lax.ppermute(x, axis, [(i, i ^ mask) for i in range(count)])


def chips_gather(dim, x):
    return [x] + [swap(x, "seq", k) for k in range(2, dim.S, 2)]


def cores_gather(pieces):
    return [p for x in pieces for p in (x, swap(x, "seq", 1))]


def plane_gather(dim, x):
    return cores_gather(chips_gather(dim, x))


def tree_sum(parts):
    while len(parts) > 1:
        parts = [a + b for a, b in zip(parts[::2], parts[1::2])]
    return parts[0]


def half_sums(dim, keep, send):
    got = swap(send, "seq", 1)
    return [keep[k] + got[k] for k in range(dim.S // 2)]


def plane_sums(dim, half):
    others = [swap(half[k], "seq", 2 * k) for k in range(1, dim.S // 2)]
    return [sum((o[k] for o in others), half[0][k]) for k in range(dim.D)]


def split_half(dim, half):
    cut = dim.D // 2
    a, b = [h[:cut] for h in half], [h[cut:] for h in half]
    return [jnp.stack([a[1], a[3]]), jnp.stack([b[2], b[3]]), a[0], a[2], b[0], b[1]]


def two_step_sums(dim, parts):
    send_a, send_b, a0, a2, b0, b1 = parts
    got_a, got_b = swap(send_a, "seq", 2), swap(send_b, "seq", 4)
    far_a, far_b = swap(a2 + got_a[1], "seq", 4), swap(b1 + got_b[1], "seq", 2)
    a, b = a0 + got_a[0] + far_a, b0 + got_b[0] + far_b
    cut = dim.D // 2
    return [a[d] for d in range(cut)] + [b[d] for d in range(dim.D - cut)]


def dp_sum_halving(dim, parts):
    n = dim.D
    while n > 1:
        n //= 2
        got = swap(jnp.stack(parts[n:]), "dp", n)
        parts = [parts[k] + got[k] for k in range(n)]
    return parts[0]


def dp_sum(dim, parts):
    return sum((swap(parts[k], "dp", k) for k in range(1, dim.D)), parts[0])


def unpack_kernel(dim, shares, kinds, last, *refs):
    lower, upper, outs, (mine, other) = refs[: dim.S], refs[dim.S : 2 * dim.S], refs[2 * dim.S : -2], refs[-2:]
    head = last.q + SMALL
    for dst, first in ((mine, 0), (other, 1)):
        dst[...] = tree_sum([lower[k][:head, :] for k in range(first, dim.S, 2)])
    g_gain, g_bias, g_nu, g_theta, g_gamma, g_in, g_out, g_skip, g_glu, g_glu_bias = outs
    me, my = lax.axis_index("seq"), lax.axis_index("dp")

    def place(layer, kind, rows, value):
        if kind == "in":
            g_in[layer, rows, :] = value
        elif kind == "out":
            g_out[layer, rows, :] = value
        elif kind == "gv":
            g_glu[layer, rows, 0 : dim.H] = value
        else:
            g_glu[layer, rows, dim.H : 2 * dim.H] = value

    def put(k, s):
        for share, names, src, base in zip(shares, kinds, (lower[k], upper[k]), (head, 0)):
            for off in range(0, share.q, share.step):
                p = s * share.q + off
                if p // dim.Hd < share.nm:
                    layer, kind = names[p // dim.Hd]
                    r = p % dim.Hd
                    place(layer, kind, slice(r, r + share.step), src[base + off : base + off + share.step, :])

    def vectors(d):
        def own(layer, index, lo, width, out, at=0):
            src = (mine, other)

            def copy(ref):
                start = lo + d * width
                out[layer : layer + 1, :] = ref[last.q + index : last.q + index + 1, start : start + width]

            pl.when(me & 1 == layer)(functools.partial(copy, src[0]))
            pl.when(me & 1 != layer)(functools.partial(copy, src[1]))

        for layer in range(dim.layers):
            for index, out in ((GAIN, g_gain), (BIAS, g_bias), (SKIP, g_skip)):
                own(layer, index, 0, dim.Hd, out)
            n = dim.N // dim.D
            own(layer, 5, 0, n, g_nu)
            own(layer, 5, dim.N, n, g_theta)
            own(layer, 6, 0, n, g_gamma)
            width = 2 * dim.H // dim.D
            index = BIAS_V if d * width < dim.H else BIAS_G
            own(layer, index, 0 if index == BIAS_V else -dim.H, width, g_glu_bias)

    for who in range(dim.S):

        def all_of(who=who):
            for k in range(dim.S):
                put(k, k ^ who)
            half = who & 1
            for ref, part in ((mine, half), (other, 1 - half)):
                place(0, "in", slice(part * last.q, (part + 1) * last.q), ref[: last.q, :])

        pl.when(me == who)(all_of)
    for d in range(dim.D):
        pl.when(my == d)(functools.partial(vectors, d))


def unpack(dim, shares, kinds, last, lower, upper):
    n, l = dim.N // dim.D, dim.layers
    vec, small = f32(l, dim.Hd), f32(l, n)
    mat, wide = f32(l, dim.Hd, dim.H), f32(l, dim.Hd, 2 * dim.H)
    outs = [vec, vec, small, small, small, mat, mat, vec, wide, f32(l, 2 * dim.H // dim.D)]
    return call(functools.partial(unpack_kernel, dim, shares, kinds, last), outs, [pltpu.VMEM((last.q + SMALL, dim.H), F32)] * 2, *lower, *upper)


def body(inputs, out_grad, ln_gain, ln_bias, nu_log, theta_log, gamma_log, in_map, out_map, skip_gain, glu_weight, glu_bias):
    dim = Dims(inputs, in_map, lax.axis_size("dp"), lax.axis_size("seq"))
    T, H, N, R, B, D, S = dim.T, dim.H, dim.N, dim.R, dim.B, dim.D, dim.S
    me, my = lax.axis_index("seq"), lax.axis_index("dp")
    x = inputs.reshape(R, dim.L, H)
    og = out_grad.reshape(R, dim.L, H)

    heads = [SMALL, SMALL, 0]
    vectors = (ln_gain, ln_bias, skip_gain, nu_log, theta_log, gamma_log, glu_bias)
    messages = call(
        functools.partial(pack_kernel, dim),
        [f32(head + len(chunk) * dim.q, H) for head, chunk in zip(heads, CHUNKS)],
        [pltpu.VMEM(v.shape, F32) for v in vectors] + [pltpu.SemaphoreType.DMA((len(vectors) + sum(map(len, CHUNKS)),))],
        in_map, out_map, glu_weight, *vectors,
        anywhere=3 + len(vectors),
    )
    def stacked(others, head):
        return jnp.stack([other[head:].reshape(-1, dim.q, H) for other in others], 1)

    def along_dp(mine):
        return [swap(mine, "dp", k) for k in range(1, D)]

    def table_of(mine, others, head=SMALL):
        total = mine[:head]
        for other in others:
            total = total + other[:head]
        return call(functools.partial(prep_kernel, dim), [f32(TABLE, H)], [], total)[0]

    mine0, mine1, mine2 = messages
    others0 = along_dp(mine0)
    table0 = table_of(mine0, others0)
    mine1, others0 = tie(mine1, others0)
    others1 = along_dp(mine1)
    table1 = table_of(mine1, others1)
    chips0 = chips_gather(dim, stacked(others0, SMALL))
    joined1, chips0 = tie(stacked(others1, SMALL), chips0)
    pieces0 = cores_gather(chips0)
    mine2, (joined1,) = tie(mine2, [joined1])
    chips1 = chips_gather(dim, joined1)
    blocks = mine2[None]
    while blocks.shape[0] < D:
        blocks = jnp.concatenate([blocks, swap(blocks, "dp", blocks.shape[0])], 0)
    joined2 = stacked([blocks[k] for k in range(1, D)], 0)
    pieces = [pieces0, cores_gather(chips1), None]

    big, ent, fins = pltpu.VMEM((T, H), F32), pltpu.VMEM((R, H), F32), f32(B, H)
    stat = pltpu.VMEM((T, 128), F32)
    vec = pltpu.VMEM((SMALL, H), F32)

    def k(fn, names, outs, scratch, *args, us, late=(), sinks=()):
        chunks = [c for c, chunk in enumerate(CHUNKS) if set(chunk) & set(names)]
        kernel, count, own = weights_in(dim, chunks, names, fn)
        sources = [in_map, out_map, glu_weight] + [p for c in chunks for p in pieces[c]]
        late = [count + i for i in late]
        return call(kernel, outs, scratch + own, *sources, *args, us=us, anywhere=count, late=late, sinks=sinks)

    def carried(fin):
        return lax.all_gather(fin, "seq")

    part = [pltpu.VMEM((T, H), BF16)] * 2
    split_weight = [pltpu.VMEM((H, H), BF16)] * 2
    xhat0, rstd0, drive0, cf0, fin0, *normed0 = k(
        k_a0, [(0, 0)], [big, stat, big, ent, fins] + part, split_weight, x, table0, us=2.8
    )
    g0 = carried(fin0)
    joined2, (g0,) = tie(joined2, [g0])
    chips2 = chips_gather(dim, joined2)
    en0, states0, mixed0, v0, s0, sh0, sl0, ch0, cl0, act1, xhat1, rstd1, drive1, cf1, fin1, *normed1 = k(
        k_b0,
        [(0, 1), (0, 2), (0, 3), (1, 0)],
        [ent, big, big, big, big] + part * 2 + [big, big, stat, big, ent, fins] + part,
        split_weight,
        x, table0, table1, drive0, cf0, g0, xhat0,
        us=9.0,
    )
    fin1, chips2 = tie(fin1, chips2)
    g1 = carried(fin1)
    pieces[2] = cores_gather(chips2)
    spare = [pltpu.VMEM((T, H), F32)]
    out, en1, states1, dmixed1, ds1, rcf1, rfin1, sums1a, sh1, sl1, ch1, cl1, dvh1, dvl1, dgh1, dgl1, mh1, ml1 = k(
        k_b1,
        [(1, 1), (1, 2), (1, 3)],
        [f32(R, dim.L, H), ent, big, big, big, ent, fins, vec] + part * 5,
        split_weight + spare * 3,
        act1, og, table1, drive1, cf1, g1, xhat1,
        us=12.5, sinks=[0],
    )
    share1, share2, share3 = Share(dim, 3), Share(dim, 4), Halves(dim)
    tile = [pltpu.VMEM((WIDE, H), F32)]
    keep1, send1 = call(
        functools.partial(k_w1, dim, share1), [f32(*share1.shape)] * 2, tile,
        ch1, cl1, dvh1, dvl1, dgh1, dgl1, sh1, sl1, mh1, ml1, us=4.0,
    )
    rfin1, (send1,) = tie(rfin1, [send1])
    gr1 = carried(rfin1)
    gr1, half1 = tie(gr1, half_sums(dim, keep1, send1))
    dmid, dmixed0, ds0, rcf0, rfin0, sums1b, sums0a, dph1, dpl1, dvh0, dvl0, dgh0, dgl0, mh0, ml0 = k(
        k_c1,
        [(1, 0), (0, 2), (0, 3), (0, 1)],
        [big, big, big, ent, fins, vec, vec] + part * 4,
        split_weight + [pltpu.VMEM((R, H), F32)],
        og, table1, table0, ds1, rcf1, gr1, states1, en1, drive1, xhat1, rstd1, dmixed1,
        xhat0, mixed0, v0, s0,
        us=9.5,
    )
    keep2, send2 = call(
        functools.partial(k_w2, dim, share2), [f32(*share2.shape)] * 2, tile,
        ch0, cl0, dvh0, dvl0, dgh0, dgl0, sh0, sl0, mh0, ml0, *normed1, dph1, dpl1, us=5.3,
    )
    rfin0, (send2, *sums1) = tie(rfin0, [send2, *plane_sums(dim, half1)])
    gr0 = carried(rfin0)
    half2 = half_sums(dim, keep2, send2)
    two_steps = S == 8
    gr0, half2 = tie(gr0, split_half(dim, half2) if two_steps else half2)
    input_grad, keep3, send3 = k(
        functools.partial(k_c0, share3),
        [(0, 0)],
        [f32(R, dim.L, H)] + [f32(*share3.shape)] * 2,
        part + split_weight + [pltpu.VMEM((R, H), F32)] + spare + [pltpu.VMEM((SMALL, H), F32)] + tile,
        table0, ds0, rcf0, gr0, states0, en0, drive0, xhat0, rstd0, dmixed0, dmid, sums1a, sums1b, sums0a, *normed0,
        us=6.0, sinks=[0],
    )
    sums2 = two_step_sums(dim, half2) if two_steps else plane_sums(dim, half2)
    got3 = swap(send3, "seq", 1)
    half3 = [keep3[d] + got3[d] for d in range(D)]
    total3 = tree_sum([half3[0]] + [swap(half3[k], "dp", k) for k in range(1, D)])
    upper1 = dp_sum(dim, sums1)
    chips3 = chips_gather(dim, jnp.concatenate([total3, upper1], 0))
    last = cores_gather(chips3)
    upper = plane_gather(dim, dp_sum(dim, sums2))
    kinds = [[(1, "gv"), (1, "gg"), (1, "out")], [(0, "gv"), (0, "gg"), (0, "out"), (1, "in")]]
    grads = unpack(dim, (share1, share2), kinds, share3, last, upper)
    return (out.reshape(inputs.shape), input_grad.reshape(inputs.shape), *grads)


def solution(mesh):
    act, vec, mat = P("dp", "seq", None), P(None, "dp"), P(None, "dp", None)
    in_specs = (act, act, vec, vec, vec, vec, vec, mat, mat, vec, mat, vec)
    out_specs = (act, act, vec, vec, vec, vec, vec, mat, mat, vec, mat, vec)
    return jax.shard_map(body, mesh=mesh, in_specs=in_specs, out_specs=out_specs, check_vma=False)
```

```python
import functools
import math

import jax
import jax.numpy as jnp
from jax import lax
from jax.experimental import pallas as pl
from jax.experimental.pallas import tpu as pltpu
from jax.sharding import PartitionSpec as P

NORM_EPS = 1e-05
GROUPS = 8
WIDE = 256
SMALL = 8
TABLE = 16
F32 = jnp.float32
BF16 = jnp.bfloat16
GELU_C = math.sqrt(2.0 / math.pi)

GAIN, BIAS, SKIP, BIAS_V, BIAS_G, GAMMA, LAM, LAM1, LAM2, LAM4, LAM8, RATES = range(12)


CHUNKS = (((0, 0), (1, 0)), ((0, 1), (0, 2), (0, 3)), ((1, 1), (1, 2), (1, 3)))


class Dims:
    def __init__(self, inputs, in_map, dp, seq):
        self.B, self.Tb, self.H = inputs.shape
        self.layers, self.Hd = in_map.shape[:2]
        self.N = self.H // 2
        self.T = self.B * self.Tb
        self.R = self.B * GROUPS
        self.L = self.Tb // GROUPS
        self.D, self.S = dp, seq
        self.q = max(16, self.Hd // seq)
        self.used = self.Hd // self.q


def cmul(ar, ai, br, bi):
    return ar * br - ai * bi, ar * bi + ai * br


def split(x):
    hi = x.astype(BF16)
    return hi, (x - hi.astype(F32)).astype(BF16)


def dot3(ah, al, bh, bl, dims):
    def one(a, b):
        return lax.dot_general(a, b, (dims, ((), ())), preferred_element_type=F32)

    return one(ah, bh) + (one(ah, bl) + one(al, bh))


def product(ah, al, wh, wl, dst, transposed=False, add=False):
    for n in range(dst.shape[1] // WIDE):
        cols = slice(n * WIDE, (n + 1) * WIDE)
        if transposed:
            res = dot3(ah[...], al[...], wh[cols, :], wl[cols, :], ((1,), (1,)))
        else:
            res = dot3(ah[...], al[...], wh[:, cols], wl[:, cols], ((1,), (0,)))
        dst[:, cols] = dst[:, cols] + res if add else res


def each_step(dim, fn, unroll=2, reverse=False, init=0):
    def one(i, carry):
        j = dim.L - 1 - i if reverse else i
        rows = pl.ds(pl.multiple_of(j * dim.R, dim.R), dim.R)
        return fn(j, rows, carry)

    return lax.fori_loop(0, dim.L, one, init, unroll=unroll)


def each_span(dim, fn, init=0, steps=8):
    def one(i, carry):
        rows = pl.ds(pl.multiple_of(i * steps * dim.R, steps * dim.R), steps * dim.R)
        return fn([i * steps + u for u in range(steps)], rows, carry)

    return lax.fori_loop(0, dim.L // steps, one, init)


def fold(x):
    return jnp.sum(x.reshape(x.shape[0] // 8, 8, x.shape[1]), 0)


def row(table, index, n=1):
    return table[index : index + n, :]


def lam_of(dim, table, index, reverse):
    pair = table[index : index + 1, :]
    real, imag = pair[:, : dim.N], pair[:, dim.N :]
    return real, -imag if reverse else imag


def chunk_scan(dim, table, yr, yi, reverse):
    place = lax.broadcasted_iota(jnp.int32, yr.shape, 0)
    for dist, index in ((1, LAM1), (2, LAM2), (4, LAM4)):
        pr, pi = lam_of(dim, table, index, reverse)
        if reverse:
            shift, seen = GROUPS - dist, place < GROUPS - dist
        else:
            shift, seen = dist, place >= dist
        sr = jnp.where(seen, pltpu.roll(yr, shift, 0), 0.0)
        si = jnp.where(seen, pltpu.roll(yi, shift, 0), 0.0)
        mr, mi = cmul(pr, pi, sr, si)
        yr, yi = yr + mr, yi + mi
    return yr, yi


def local_finals(dim, table, drive_ref, cf_ref, f_ref, reverse):
    lr, li = lam_of(dim, table, LAM, reverse)
    lr = jnp.broadcast_to(lr, (dim.R, dim.N))
    li = jnp.broadcast_to(li, (dim.R, dim.N))

    def step(j, rows, carry):
        d = drive_ref[rows, :]
        mr, mi = cmul(lr, li, *carry)
        return mr + d[:, : dim.N], mi + d[:, dim.N :]

    zero = jnp.zeros((dim.R, dim.N), F32)
    fr, fi = each_step(dim, step, 4, reverse, (zero, zero))
    cf_ref[:, : dim.N] = fr
    cf_ref[:, dim.N :] = fi
    last = 0 if reverse else GROUPS - 1
    for b in range(dim.B):
        rows = slice(b * GROUPS, (b + 1) * GROUPS)
        yr, yi = chunk_scan(dim, table, fr[rows], fi[rows], reverse)
        f_ref[b : b + 1, : dim.N] = yr[last : last + 1]
        f_ref[b : b + 1, dim.N :] = yi[last : last + 1]


def entries_of(dim, table, cf_ref, g_ref, en_ref, reverse):
    me = lax.axis_index("seq")
    lr, li = lam_of(dim, table, LAM8, reverse)
    xr = jnp.zeros((dim.B, dim.N), F32)
    xi = xr
    order = reversed(range(dim.S)) if reverse else range(dim.S)
    for other in order:
        ahead = other > me if reverse else other < me
        g = g_ref[other]
        mr, mi = cmul(lr, li, xr, xi)
        xr = jnp.where(ahead, mr + g[:, : dim.N], xr)
        xi = jnp.where(ahead, mi + g[:, dim.N :], xi)
    for b in range(dim.B):
        rows = slice(b * GROUPS, (b + 1) * GROUPS)
        f = cf_ref[rows, :]
        place = lax.broadcasted_iota(jnp.int32, f.shape, 0)
        x = jnp.concatenate([xr[b : b + 1], xi[b : b + 1]], 1)
        if reverse:
            y = jnp.where(place == GROUPS - 1, x, pltpu.roll(f, GROUPS - 1, 0))
        else:
            y = jnp.where(place == 0, x, pltpu.roll(f, 1, 0))
        yr, yi = chunk_scan(dim, table, y[:, : dim.N], y[:, dim.N :], reverse)
        en_ref[rows, : dim.N] = yr
        en_ref[rows, dim.N :] = yi


def norm_step(dim, x, table):
    mean = jnp.mean(x, -1, keepdims=True)
    centred = x - mean
    var = jnp.mean(centred * centred, -1, keepdims=True)
    rstd = lax.rsqrt(var + NORM_EPS)
    xhat = centred * rstd
    return xhat, rstd, xhat * row(table, GAIN) + row(table, BIAS)


def front(dim, load_act, table, w_in, xhat, rstd, drive, cf, fin, ah, al, wh, wl):
    def norm(steps, rows, _):
        xh, rs, normed = norm_step(dim, load_act(steps, rows), table)
        xhat[rows, :] = xh
        rstd[rows, :] = jnp.broadcast_to(rs, (rs.shape[0], 128))
        ah[rows, :], al[rows, :] = split(normed)
        return 0

    each_span(dim, norm)
    product(ah, al, *w_in.fill(*halves_of(w_in, wh, wl)), drive)

    def scale(j, rows, _):
        drive[rows, :] = drive[rows, :] * row(table, GAMMA)
        return 0

    each_step(dim, scale, 4)
    local_finals(dim, table, drive, cf, fin, False)


def gelu_parts(m):
    inner = GELU_C * (m + 0.044715 * (m * m * m))
    th = jnp.tanh(inner)
    return th


def back(dim, table, drive, cf, g, xhat, w_out, w_gv, w_gg, en, states, mixed, v, s, sh, sl, ch, cl, wh, wl):
    entries_of(dim, table, cf, g, en, False)
    lr, li = lam_of(dim, table, LAM, False)
    lr = jnp.broadcast_to(lr, (dim.R, dim.N))
    li = jnp.broadcast_to(li, (dim.R, dim.N))

    def scan(j, rows, carry):
        d = drive[rows, :]
        mr, mi = cmul(lr, li, *carry)
        both = jnp.concatenate([mr + d[:, : dim.N], mi + d[:, dim.N :]], 1)
        states[rows, :] = both
        sh[rows, :], sl[rows, :] = split(both)
        return both[:, : dim.N], both[:, dim.N :]

    each_step(dim, scan, 4, False, (en[:, : dim.N], en[:, dim.N :]))
    product(sh, sl, *w_out.fill(*halves_of(w_out, wh, wl)), mixed)

    def gelu(j, rows, _):
        normed = xhat[rows, :] * row(table, GAIN) + row(table, BIAS)
        m = mixed[rows, :] + row(table, SKIP) * normed
        mixed[rows, :] = m
        a = (0.5 * m) * (1.0 + gelu_parts(m))
        ch[rows, :], cl[rows, :] = split(a)
        return 0

    each_step(dim, gelu, 4)
    product(ch, cl, *w_gv.fill(*halves_of(w_gv, wh, wl)), v)
    product(ch, cl, *w_gg.fill(*halves_of(w_gg, wh, wl)), s)


def gate(dim, table, v, s, rows):
    vv = v[rows, :] + row(table, BIAS_V)
    ss = jax.nn.sigmoid(s[rows, :] + row(table, BIAS_G))
    v[rows, :] = vv
    s[rows, :] = ss
    return vv * ss


def top(dim, table, load_dact, v, s, mixed, xhat, w_gv, w_gg, w_out, dmixed, ds, rcf, rfin, sums, ah, al, bh, bl, mh, ml, wh, wl):
    def dgate(j, rows, carry):
        dact = load_dact(j, rows)
        ss, vv = s[rows, :], v[rows, :]
        a = dact * ss
        b = a * vv * (1.0 - ss)
        ah[rows, :], al[rows, :] = split(a)
        bh[rows, :], bl[rows, :] = split(b)
        return carry[0] + a, carry[1] + b

    zero = jnp.zeros((dim.R, dim.H), F32)
    sv, sg = each_step(dim, dgate, 2, False, (zero, zero))
    sums[BIAS_V : BIAS_V + 1, :] = jnp.sum(sv, 0, keepdims=True)
    sums[BIAS_G : BIAS_G + 1, :] = jnp.sum(sg, 0, keepdims=True)
    product(ah, al, *w_gv.fill(*halves_of(w_gv, wh, wl)), dmixed, True)
    product(bh, bl, *w_gg.fill(*halves_of(w_gg, wh, wl)), dmixed, True, True)

    def dgelu(j, rows, carry):
        m = mixed[rows, :]
        th = gelu_parts(m)
        slope = 0.5 * (1.0 + th) + (0.5 * m) * (1.0 - th * th) * (GELU_C * (1.0 + (3 * 0.044715) * (m * m)))
        d = dmixed[rows, :] * slope
        dmixed[rows, :] = d
        mh[rows, :], ml[rows, :] = split(d)
        normed = xhat[rows, :] * row(table, GAIN) + row(table, BIAS)
        return carry + d * normed

    sums[SKIP : SKIP + 1, :] = jnp.sum(each_step(dim, dgelu, 2, False, zero), 0, keepdims=True)
    product(mh, ml, *w_out.fill(*halves_of(w_out, wh, wl)), ds, True)
    local_finals(dim, table, ds, rcf, rfin, True)


def bottom(dim, table, ds, rcf, gr, states, en, drive, xhat, rstd, dmixed, w_in, load_dact, store, buf, adj_en, sums, ah, al, wh, wl):
    entries_of(dim, table, rcf, gr, adj_en, True)
    lr, li = lam_of(dim, table, LAM, True)
    lr = jnp.broadcast_to(lr, (dim.R, dim.N))
    li = jnp.broadcast_to(li, (dim.R, dim.N))
    zero = jnp.zeros((dim.R, dim.N), F32)

    def scan(j, rows, carry):
        ar, ai, dr, di, dgam = carry
        d = ds[rows, :]
        mr, mi = cmul(lr, li, ar, ai)
        ar, ai = mr + d[:, : dim.N], mi + d[:, dim.N :]
        earlier = pl.ds(pl.multiple_of(jnp.maximum(j - 1, 0) * dim.R, dim.R), dim.R)
        before = jnp.where(j == 0, en[...], states[earlier, :])
        br, bi = before[:, : dim.N], before[:, dim.N :]
        dr = dr + (ar * br + ai * bi)
        di = di + (ai * br - ar * bi)
        u = drive[rows, :]
        dgam = dgam + (ar * u[:, : dim.N] + ai * u[:, dim.N :])
        dp = jnp.concatenate([ar, ai], 1) * row(table, GAMMA)
        ah[rows, :], al[rows, :] = split(dp)
        return ar, ai, dr, di, dgam

    start = (adj_en[:, : dim.N], adj_en[:, dim.N :], zero, zero, zero)
    _, _, dr, di, dgam = each_step(dim, scan, 2, True, start)
    dr, di, dgam = (jnp.sum(x, 0, keepdims=True) for x in (dr, di, dgam))
    fr, fi = lam_of(dim, table, LAM, False)
    rates = row(table, RATES)
    rate, angle = rates[:, : dim.N], rates[:, dim.N :]
    sums[5:6, : dim.N] = -rate * (dr * fr + di * fi)
    sums[5:6, dim.N :] = angle * (di * fr - dr * fi)
    sums[6:7, : dim.N] = dgam
    sums[6:7, dim.N :] = jnp.zeros_like(dgam)
    sums[7:8, :] = jnp.zeros((1, dim.H), F32)

    product(ah, al, *w_in.fill(*halves_of(w_in, wh, wl)), buf, True)
    wide = jnp.zeros((8, dim.H), F32)

    def dnorm(steps, rows, carry):
        dn = buf[rows, :] + dmixed[rows, :] * row(table, SKIP)
        xh = xhat[rows, :]
        dx = dn * row(table, GAIN)
        m1 = jnp.mean(dx, -1, keepdims=True)
        m2 = jnp.mean(dx * xh, -1, keepdims=True)
        store(steps, rows, load_dact(steps, rows) + rstd[rows, 0:1] * (dx - m1 - xh * m2))
        return carry[0] + fold(dn * xh), carry[1] + fold(dn)

    sgain, sbias = each_span(dim, dnorm, (wide, wide))
    sums[GAIN : GAIN + 1, :] = jnp.sum(sgain, 0, keepdims=True)
    sums[BIAS : BIAS + 1, :] = jnp.sum(sbias, 0, keepdims=True)


def split_rows(dim, load, xh, xl):
    def one(j, rows, _):
        xh[rows, :], xl[rows, :] = split(load(rows))
        return 0

    each_step(dim, one, 4)


class Share:
    def __init__(self, dim, nm):
        self.dim, self.nm = dim, nm
        self.q = -(-nm * dim.Hd // (8 * dim.S)) * 8
        self.step = math.gcd(self.q, dim.Hd)
        self.shape = (dim.S // 2, dim.D, self.q, dim.H)

    def place(self, m, d, r, me, my):
        p = m * self.dim.Hd + r
        s = p // self.q
        return s & 1, ((s ^ me) >> 1, d ^ my), p % self.q


class Halves:
    def __init__(self, dim):
        self.dim = dim
        self.q = dim.Hd // 2
        self.step = math.gcd(self.q, WIDE)
        self.shape = (dim.D, self.q + SMALL, dim.H)

    def place(self, m, d, r, me, my):
        return r // self.q, (d ^ my,), r % self.q


def weight_grad(dim, share, m, ah, al, bh, bl, tile, keep, send):
    for h0 in range(0, dim.H, WIDE):
        tile[...] = dot3(ah[:, h0 : h0 + WIDE], al[:, h0 : h0 + WIDE], bh[...], bl[...], ((0,), (0,)))
        put_rows(dim, share, m, h0, tile, keep, send)


def put_rows(dim, share, m, h0, tile, keep, send):
    me = lax.axis_index("seq")
    my = lax.axis_index("dp")

    def put(mine):
        for r0 in range(0, WIDE, share.step):
            h = h0 + r0
            odd, index, off = share.place(m, h // dim.Hd, h % dim.Hd, me, my)
            dst = keep if odd == mine else send
            dst[(*index, slice(off, off + share.step), slice(None))] = tile[r0 : r0 + share.step, :]

    for mine in range(2):
        pl.when(me & 1 == mine)(functools.partial(put, mine))


class Kept:
    def __init__(self, value):
        self.value = value
        self.shape = value.shape


class Moved:
    def __init__(self, far, near, sem):
        self.far, self.near, self.sem, self.copies = far, near, sem, []

    def fetch(self):
        self.copies.append(pltpu.make_async_copy(self.far, self.near, self.sem.at[0]))
        self.copies[0].start()

    def flush(self, *index):
        sem = self.sem.at[len(self.copies)]
        near, far = (self.near.at[index], self.far.at[index]) if index else (self.near, self.far)
        self.copies.append(pltpu.make_async_copy(near, far, sem))
        self.copies[-1].start()

    def get(self):
        for copy in self.copies:
            copy.wait()
        return self.near


def call(fn, outs, scratch, *args, us=1.0, anywhere=0, late=(), sinks=()):
    scratch = list(scratch)
    first, total = len(args), len(args) + len(outs)
    moved = list(late) + [first + i for i in sinks]
    if moved:
        inner = fn
        for i in moved:
            shape = args[i].shape if i < first else outs[i - first].shape
            scratch += [pltpu.VMEM(shape, F32), pltpu.SemaphoreType.DMA((8,))]

        def fn(*refs):
            refs, spare = list(refs[: -2 * len(moved)]), refs[-2 * len(moved) :]
            for n, i in enumerate(moved):
                refs[i] = Moved(refs[i], *spare[2 * n : 2 * n + 2])
                if i < first:
                    refs[i].fetch()
            inner(*refs)
            for i in moved:
                if i >= first:
                    refs[i].get()

    spaces = [pltpu.HBM if i < anywhere or i in late else pltpu.VMEM for i in range(first)]

    def placed(x, space):
        if isinstance(x, Kept):
            return pltpu.with_memory_space_constraint(x.value, pltpu.VMEM)
        return pltpu.with_memory_space_constraint(x, pltpu.HBM) if space is pltpu.HBM else x

    values = [placed(x, space) for x, space in zip(args, spaces)]
    room = 10 << 20
    for x in scratch:
        if len(x.shape) > 1:
            room += math.prod(x.shape) * (2 if x.dtype == BF16 else 4)
    results = pl.pallas_call(
        fn,
        out_shape=outs,
        in_specs=[pl.BlockSpec(memory_space=space) for space in spaces],
        out_specs=[pl.BlockSpec(memory_space=pl.ANY if i in sinks else pltpu.VMEM) for i in range(len(outs))],
        scratch_shapes=scratch,
        compiler_params=pltpu.CompilerParams(vmem_limit_bytes=max(20 << 20, room)),
        cost_estimate=pl.CostEstimate(flops=1, bytes_accessed=int(us * 3.6e6), transcendentals=0),
    )(*values)
    return [x if isinstance(o, jax.ShapeDtypeStruct) else Kept(x) for x, o in zip(results, outs)]


def f32(*shape):
    return jax.ShapeDtypeStruct(shape, F32)


def prep_kernel(dim, small, table):
    s = small[...]
    nu, theta, gam = s[5:6, : dim.N], s[5:6, dim.N :], s[6:7, : dim.N]
    rate, angle = jnp.exp(nu), jnp.exp(theta)
    mod = jnp.exp(-rate)
    re, im = mod * jnp.cos(angle), mod * jnp.sin(angle)
    gamma = jnp.exp(gam)

    def put(index, a, b):
        table[index : index + 1, : dim.N] = a
        table[index : index + 1, dim.N :] = b

    table[...] = jnp.zeros((TABLE, dim.H), F32)
    table[:5, :] = s[:5]
    put(GAMMA, gamma, gamma)
    put(LAM, re, im)
    put(RATES, rate, angle)
    power = 1
    while power < dim.L:
        re, im = cmul(re, im, re, im)
        power *= 2
    for index in (LAM1, LAM2, LAM4, LAM8):
        put(index, re, im)
        re, im = cmul(re, im, re, im)


def shard_of(sources, name, rows, H):
    layer, m = name
    return sources[(0, 1, 2, 2)[m]].at[layer, rows, pl.ds(H if m == 3 else 0, H)]


def pack_kernel(dim, in_map, out_map, glu, gain, bias, skip, nu, theta, gamma, glu_bias, *refs):
    outs, held, sem = refs[:3], refs[3:-1], refs[-1]
    vectors = (gain, bias, skip, nu, theta, gamma, glu_bias)
    me, my = lax.axis_index("seq"), lax.axis_index("dp")
    start = pl.multiple_of(jnp.minimum(me, dim.used - 1) * dim.q, 16)
    moves = []
    for src, dst in zip(vectors, held):
        moves.append(pltpu.make_async_copy(src, dst, sem.at[len(moves)]))
    gain, bias, skip, nu, theta, gamma, glu_bias = held
    for out, chunk in zip(outs, CHUNKS):
        head = out.shape[0] - len(chunk) * dim.q
        for i, name in enumerate(chunk):
            src = shard_of((in_map, out_map, glu), name, pl.ds(start, dim.q), dim.H)
            dst = out.at[head + i * dim.q : head + (i + 1) * dim.q, :]
            moves.append(pltpu.make_async_copy(src, dst, sem.at[len(moves)]))
    for move in moves:
        move.start()
    for move in moves[: len(held)]:
        move.wait()

    def spread(ref, layer, width):
        vec = ref[layer : layer + 1, :]
        full = jnp.concatenate([vec] * (width // vec.shape[1]), 1)
        lane = lax.broadcasted_iota(jnp.int32, full.shape, 1)
        return jnp.where(lane // vec.shape[1] == my, full, 0.0)

    for layer in range(dim.layers):
        both = spread(glu_bias, layer, 2 * dim.H)
        rows = [spread(ref, layer, dim.H) for ref in (gain, bias, skip)] + [both[:, : dim.H], both[:, dim.H :]]
        rows.append(jnp.concatenate([spread(nu, layer, dim.N), spread(theta, layer, dim.N)], 1))
        rows.append(jnp.concatenate([spread(gamma, layer, dim.N), jnp.zeros((1, dim.N), F32)], 1))
        for i, value in enumerate(rows):
            outs[layer][i : i + 1, :] = value
        outs[layer][7:8, :] = jnp.zeros((1, dim.H), F32)
    for move in moves[len(held) :]:
        move.wait()


def halves_of(weight, wh, wl):
    return weight.kept or (wh, wl)


class Weight:
    def __init__(self, dim, name, place, sources, own, buf, sem):
        self.dim, self.name, self.place = dim, name, place
        self.sources, self.own, self.buf, self.sem = sources, own, buf, sem
        self.here, self.kept, self.halves = False, False, None

    def moves(self):
        shard = shard_of(self.sources, self.name, slice(None), self.dim.H)
        yield pltpu.make_async_copy(shard, self.own, self.sem.at[self.dim.S])
        for k, piece in enumerate(self.sources[3:]):
            yield pltpu.make_async_copy(piece.at[self.place], self.buf.at[k], self.sem.at[k])

    def start(self):
        for move in self.moves():
            move.start()

    def fill(self, wh, wl):
        if self.halves is None:
            self.write(wh, wl)
            if self.kept:
                self.halves = wh, wl
            return wh, wl
        return self.halves

    def write(self, wh, wl):
        dim, q = self.dim, self.dim.q
        if not self.here:
            for move in self.moves():
                move.wait()
        self.here = True
        me, my = lax.axis_index("seq"), lax.axis_index("dp")

        def put(start, n, value):
            rows = pl.ds(pl.multiple_of(start, 16), n)
            wh[rows, :], wl[rows, :] = split(value)

        def mine(i, _):
            put(my * dim.Hd + i * 32, 32, self.own[pl.ds(pl.multiple_of(i * 32, 32), 32), :])
            return 0

        lax.fori_loop(0, dim.Hd // 32, mine, 0)

        def one(k, _):
            s = k ^ me

            def block():
                for kz in range(1, dim.D):
                    put((kz ^ my) * dim.Hd + s * q, q, self.buf[k, kz - 1])

            if dim.used < dim.S:
                pl.when(s < dim.used)(block)
            else:
                block()
            return 0

        lax.fori_loop(0, dim.S, one, 0)


def weights_in(dim, chunks, names, fn):
    first = 3 + len(chunks) * dim.S

    def kernel(*refs):
        spare = refs[len(refs) - 3 * len(names) :]
        weights = []
        for i, name in enumerate(names):
            (n,) = [n for n, c in enumerate(chunks) if name in CHUNKS[c]]
            sources = refs[:3] + refs[3 + n * dim.S : 3 + (n + 1) * dim.S]
            place = CHUNKS[chunks[n]].index(name)
            weights.append(Weight(dim, name, place, sources, *spare[3 * i : 3 * i + 3]))
        for w in weights:
            w.start()
        fn(dim, weights, *refs[first : len(refs) - 3 * len(names)])

    scratch = [
        pltpu.VMEM((dim.Hd, dim.H), F32),
        pltpu.VMEM((dim.S, dim.D - 1, dim.q, dim.H), F32),
        pltpu.SemaphoreType.DMA((dim.S + 1,)),
    ] * len(names)
    return kernel, first, scratch


def strided(dim, ref):
    def load(steps, rows):
        if isinstance(steps, list):
            return jnp.concatenate([ref[:, j, :] for j in steps], 0)
        return ref[:, steps, :]

    return load


def plain(ref):
    return lambda j, rows: ref[rows, :]


def k_a0(dim, weights, x, table, xhat, rstd, drive, cf, fin, nh, nl, wh, wl):
    front(dim, strided(dim, x), table, weights[0], xhat, rstd, drive, cf, fin, nh, nl, wh, wl)


def k_b0(dim, weights, x, t, t1, drive, cf, g, xhat,
         en, states, mixed, v, s, sh, sl, ch, cl, act1, xhat1, rstd1, drive1, cf1, fin1, nh, nl, wh, wl):
    w_out, w_gv, w_gg, w_in1 = weights
    back(dim, t, drive, cf, g, xhat, w_out, w_gv, w_gg, en, states, mixed, v, s, sh, sl, ch, cl, wh, wl)
    load = strided(dim, x)

    def residual(steps, rows):
        act = load(steps, rows) + gate(dim, t, v, s, rows)
        act1[rows, :] = act
        return act

    front(dim, residual, t1, w_in1, xhat1, rstd1, drive1, cf1, fin1, nh, nl, wh, wl)


def k_b1(dim, weights, act1, out_grad, t, drive, cf, g, xhat,
         out, en, states, dmixed, ds, rcf, rfin, sums, sh, sl, ch, cl, dvh, dvl, dgh, dgl, mh, ml, *scratch):
    w_out, w_gv, w_gg = weights
    for i, w in enumerate(weights):
        w.kept = scratch[2 * i : 2 * i + 2]
    wh, wl, (mixed, v, s) = None, None, scratch[6:]
    back(dim, t, drive, cf, g, xhat, w_out, w_gv, w_gg, en, states, mixed, v, s, sh, sl, ch, cl, wh, wl)

    def residual(j, rows, _):
        out.near[:, j, :] = act1[rows, :] + gate(dim, t, v, s, rows)
        return 0

    each_step(dim, residual, 2)
    out.flush()
    sums[...] = jnp.zeros((SMALL, dim.H), F32)
    top(dim, t, strided(dim, out_grad), v, s, mixed, xhat, w_gv, w_gg, w_out, dmixed, ds, rcf, rfin, sums,
        dvh, dvl, dgh, dgl, mh, ml, wh, wl)


def k_w1(dim, share, ch, cl, dvh, dvl, dgh, dgl, sh, sl, mh, ml, keep, send, tile):
    for m, (ah, al, bh, bl) in enumerate(((ch, cl, dvh, dvl), (ch, cl, dgh, dgl), (sh, sl, mh, ml))):
        weight_grad(dim, share, m, ah, al, bh, bl, tile, keep, send)


def k_w2(dim, share, ch, cl, dvh, dvl, dgh, dgl, sh, sl, mh, ml, nh, nl, dph, dpl, keep, send, tile):
    k_w1(dim, share, ch, cl, dvh, dvl, dgh, dgl, sh, sl, mh, ml, keep, send, tile)
    weight_grad(dim, share, 3, nh, nl, dph, dpl, tile, keep, send)


def k_c1(dim, weights, out_grad, t, t0, ds, rcf, gr, states, en, drive, xhat, rstd, dmixed,
         xhat0, mixed0, v0, s0,
         dmid, dmixed0, ds0, rcf0, rfin0, sums1, sums0, dph, dpl, dvh, dvl, dgh, dgl, mh, ml, wh, wl, adj_en):
    w_in, w_gv, w_gg, w_out = weights

    def store(j, rows, value):
        dmid[rows, :] = value

    bottom(dim, t, ds, rcf, gr, states, en, drive, xhat, rstd, dmixed, w_in, strided(dim, out_grad), store,
           ds0, adj_en, sums1, dph, dpl, wh, wl)
    sums0[...] = jnp.zeros((SMALL, dim.H), F32)
    top(dim, t0, plain(dmid), v0, s0, mixed0, xhat0, w_gv, w_gg, w_out, dmixed0, ds0, rcf0, rfin0,
        sums0, dvh, dvl, dgh, dgl, mh, ml, wh, wl)


def k_c0(share, dim, weights, t, ds, rcf, gr, states, en, drive, xhat, rstd, dmixed, dmid, sums1a, sums1b, sums0a, nh, nl,
         input_grad, keep, send, ah, al, wh, wl, adj_en, buf, sums0, tile):
    def store(steps, rows, value):
        for u, j in enumerate(steps):
            input_grad.near[:, j, :] = value[u * dim.R : (u + 1) * dim.R, :]

    bottom(dim, t, ds, rcf, gr, states, en, drive, xhat, rstd, dmixed, weights[0], plain(dmid), store, buf, adj_en,
           sums0, ah, al, wh, wl)
    input_grad.flush()
    weight_grad(dim, share, 0, nh, nl, ah, al, tile, keep, send)
    place = lax.broadcasted_iota(jnp.int32, (SMALL, dim.H), 0)
    upper = (place >= SKIP) & (place <= BIAS_G)
    tile[0:SMALL, :] = jnp.where(upper, sums0a[...], sums0[...])
    tile[SMALL : 2 * SMALL, :] = jnp.where(upper, sums1a[...], sums1b[...])
    me = lax.axis_index("seq")

    def put(mine):
        for layer in range(dim.layers):
            dst = keep if layer == mine else send
            for d in range(dim.D):
                dst[d, share.q :, :] = tile[layer * SMALL : (layer + 1) * SMALL, :]

    for mine in range(2):
        pl.when(me & 1 == mine)(functools.partial(put, mine))


def tie(x, others):
    x, *others = lax.optimization_barrier((x, *others))
    return x, others


def swap(x, axis, mask):
    count = lax.axis_size(axis)
    return lax.ppermute(x, axis, [(i, i ^ mask) for i in range(count)])


def chips_gather(dim, x):
    return [x] + [swap(x, "seq", k) for k in range(2, dim.S, 2)]


def cores_gather(pieces):
    return [p for x in pieces for p in (x, swap(x, "seq", 1))]


def plane_gather(dim, x):
    return cores_gather(chips_gather(dim, x))


def tree_sum(parts):
    while len(parts) > 1:
        parts = [a + b for a, b in zip(parts[::2], parts[1::2])]
    return parts[0]


def half_sums(dim, keep, send):
    got = swap(send, "seq", 1)
    return [keep[k] + got[k] for k in range(dim.S // 2)]


def plane_sums(dim, half):
    others = [swap(half[k], "seq", 2 * k) for k in range(1, dim.S // 2)]
    return [sum((o[k] for o in others), half[0][k]) for k in range(dim.D)]


def split_half(dim, half):
    cut = dim.D // 2
    a, b = [h[:cut] for h in half], [h[cut:] for h in half]
    return [jnp.stack([a[1], a[3]]), jnp.stack([b[2], b[3]]), a[0], a[2], b[0], b[1]]


def two_step_sums(dim, parts):
    send_a, send_b, a0, a2, b0, b1 = parts
    got_a, got_b = swap(send_a, "seq", 2), swap(send_b, "seq", 4)
    far_a, far_b = swap(a2 + got_a[1], "seq", 4), swap(b1 + got_b[1], "seq", 2)
    a, b = a0 + got_a[0] + far_a, b0 + got_b[0] + far_b
    cut = dim.D // 2
    return [a[d] for d in range(cut)] + [b[d] for d in range(dim.D - cut)]


def dp_sum_halving(dim, parts):
    n = dim.D
    while n > 1:
        n //= 2
        got = swap(jnp.stack(parts[n:]), "dp", n)
        parts = [parts[k] + got[k] for k in range(n)]
    return parts[0]


def dp_sum(dim, parts):
    return sum((swap(parts[k], "dp", k) for k in range(1, dim.D)), parts[0])


def unpack_kernel(dim, shares, kinds, last, *refs):
    lower, upper, outs, (mine, other) = refs[: dim.S], refs[dim.S : 2 * dim.S], refs[2 * dim.S : -2], refs[-2:]
    head = last.q + SMALL
    for dst, first in ((mine, 0), (other, 1)):
        dst[...] = tree_sum([lower[k][:head, :] for k in range(first, dim.S, 2)])
    g_gain, g_bias, g_nu, g_theta, g_gamma, g_in, g_out, g_skip, g_glu, g_glu_bias = outs
    me, my = lax.axis_index("seq"), lax.axis_index("dp")

    def place(layer, kind, rows, value):
        if kind == "in":
            g_in[layer, rows, :] = value
        elif kind == "out":
            g_out[layer, rows, :] = value
        elif kind == "gv":
            g_glu[layer, rows, 0 : dim.H] = value
        else:
            g_glu[layer, rows, dim.H : 2 * dim.H] = value

    def put(k, s):
        for share, names, src, base in zip(shares, kinds, (lower[k], upper[k]), (head, 0)):
            for off in range(0, share.q, share.step):
                p = s * share.q + off
                if p // dim.Hd < share.nm:
                    layer, kind = names[p // dim.Hd]
                    r = p % dim.Hd
                    place(layer, kind, slice(r, r + share.step), src[base + off : base + off + share.step, :])

    def vectors(d):
        def own(layer, index, lo, width, out, at=0):
            src = (mine, other)

            def copy(ref):
                start = lo + d * width
                out[layer : layer + 1, :] = ref[last.q + index : last.q + index + 1, start : start + width]

            pl.when(me & 1 == layer)(functools.partial(copy, src[0]))
            pl.when(me & 1 != layer)(functools.partial(copy, src[1]))

        for layer in range(dim.layers):
            for index, out in ((GAIN, g_gain), (BIAS, g_bias), (SKIP, g_skip)):
                own(layer, index, 0, dim.Hd, out)
            n = dim.N // dim.D
            own(layer, 5, 0, n, g_nu)
            own(layer, 5, dim.N, n, g_theta)
            own(layer, 6, 0, n, g_gamma)
            width = 2 * dim.H // dim.D
            index = BIAS_V if d * width < dim.H else BIAS_G
            own(layer, index, 0 if index == BIAS_V else -dim.H, width, g_glu_bias)

    for who in range(dim.S):

        def all_of(who=who):
            for k in range(dim.S):
                put(k, k ^ who)
            half = who & 1
            for ref, part in ((mine, half), (other, 1 - half)):
                place(0, "in", slice(part * last.q, (part + 1) * last.q), ref[: last.q, :])

        pl.when(me == who)(all_of)
    for d in range(dim.D):
        pl.when(my == d)(functools.partial(vectors, d))


def unpack(dim, shares, kinds, last, lower, upper):
    n, l = dim.N // dim.D, dim.layers
    vec, small = f32(l, dim.Hd), f32(l, n)
    mat, wide = f32(l, dim.Hd, dim.H), f32(l, dim.Hd, 2 * dim.H)
    outs = [vec, vec, small, small, small, mat, mat, vec, wide, f32(l, 2 * dim.H // dim.D)]
    return call(functools.partial(unpack_kernel, dim, shares, kinds, last), outs, [pltpu.VMEM((last.q + SMALL, dim.H), F32)] * 2, *lower, *upper)


def body(inputs, out_grad, ln_gain, ln_bias, nu_log, theta_log, gamma_log, in_map, out_map, skip_gain, glu_weight, glu_bias):
    dim = Dims(inputs, in_map, lax.axis_size("dp"), lax.axis_size("seq"))
    T, H, N, R, B, D, S = dim.T, dim.H, dim.N, dim.R, dim.B, dim.D, dim.S
    me, my = lax.axis_index("seq"), lax.axis_index("dp")
    x = inputs.reshape(R, dim.L, H)
    og = out_grad.reshape(R, dim.L, H)

    heads = [SMALL, SMALL, 0]
    vectors = (ln_gain, ln_bias, skip_gain, nu_log, theta_log, gamma_log, glu_bias)
    messages = call(
        functools.partial(pack_kernel, dim),
        [f32(head + len(chunk) * dim.q, H) for head, chunk in zip(heads, CHUNKS)],
        [pltpu.VMEM(v.shape, F32) for v in vectors] + [pltpu.SemaphoreType.DMA((len(vectors) + sum(map(len, CHUNKS)),))],
        in_map, out_map, glu_weight, *vectors,
        anywhere=3 + len(vectors),
    )
    def stacked(others, head):
        return jnp.stack([other[head:].reshape(-1, dim.q, H) for other in others], 1)

    def along_dp(mine):
        return [swap(mine, "dp", k) for k in range(1, D)]

    def table_of(mine, others, head=SMALL):
        total = mine[:head]
        for other in others:
            total = total + other[:head]
        return call(functools.partial(prep_kernel, dim), [f32(TABLE, H)], [], total)[0]

    mine0, mine1, mine2 = messages
    others0 = along_dp(mine0)
    table0 = table_of(mine0, others0)
    mine1, others0 = tie(mine1, others0)
    others1 = along_dp(mine1)
    table1 = table_of(mine1, others1)
    chips0 = chips_gather(dim, stacked(others0, SMALL))
    joined1, chips0 = tie(stacked(others1, SMALL), chips0)
    pieces0 = cores_gather(chips0)
    mine2, (joined1,) = tie(mine2, [joined1])
    chips1 = chips_gather(dim, joined1)
    blocks = mine2[None]
    while blocks.shape[0] < D:
        blocks = jnp.concatenate([blocks, swap(blocks, "dp", blocks.shape[0])], 0)
    joined2 = stacked([blocks[k] for k in range(1, D)], 0)
    pieces = [pieces0, cores_gather(chips1), None]

    big, ent, fins = pltpu.VMEM((T, H), F32), pltpu.VMEM((R, H), F32), f32(B, H)
    stat = pltpu.VMEM((T, 128), F32)
    vec = pltpu.VMEM((SMALL, H), F32)

    def k(fn, names, outs, scratch, *args, us, late=(), sinks=()):
        chunks = [c for c, chunk in enumerate(CHUNKS) if set(chunk) & set(names)]
        kernel, count, own = weights_in(dim, chunks, names, fn)
        sources = [in_map, out_map, glu_weight] + [p for c in chunks for p in pieces[c]]
        late = [count + i for i in late]
        return call(kernel, outs, scratch + own, *sources, *args, us=us, anywhere=count, late=late, sinks=sinks)

    def carried(fin):
        return lax.all_gather(fin, "seq")

    part = [pltpu.VMEM((T, H), BF16)] * 2
    split_weight = [pltpu.VMEM((H, H), BF16)] * 2
    xhat0, rstd0, drive0, cf0, fin0, *normed0 = k(
        k_a0, [(0, 0)], [big, stat, big, ent, fins] + part, split_weight, x, table0, us=2.8
    )
    g0 = carried(fin0)
    joined2, (g0,) = tie(joined2, [g0])
    chips2 = chips_gather(dim, joined2)
    en0, states0, mixed0, v0, s0, sh0, sl0, ch0, cl0, act1, xhat1, rstd1, drive1, cf1, fin1, *normed1 = k(
        k_b0,
        [(0, 1), (0, 2), (0, 3), (1, 0)],
        [ent, big, big, big, big] + part * 2 + [big, big, stat, big, ent, fins] + part,
        split_weight,
        x, table0, table1, drive0, cf0, g0, xhat0,
        us=9.0,
    )
    fin1, chips2 = tie(fin1, chips2)
    g1 = carried(fin1)
    pieces[2] = cores_gather(chips2)
    spare = [pltpu.VMEM((T, H), F32)]
    out, en1, states1, dmixed1, ds1, rcf1, rfin1, sums1a, sh1, sl1, ch1, cl1, dvh1, dvl1, dgh1, dgl1, mh1, ml1 = k(
        k_b1,
        [(1, 1), (1, 2), (1, 3)],
        [f32(R, dim.L, H), ent, big, big, big, ent, fins, vec] + part * 5,
        split_weight * 3 + spare * 3,
        act1, og, table1, drive1, cf1, g1, xhat1,
        us=12.5, sinks=[0],
    )
    share1, share2, share3 = Share(dim, 3), Share(dim, 4), Halves(dim)
    tile = [pltpu.VMEM((WIDE, H), F32)]
    keep1, send1 = call(
        functools.partial(k_w1, dim, share1), [f32(*share1.shape)] * 2, tile,
        ch1, cl1, dvh1, dvl1, dgh1, dgl1, sh1, sl1, mh1, ml1, us=4.0,
    )
    rfin1, (send1,) = tie(rfin1, [send1])
    gr1 = carried(rfin1)
    gr1, half1 = tie(gr1, half_sums(dim, keep1, send1))
    dmid, dmixed0, ds0, rcf0, rfin0, sums1b, sums0a, dph1, dpl1, dvh0, dvl0, dgh0, dgl0, mh0, ml0 = k(
        k_c1,
        [(1, 0), (0, 2), (0, 3), (0, 1)],
        [big, big, big, ent, fins, vec, vec] + part * 4,
        split_weight + [pltpu.VMEM((R, H), F32)],
        og, table1, table0, ds1, rcf1, gr1, states1, en1, drive1, xhat1, rstd1, dmixed1,
        xhat0, mixed0, v0, s0,
        us=9.5,
    )
    keep2, send2 = call(
        functools.partial(k_w2, dim, share2), [f32(*share2.shape)] * 2, tile,
        ch0, cl0, dvh0, dvl0, dgh0, dgl0, sh0, sl0, mh0, ml0, *normed1, dph1, dpl1, us=5.3,
    )
    rfin0, (send2, *sums1) = tie(rfin0, [send2, *plane_sums(dim, half1)])
    gr0 = carried(rfin0)
    half2 = half_sums(dim, keep2, send2)
    two_steps = S == 8
    gr0, half2 = tie(gr0, split_half(dim, half2) if two_steps else half2)
    input_grad, keep3, send3 = k(
        functools.partial(k_c0, share3),
        [(0, 0)],
        [f32(R, dim.L, H)] + [f32(*share3.shape)] * 2,
        part + split_weight + [pltpu.VMEM((R, H), F32)] + spare + [pltpu.VMEM((SMALL, H), F32)] + tile,
        table0, ds0, rcf0, gr0, states0, en0, drive0, xhat0, rstd0, dmixed0, dmid, sums1a, sums1b, sums0a, *normed0,
        us=6.0, sinks=[0],
    )
    sums2 = two_step_sums(dim, half2) if two_steps else plane_sums(dim, half2)
    got3 = swap(send3, "seq", 1)
    half3 = [keep3[d] + got3[d] for d in range(D)]
    total3 = tree_sum([half3[0]] + [swap(half3[k], "dp", k) for k in range(1, D)])
    upper1 = dp_sum(dim, sums1)
    chips3 = chips_gather(dim, jnp.concatenate([total3, upper1], 0))
    last = cores_gather(chips3)
    upper = plane_gather(dim, dp_sum(dim, sums2))
    kinds = [[(1, "gv"), (1, "gg"), (1, "out")], [(0, "gv"), (0, "gg"), (0, "out"), (1, "in")]]
    grads = unpack(dim, (share1, share2), kinds, share3, last, upper)
    return (out.reshape(inputs.shape), input_grad.reshape(inputs.shape), *grads)


def solution(mesh):
    act, vec, mat = P("dp", "seq", None), P(None, "dp"), P(None, "dp", None)
    in_specs = (act, act, vec, vec, vec, vec, vec, mat, mat, vec, mat, vec)
    out_specs = (act, act, vec, vec, vec, vec, vec, mat, mat, vec, mat, vec)
    return jax.shard_map(body, mesh=mesh, in_specs=in_specs, out_specs=out_specs, check_vma=False)
```
